512 devices in a mesh: chan: 32 (over z_lo, y, core), row: 16 (over x, z_hi).
Axes of the slice: x: 4, y: 8, z: 8 (z_hi: 4, z_lo: 2; z = z_hi * 2 + z_lo), core: 2. Of those that a mesh axis runs over, the one named last changes fastest.
Arguments:
- pair_acts: bfloat16 [1280, 1280, 128], P('row', 'chan'), may hold values from -6 to 6
- residue_valid: int32 [1280], replicated, may hold values 0 or 1
- chain_index: int32 [1280], replicated, may hold values from 0 to 3, never falling along the last dimension, each value on 1 to 640 neighbouring positions
- norm_gain: float32 [2, 128], replicated, may hold values from 0.5 to 1.5
- norm_bias: float32 [2, 128], replicated, may hold values from -3 to 3
- projection: bfloat16 [2, 128, 256], replicated, may hold values from -0.5 to 0.5
- gate_weight: bfloat16 [2, 128, 128], replicated, may hold values from -0.5 to 0.5
- chain_bias: float32 [2, 128], replicated, may hold values from -4 to 4
- out_gain: float32 [2, 64], replicated, may hold values from 0.5 to 1.5
- out_weight: bfloat16 [2, 64, 128], replicated, may hold values from -0.75 to 0.75
Outputs:
- updated: bfloat16 [1280, 1280, 128], P('row', 'chan')
The draws below stay inside these ranges and needn't reach their ends.
Inputs may be any that keep to these rules, and one draw needn't show every extreme that they name: `chain_index`: chain numbers never fall along the residues, and no chain is longer than 640 residues.
All inputs are finite; a program needn't handle non-finite values.
Results may differ from the reference program's by a relative error of at most 0.0065.
Values may be sent and summed in bfloat16 or wider, within the bound.
No kernel may reach another device: no remote copies, remote signals or barrier semaphores. Data moves between devices by JAX's collectives and lax.ppermute only.
A program may use at most 64 MiB of HBM per device.

```python
import math
import jax
import jax.numpy as jnp
import numpy as np
from jax import lax

C = 128
H = 64
N = 1280
N_ROW = 16


def plant(drawn, rng, low, high):
    longest = drawn.shape.index(max(drawn.shape))
    spots = []
    for shift in (0, 1):
        where = [jax.random.randint(jax.random.fold_in(rng, axis), (), 0, length) for axis, length in enumerate(drawn.shape)]
        where[longest] = (where[longest] + shift) % drawn.shape[longest]
        spots.append(tuple(where))
    return drawn.at[spots[0]].set(low).at[spots[1]].set(high)


def levels(key, extent, pieces, low, largest):
    def one(position, parts):
        draws = jax.random.uniform(jax.random.fold_in(jax.random.fold_in(key, 6), position), (parts,), jnp.float32, low / len(pieces), largest / len(pieces))
        return jnp.repeat(jnp.exp(draws), extent[position] // parts).reshape((-1,) + (1,) * (len(extent) - position - 1))

    gain = one(*pieces[0])
    for cut in pieces[1:]:
        gain = gain * one(*cut)
    return gain


def length_profile(count, total, reach, skew):
    loads = [(1 << 20) // math.isqrt(grade ** skew) + 1 for grade in range(2, count + 1)]
    rest, holding = total - reach - (count - 1), [1] * (count - 1)
    while rest > 0:
        movable = [i for i in range(count - 1) if holding[i] < reach]
        whole, remaining = sum([loads[i] for i in movable]), rest
        for i in movable:
            addition = min(reach - holding[i], max(1, remaining * loads[i] // whole), rest)
            holding[i] = holding[i] + addition
            rest = rest - addition
    return np.array([reach] + holding)


def uneven(own_key, amount, total, most, slope):
    if amount == 2:
        one = jax.random.randint(own_key, (), max(1, total - most), min(most, total - 1) + 1)
        return jnp.stack([one, total - one])
    tallies = jnp.asarray(length_profile(amount, total, most, slope), jnp.int32)
    twos = (amount - 1) // 2
    donor, taker = tallies[1:1 + 2 * twos:2], tallies[2:2 + 2 * twos:2]
    room = jnp.minimum(donor - 1, most - taker)
    moved = jax.random.randint(jax.random.fold_in(own_key, 1), (twos,), 0, 1 << 20) % (room + 1)
    tallies = tallies.at[1:1 + 2 * twos:2].set(donor - moved).at[2:2 + 2 * twos:2].set(taker + moved)
    return tallies[jax.random.permutation(jax.random.fold_in(own_key, 2), amount)]


def gaussian(own_key, shape, scale, most, shards=(), kind=jnp.bfloat16):
    entries = scale * jax.random.normal(own_key, shape, jnp.float32)
    if shards:
        entries = entries * levels(own_key, shape, shards, -0.22, 0.18)
    return jnp.clip(entries, -most, most).astype(kind)


def setup_inputs(seed: int = 0) -> dict:
    streams_of = jax.random.split(jax.random.key(seed), 11)
    return {
        "pair_acts": gaussian(streams_of[0], (N, N, C), 1.0, 6.0, ((0, 16), (1, 32))),
        "residue_valid": plant((jax.random.randint(streams_of[1], (N,), 0, 8) < 7).astype(jnp.int32), jax.random.fold_in(streams_of[1], 1), 0, 1),
        "chain_index": jnp.searchsorted(jnp.cumsum(uneven(streams_of[2], 4, N, N // 2, 0)), jnp.arange(N), side="right").astype(jnp.int32),
        "norm_gain": jnp.clip(1.0 + 0.1 * jax.random.normal(streams_of[3], (2, C), jnp.float32), 0.5, 1.5),
        "norm_bias": gaussian(streams_of[4], (2, C), 0.5, 3.0, (), jnp.float32),
        "projection": gaussian(streams_of[5], (2, C, 4 * H), C ** -0.5, 0.5),
        "gate_weight": gaussian(streams_of[6], (2, C, C), C ** -0.5, 0.5),
        "chain_bias": gaussian(streams_of[7], (2, C), 1.0, 4.0, (), jnp.float32),
        "out_gain": jnp.clip(1.0 + 0.1 * jax.random.normal(streams_of[8], (2, H), jnp.float32), 0.5, 1.5),
        "out_weight": gaussian(streams_of[9], (2, H, C), H ** -0.5, 0.75),
    }


def layer_norm(values, axis):
    average = lax.optimization_barrier(jnp.mean(values, axis=axis, keepdims=True))
    spread = lax.optimization_barrier(jnp.mean((values - average) ** 2, axis=axis, keepdims=True))
    return (values - average) * lax.rsqrt(spread + 1e-05)

def normalize_pair(block, which, norm_gain, norm_bias):
    pair_float = block.astype(jnp.float32)
    return (layer_norm(pair_float, -1) * norm_gain[which] + norm_bias[which]).astype(jnp.bfloat16)

def reference(pair_acts, residue_valid, chain_index, norm_gain, norm_bias, projection, gate_weight, chain_bias, out_gain, out_weight):
    hidden = out_weight.shape[1]
    width = pair_acts.shape[2]
    block_rows = N // N_ROW
    valid = residue_valid.astype(jnp.float32)

    def prepare(which, state):

        def one_block(items):
            block, valid_rows = items
            normed = normalize_pair(block, which, norm_gain, norm_bias)
            proj = jnp.dot(normed, projection[which], preferred_element_type=jnp.float32)
            pair_mask = (valid_rows[:, None] * valid[None, :])[:, :, None]
            left_factor = (jax.nn.sigmoid(proj[..., hidden:2 * hidden]) * proj[..., :hidden] * pair_mask).astype(jnp.bfloat16)
            right_factor = (jax.nn.sigmoid(proj[..., 3 * hidden:]) * proj[..., 2 * hidden:3 * hidden] * pair_mask).astype(jnp.bfloat16)
            return (left_factor, right_factor)
        blocks = state.reshape(N_ROW, block_rows, N, width)
        left_factor, right_factor = lax.map(one_block, (blocks, valid.reshape(N_ROW, block_rows)))
        return (left_factor.reshape(N, N, hidden), right_factor.reshape(N, N, hidden))

    def finish(which, state, product):

        def one_block(items):
            block, tri_block, chain_rows = items
            pair_float = block.astype(jnp.float32)
            normed = normalize_pair(block, which, norm_gain, norm_bias)
            same_chain = (chain_rows[:, None] == chain_index[None, :]).astype(jnp.float32)[:, :, None]
            gate = jax.nn.sigmoid(jnp.dot(normed, gate_weight[which], preferred_element_type=jnp.float32) + same_chain * chain_bias[which])
            hidden_norm = (layer_norm(tri_block.astype(jnp.float32), -1) * out_gain[which]).astype(jnp.bfloat16)
            branch = jnp.dot(hidden_norm, out_weight[which], preferred_element_type=jnp.float32)
            return (pair_float + gate * branch).astype(jnp.bfloat16)
        blocks = state.reshape(N_ROW, block_rows, N, width)
        tri_blocks = product.reshape(N_ROW, block_rows, N, hidden)
        result = lax.map(one_block, (blocks, tri_blocks, chain_index.reshape(N_ROW, block_rows)))
        return result.reshape(N, N, width)
    left_factor, right_factor = prepare(0, pair_acts)
    left_major = jnp.transpose(left_factor, (2, 0, 1)).astype(jnp.float32)
    right_major = jnp.transpose(right_factor, (2, 0, 1)).astype(jnp.float32)
    product = jnp.einsum('cik,cjk->cij', left_major, right_major, precision=lax.Precision.HIGHEST)
    product = jnp.transpose(product.astype(jnp.bfloat16), (1, 2, 0))
    middle = finish(0, pair_acts, product)
    left_factor, right_factor = prepare(1, middle)
    left_major = jnp.transpose(left_factor, (2, 0, 1)).astype(jnp.float32)
    right_major = jnp.transpose(right_factor, (2, 0, 1)).astype(jnp.float32)
    product = jnp.einsum('cki,ckj->cij', left_major, right_major, precision=lax.Precision.HIGHEST)
    product = jnp.transpose(product.astype(jnp.bfloat16), (1, 2, 0))
    return finish(1, middle, product)
```

```python
import jax
import jax.numpy as jnp
from jax import lax
from jax.sharding import Mesh
from jax.sharding import PartitionSpec as P

AXES = ("zl", "y", "core", "x", "zh")
SIZES = (2, 8, 2, 4, 4)
PLANE = ("zl", "y", "zh")
ROWS = 80
COLUMNS = 40
PAIRS = ROWS * COLUMNS
HIDDEN = 64
X = 4
ZH = 4
SPAN = 16
EPS = 1e-05


def layer_norm(values, axis):
    average = jnp.mean(values, axis=axis, keepdims=True)
    spread = jnp.mean((values - average) ** 2, axis=axis, keepdims=True)
    return (values - average) * lax.rsqrt(spread + EPS)


def exchange(values, axes):
    return lax.all_to_all(values, axes, split_axis=0, concat_axis=0, tiled=True)


def to_plane(flat):
    return exchange(flat, PLANE).reshape(SPAN, ZH, ROWS, COLUMNS)


def from_plane(blocks):
    return exchange(blocks.reshape(HIDDEN, PAIRS), PLANE)


def both_cores(values):
    return exchange(jnp.broadcast_to(values[None], (2,) + values.shape), "core")


def outgoing(left_factor, right_factor):
    right = to_plane(right_factor).reshape(SPAN, ZH, 2, COLUMNS, COLUMNS)
    right = exchange(right.transpose(2, 1, 3, 0, 4), "core")
    right = right.reshape(2, ZH * COLUMNS, SPAN * COLUMNS).transpose(1, 0, 2)
    right = lax.all_gather(right, "x", axis=0, tiled=True)
    left = to_plane(left_factor).transpose(1, 2, 0, 3).reshape(ZH * ROWS, SPAN * COLUMNS)
    left = both_cores(left)
    product = jnp.einsum("aik,jak->ij", left, right, preferred_element_type=jnp.float32)
    product = product.astype(jnp.bfloat16).reshape(ZH, ROWS, SPAN, COLUMNS)
    return from_plane(product.transpose(2, 0, 1, 3))


def incoming(left_factor, right_factor):
    right = to_plane(right_factor).transpose(1, 2, 0, 3).reshape(ZH * ROWS, SPAN * COLUMNS)
    right = lax.all_gather(right, "x", axis=0, tiled=True)
    left = to_plane(left_factor).reshape(X, ZH, ZH, ROWS, COLUMNS)
    left = exchange(left.transpose(0, 2, 3, 1, 4), "x")
    left = both_cores(left.reshape(X * ZH * ROWS, ZH * COLUMNS))
    product = jnp.einsum("aki,kj->aij", left, right, preferred_element_type=jnp.float32)
    product = product.astype(jnp.bfloat16).reshape(2, ZH, COLUMNS, SPAN, COLUMNS)
    return from_plane(product.transpose(3, 1, 0, 2, 4))


def body(
    pair_acts,
    residue_valid,
    chain_index,
    norm_gain,
    norm_bias,
    projection,
    gate_weight,
    chain_bias,
    out_gain,
    out_weight,
):
    row_start = (lax.axis_index("x") * ZH + lax.axis_index("zh")) * ROWS
    column_block = (lax.axis_index("zl") * 8 + lax.axis_index("y")) * 2 + lax.axis_index("core")
    column_start = column_block * COLUMNS
    valid_rows = lax.dynamic_slice_in_dim(residue_valid, row_start, ROWS).astype(jnp.float32)
    valid_columns = lax.dynamic_slice_in_dim(residue_valid, column_start, COLUMNS).astype(
        jnp.float32
    )
    chain_rows = lax.dynamic_slice_in_dim(chain_index, row_start, ROWS)
    chain_columns = lax.dynamic_slice_in_dim(chain_index, column_start, COLUMNS)
    pair_mask = (valid_rows[:, None] * valid_columns[None, :]).reshape(PAIRS)
    same_chain = (
        (chain_rows[:, None] == chain_columns[None, :]).astype(jnp.float32).reshape(PAIRS, 1)
    )

    def project(state, which):
        pair_float = state.astype(jnp.float32)
        normed = (layer_norm(pair_float, -1) * norm_gain[which] + norm_bias[which]).astype(
            jnp.bfloat16
        )
        proj = jnp.einsum(
            "pd,de->ep", normed, projection[which], preferred_element_type=jnp.float32
        )
        blocks = [proj[HIDDEN * n : HIDDEN * (n + 1)] for n in range(4)]
        left_factor = (jax.nn.sigmoid(blocks[1]) * blocks[0] * pair_mask).astype(jnp.bfloat16)
        right_factor = (jax.nn.sigmoid(blocks[3]) * blocks[2] * pair_mask).astype(jnp.bfloat16)
        return normed, left_factor, right_factor

    def finish(state, normed, product, which):
        pair_float = state.astype(jnp.float32)
        hidden_norm = (
            layer_norm(product.astype(jnp.float32), 0) * out_gain[which][:, None]
        ).astype(jnp.bfloat16)
        branch = jnp.einsum(
            "cp,cd->pd", hidden_norm, out_weight[which], preferred_element_type=jnp.float32
        )
        gate = jax.nn.sigmoid(
            jnp.dot(normed, gate_weight[which], preferred_element_type=jnp.float32)
            + same_chain * chain_bias[which]
        )
        return (pair_float + gate * branch).astype(jnp.bfloat16)

    state = pair_acts.reshape(PAIRS, pair_acts.shape[2])
    normed, left_factor, right_factor = project(state, 0)
    state = finish(state, normed, outgoing(left_factor, right_factor), 0)
    normed, left_factor, right_factor = project(state, 1)
    state = finish(state, normed, incoming(left_factor, right_factor), 1)
    return state.reshape(pair_acts.shape)


def solution(mesh):
    fine = Mesh(mesh.devices.reshape(SIZES), AXES)
    pairs = P(("x", "zh"), ("zl", "y", "core"), None)
    placed = (pairs, P(), P(), P(), P(), P(), P(), P(), P(), P())
    return jax.shard_map(body, mesh=fine, in_specs=placed, out_specs=pairs, check_vma=False)
```

```python
import functools

import jax
import jax.numpy as jnp
from jax import lax
from jax.experimental import pallas as pl
from jax.experimental.pallas import tpu as pltpu
from jax.sharding import Mesh
from jax.sharding import PartitionSpec as P

AXES = ("zl", "y", "core", "x", "zh")
SIZES = (2, 8, 2, 4, 4)
PLANE = ("zl", "y", "zh")
ROWS = 80
COLUMNS = 40
WIDTH = 128
HIDDEN = 64
X = 4
ZH = 4
SPAN = 16
EPS = 1e-05
DEPTH = 32
LANES = 128
GROUPS = ((0, 32), (32, 32), (64, 16))
STRIDE = 40
CHUNKS = jax.ShapeDtypeStruct((HIDDEN, DEPTH, LANES), jnp.bfloat16)
VMEM = pl.BlockSpec(memory_space=pltpu.VMEM)
SMEM = pl.BlockSpec(memory_space=pltpu.SMEM)


def call(kernel, out_shape, in_specs, scratch_shapes=(), flops=10**8, moved=4 * 10**6):
    outs = jax.tree.map(lambda _: VMEM, out_shape)
    return pl.pallas_call(
        kernel,
        out_shape=out_shape,
        in_specs=in_specs,
        out_specs=outs,
        scratch_shapes=scratch_shapes,
        compiler_params=pltpu.CompilerParams(vmem_limit_bytes=40 * 2**20),
        cost_estimate=pl.CostEstimate(flops=flops, bytes_accessed=moved, transcendentals=0),
    )


def normalize(values, gain, bias):
    average = jnp.mean(values, axis=-1, keepdims=True)
    centred = values - average
    spread = jnp.mean(centred * centred, axis=-1, keepdims=True)
    return (centred * lax.rsqrt(spread + EPS) * gain + bias).astype(jnp.bfloat16)


def block_rows(step, count):
    return [step + DEPTH * group for group in range(count)]


def spread_columns(place_ref, valid_ref):
    lane = lax.broadcasted_iota(jnp.int32, (1, LANES), 1)
    inside = lane % COLUMNS
    found = jnp.zeros((1, LANES), jnp.float32)
    for column in range(COLUMNS):
        value = valid_ref[place_ref[1] + column].astype(jnp.float32)
        found = jnp.where(inside == column, value, found)
    return jnp.where(lane < 3 * COLUMNS, found, 0.0)


def mask_of(step, count, place_ref, valid_ref, columns):
    lane = lax.broadcasted_iota(jnp.int32, (1, LANES), 1)
    mask = jnp.zeros((1, LANES), jnp.float32)
    for group, row in enumerate(block_rows(step, count)):
        value = valid_ref[place_ref[0] + row].astype(jnp.float32)
        inside = (lane >= group * COLUMNS) & (lane < (group + 1) * COLUMNS)
        mask = jnp.where(inside, value, mask)
    return mask * columns


def project_rows(step, count, normed, weight_ref, mask, left_scratch, right_scratch):
    rows = count * COLUMNS
    padded = jnp.concatenate([normed, jnp.zeros((LANES - rows, WIDTH), jnp.bfloat16)], axis=0)
    proj = lax.dot_general(
        weight_ref[...], padded, (((1,), (1,)), ((), ())), preferred_element_type=jnp.float32
    )
    parts = [proj[HIDDEN * n : HIDDEN * (n + 1)] for n in range(4)]
    place = pl.ds(step, HIDDEN, stride=STRIDE)
    left_scratch[place, :] = jax.nn.sigmoid(parts[1]) * parts[0] * mask
    right_scratch[place, :] = jax.nn.sigmoid(parts[3]) * parts[2] * mask


def put_chunks(scratch, out_ref):
    for channel in range(HIDDEN):
        out_ref[channel] = scratch[pl.ds(channel * STRIDE, DEPTH), :].astype(jnp.bfloat16)


def project_kernel(
    place_ref, valid_ref, pair_ref, gain_ref, bias_ref, weight_ref, left_ref, right_ref, left_s, right_s
):
    columns = spread_columns(place_ref, valid_ref)

    def one(step, count):
        values = jnp.concatenate(
            [pair_ref[row].astype(jnp.float32) for row in block_rows(step, count)], axis=0
        )
        normed = normalize(values, gain_ref[...], bias_ref[...])
        mask = mask_of(step, count, place_ref, valid_ref, columns)
        project_rows(step, count, normed, weight_ref, mask, left_s, right_s)

    pl.loop(0, 16)(functools.partial(one, count=3))
    pl.loop(16, DEPTH)(functools.partial(one, count=2))
    put_chunks(left_s, left_ref)
    put_chunks(right_s, right_ref)


SCRATCH = pltpu.VMEM(((HIDDEN + 1) * STRIDE, LANES), jnp.float32)


def project(place, valid, pair, gain, bias, weight):
    return call(
        project_kernel,
        [CHUNKS, CHUNKS],
        [SMEM, SMEM, VMEM, VMEM, VMEM, VMEM],
        [SCRATCH, SCRATCH],
    )(place, valid, pair, gain, bias, weight)


def finish_kernel(
    then,
    place_ref,
    valid_ref,
    chain_ref,
    out_gain_ref,
    pair_ref,
    product_ref,
    gain_ref,
    bias_ref,
    gate_ref,
    chain_bias_ref,
    out_weight_ref,
    *rest,
):
    if then:
        next_gain_ref, next_bias_ref, weight_ref, out_ref, left_ref, right_ref = rest[:6]
        hidden_s, left_s, right_s = rest[6:]
        columns = spread_columns(place_ref, valid_ref)
    else:
        out_ref, hidden_s = rest
    row = lax.broadcasted_iota(jnp.int32, (COLUMNS, WIDTH), 0)
    chain_columns = jnp.full((COLUMNS, WIDTH), -1, jnp.int32)
    for column in range(COLUMNS):
        chain_columns = jnp.where(row == column, chain_ref[place_ref[1] + column], chain_columns)

    def channel(n):
        return product_ref[n].astype(jnp.float32)

    average = jnp.zeros((DEPTH, LANES), jnp.float32)
    for n in range(HIDDEN):
        average = average + channel(n)
    average = average / HIDDEN
    spread = jnp.zeros((DEPTH, LANES), jnp.float32)
    for n in range(HIDDEN):
        centred = channel(n) - average
        spread = spread + centred * centred
    scale = lax.rsqrt(spread / HIDDEN + EPS)
    for n in range(HIDDEN):
        hidden_s[pl.ds(n * STRIDE, DEPTH), :] = (channel(n) - average) * scale * out_gain_ref[n]

    def one(step, count):
        rows = block_rows(step, count)
        values = jnp.concatenate([pair_ref[row].astype(jnp.float32) for row in rows], axis=0)
        normed = normalize(values, gain_ref[...], bias_ref[...])
        gate = jnp.dot(normed, gate_ref[...], preferred_element_type=jnp.float32)
        same = jnp.concatenate(
            [
                jnp.where(chain_columns == chain_ref[place_ref[0] + row], chain_bias_ref[...], 0.0)
                for row in rows
            ],
            axis=0,
        )
        hidden = hidden_s[pl.ds(step, HIDDEN, stride=STRIDE), :].astype(jnp.bfloat16)
        branch = lax.dot_general(
            hidden,
            out_weight_ref[...],
            (((0,), (0,)), ((), ())),
            preferred_element_type=jnp.float32,
        )[: count * COLUMNS]
        new = (values + jax.nn.sigmoid(gate + same) * branch).astype(jnp.bfloat16)
        for group, row in enumerate(rows):
            out_ref[row] = new[group * COLUMNS : (group + 1) * COLUMNS]
        if then:
            normed = normalize(
                new.astype(jnp.float32), next_gain_ref[...], next_bias_ref[...]
            )
            mask = mask_of(step, count, place_ref, valid_ref, columns)
            project_rows(step, count, normed, weight_ref, mask, left_s, right_s)

    pl.loop(0, 16)(functools.partial(one, count=3))
    pl.loop(16, DEPTH)(functools.partial(one, count=2))
    if then:
        put_chunks(left_s, left_ref)
        put_chunks(right_s, right_ref)


def finish(place, valid, chain, out_gain, pair, product, gain, bias, gate, chain_bias, out_weight, then=()):
    out = jax.ShapeDtypeStruct(pair.shape, pair.dtype)
    return call(
        functools.partial(finish_kernel, bool(then)),
        [out, CHUNKS, CHUNKS] if then else [out],
        [SMEM] * 4 + [VMEM] * (7 + len(then)),
        [SCRATCH] * (3 if then else 1),
    )(place, valid, chain, out_gain, pair, product, gain, bias, gate, chain_bias, out_weight, *then)


def gather_block(chunks_ref, zh, group, size):
    lanes = slice(group * COLUMNS, (group + 1) * COLUMNS)
    return jnp.concatenate(
        [chunks_ref[span * ZH + zh, :size, :][:, lanes] for span in range(SPAN)], axis=1
    )


def assemble_kernel(chunks_ref, out_ref):
    for zh in range(ZH):
        for group, (start, size) in enumerate(GROUPS):
            out_ref[pl.ds(zh * ROWS + start, size), :] = gather_block(chunks_ref, zh, group, size)


def assemble(chunks):
    out = jax.ShapeDtypeStruct((ZH * ROWS, SPAN * COLUMNS), jnp.bfloat16)
    return call(assemble_kernel, out, [VMEM])(chunks)


def assemble_turned_kernel(chunks_ref, out_ref, whole):
    for zh in range(ZH):
        for group, (start, size) in enumerate(GROUPS):
            whole[pl.ds(zh * ROWS + start, size), :] = gather_block(
                chunks_ref, zh, group, size
            ).astype(jnp.float32)
    whole[pl.ds(ZH * ROWS, 64), :] = jnp.zeros((64, SPAN * COLUMNS), jnp.float32)
    for part in range(SPAN * COLUMNS // 128):
        turned = whole[:, part * 128 : (part + 1) * 128].T
        out_ref[pl.ds(part * 128, 128), :] = turned[:, : ZH * ROWS].astype(jnp.bfloat16)


def assemble_turned(chunks):
    out = jax.ShapeDtypeStruct((SPAN * COLUMNS, ZH * ROWS), jnp.bfloat16)
    scratch = [pltpu.VMEM((ZH * ROWS + 64, SPAN * COLUMNS), jnp.float32)]
    return call(assemble_turned_kernel, out, [VMEM], scratch)(chunks)


def chunk_of(total, zh, start):
    pieces = []
    for first, size in GROUPS:
        piece = total[pl.ds(zh * ROWS + first, size), :][:, start : start + COLUMNS]
        if size < DEPTH:
            piece = jnp.concatenate(
                [piece, jnp.zeros((DEPTH - size, COLUMNS), jnp.float32)], axis=0
            )
        pieces.append(piece)
    pieces.append(jnp.zeros((DEPTH, LANES - 3 * COLUMNS), jnp.float32))
    return jnp.concatenate(pieces, axis=1).astype(jnp.bfloat16)


def outgoing_kernel(core_ref, left_ref, right_ref, out_ref, left_s, total):
    assemble_kernel(left_ref, left_s)
    for x in range(X):
        total[:, x * ZH * ROWS : (x + 1) * ZH * ROWS] = lax.dot_general(
            left_s[...],
            right_ref[pl.ds(x * ZH * ROWS, ZH * ROWS), :],
            (((1,), (1,)), ((), ())),
            preferred_element_type=jnp.float32,
        )
    for half in range(2):
        slot = lax.rem(core_ref[0] + half, 2)
        for span in range(SPAN):
            for zh in range(ZH):
                out_ref[slot, span * ZH + zh] = chunk_of(total, zh, (2 * span + half) * COLUMNS)


def outgoing(core, left, right):
    out = jax.ShapeDtypeStruct((2,) + CHUNKS.shape, jnp.bfloat16)
    scratch = [
        pltpu.VMEM((ZH * ROWS, SPAN * COLUMNS), jnp.bfloat16),
        pltpu.VMEM((ZH * ROWS, X * ZH * ROWS), jnp.float32),
    ]
    return call(outgoing_kernel, out, [SMEM, VMEM, VMEM], scratch, 6 * 10**8)(core, left, right)


def incoming_kernel(core_ref, own_ref, other_ref, right_ref, out_ref, total):
    for n, left_ref in enumerate((own_ref, other_ref)):
        side = lax.rem(core_ref[0] + n, 2)
        product = jnp.zeros((ZH * COLUMNS, SPAN * COLUMNS), jnp.float32)
        for x in range(X):
            product = product + jnp.dot(
                left_ref[x],
                right_ref[pl.ds(x * ZH * ROWS, ZH * ROWS), :],
                preferred_element_type=jnp.float32,
            )
        for zh in range(ZH):
            start = pl.multiple_of(zh * ROWS + side * COLUMNS, 8)
            total[pl.ds(start, COLUMNS), :] = product[zh * COLUMNS : (zh + 1) * COLUMNS]
    for span in range(SPAN):
        for zh in range(ZH):
            out_ref[span * ZH + zh] = chunk_of(total, zh, span * COLUMNS)


def incoming(core, own, other, right):
    scratch = [pltpu.VMEM((ZH * ROWS, SPAN * COLUMNS), jnp.float32)]
    return call(incoming_kernel, CHUNKS, [SMEM, VMEM, VMEM, VMEM], scratch, 6 * 10**8)(
        core, own, other, right
    )


def exchange(values, axes):
    return lax.all_to_all(values, axes, split_axis=0, concat_axis=0, tiled=True)


def swap_cores(values):
    return lax.ppermute(values, "core", [(0, 1), (1, 0)])


def body(
    pair_acts,
    residue_valid,
    chain_index,
    norm_gain,
    norm_bias,
    projection,
    gate_weight,
    chain_bias,
    out_gain,
    out_weight,
):
    row_start = (lax.axis_index("x") * ZH + lax.axis_index("zh")) * ROWS
    core_index = lax.axis_index("core")
    column_block = (lax.axis_index("zl") * 8 + lax.axis_index("y")) * 2 + core_index
    place = jnp.stack([row_start, column_block * COLUMNS]).astype(jnp.int32)
    core = core_index.reshape(1).astype(jnp.int32)
    turned = projection.transpose(0, 2, 1)

    left, right = project(
        place, residue_valid, pair_acts, norm_gain[:1], norm_bias[:1], turned[0]
    )
    right = assemble(exchange(right, PLANE))
    right = lax.all_gather(right, "x", axis=0, tiled=True)
    halves = outgoing(core, exchange(left, PLANE), right)
    total = halves[0].astype(jnp.float32) + swap_cores(halves[1]).astype(jnp.float32)
    product = exchange(total.astype(jnp.bfloat16), PLANE)
    middle, left, right = finish(
        place,
        residue_valid,
        chain_index,
        out_gain[0],
        pair_acts,
        product,
        norm_gain[:1],
        norm_bias[:1],
        gate_weight[0],
        chain_bias[:1],
        out_weight[0],
        (norm_gain[1:], norm_bias[1:], turned[1]),
    )
    right = assemble(exchange(right, PLANE))
    right = lax.all_gather(right, "x", axis=0, tiled=True)
    left = assemble_turned(exchange(left, PLANE)).reshape(X, ZH * COLUMNS, ZH * ROWS)
    left = exchange(left, "x")
    product = exchange(incoming(core, left, swap_cores(left), right), PLANE)
    return finish(
        place,
        residue_valid,
        chain_index,
        out_gain[1],
        middle,
        product,
        norm_gain[1:],
        norm_bias[1:],
        gate_weight[1],
        chain_bias[1:],
        out_weight[1],
    )[0]


def solution(mesh):
    fine = Mesh(mesh.devices.reshape(SIZES), AXES)
    pairs = P(("x", "zh"), ("zl", "y", "core"), None)
    placed = (pairs, P(), P(), P(), P(), P(), P(), P(), P(), P())
    return jax.shard_map(body, mesh=fine, in_specs=placed, out_specs=pairs, check_vma=False)
```

```python
import functools

import jax
import jax.numpy as jnp
from jax import lax
from jax.experimental import pallas as pl
from jax.experimental.pallas import tpu as pltpu
from jax.sharding import Mesh
from jax.sharding import PartitionSpec as P

AXES = ("zl", "y", "core", "x", "zh")
SIZES = (2, 8, 2, 4, 4)
PLANE = ("zl", "y", "zh")
ROWS = 80
COLUMNS = 40
WIDTH = 128
HIDDEN = 64
X = 4
ZH = 4
SPAN = 16
EPS = 1e-05
DEPTH = 32
LANES = 128
SUB = 8
GROUPS = ((0, 32), (32, 32), (64, 16))
STRIDE = 40
BATCH = 8
CHUNKS = jax.ShapeDtypeStruct((HIDDEN, SUB, DEPTH // SUB * LANES), jnp.bfloat16)
NORMED = jax.ShapeDtypeStruct((DEPTH, LANES, WIDTH), jnp.bfloat16)
GATES = jax.ShapeDtypeStruct((DEPTH, LANES, WIDTH), jnp.float32)
VMEM = pl.BlockSpec(memory_space=pltpu.VMEM)
SMEM = pl.BlockSpec(memory_space=pltpu.SMEM)


def call(kernel, out_shape, in_specs, scratch_shapes=(), flops=10**8, moved=4 * 10**6):
    outs = jax.tree.map(lambda _: VMEM, out_shape)
    return pl.pallas_call(
        kernel,
        out_shape=out_shape,
        in_specs=in_specs,
        out_specs=outs,
        scratch_shapes=scratch_shapes,
        compiler_params=pltpu.CompilerParams(vmem_limit_bytes=40 * 2**20),
        cost_estimate=pl.CostEstimate(flops=flops, bytes_accessed=moved, transcendentals=0),
    )


def normalize(values, gain, bias):
    average = jnp.mean(values, axis=-1, keepdims=True)
    centred = values - average
    spread = jnp.mean(centred * centred, axis=-1, keepdims=True)
    return centred * lax.rsqrt(spread + EPS) * gain + bias


def batches(work):
    half = DEPTH // 2 // BATCH
    pl.loop(0, half)(lambda step: work(step * BATCH, 3))
    pl.loop(half, 2 * half)(lambda step: work(step * BATCH, 2))


def block_rows(first, count):
    return [[first + n + DEPTH * group for group in range(count)] for n in range(BATCH)]


def load_pairs(pair_ref, first, count):
    rows = [row for rows in block_rows(first, count) for row in rows]
    return jnp.concatenate([pair_ref[row].astype(jnp.float32) for row in rows], axis=0)


def pad_rows(values, count):
    size = count * COLUMNS
    empty = jnp.zeros((LANES - size, WIDTH), jnp.float32)
    return [
        jnp.concatenate([values[n * size : (n + 1) * size], empty], axis=0).astype(jnp.bfloat16)
        for n in range(BATCH)
    ]


def spread_columns(place_ref, valid_ref):
    lane = lax.broadcasted_iota(jnp.int32, (1, LANES), 1)
    inside = lane % COLUMNS
    found = jnp.zeros((1, LANES), jnp.float32)
    for column in range(COLUMNS):
        value = valid_ref[place_ref[1] + column].astype(jnp.float32)
        found = jnp.where(inside == column, value, found)
    return jnp.where(lane < 3 * COLUMNS, found, 0.0)


def mask_of(first, count, place_ref, valid_ref, columns):
    lane = lax.broadcasted_iota(jnp.int32, (1, LANES), 1)
    masks = []
    for rows in block_rows(first, count):
        mask = jnp.zeros((1, LANES), jnp.float32)
        for group, row in enumerate(rows):
            value = valid_ref[place_ref[0] + row].astype(jnp.float32)
            inside = (lane >= group * COLUMNS) & (lane < (group + 1) * COLUMNS)
            mask = jnp.where(inside, value, mask)
        masks.append(mask * columns)
    return jnp.concatenate(masks, axis=1)


def factor_rows(first, normed, weight_ref, mask, scratch):
    proj = lax.dot_general(
        weight_ref[...], normed, (((1,), (1,)), ((), ())), preferred_element_type=jnp.float32
    )
    factor = jax.nn.sigmoid(proj[HIDDEN:]) * proj[:HIDDEN] * mask
    for n in range(BATCH):
        place = pl.ds(first + n, HIDDEN, stride=STRIDE)
        scratch[place, :] = factor[:, n * LANES : (n + 1) * LANES]


def flat_chunk(values):
    return jnp.concatenate([values[n : n + SUB] for n in range(0, DEPTH, SUB)], axis=1)


def put_chunks(scratch, out_ref):
    for channel in range(HIDDEN):
        rows = scratch[pl.ds(channel * STRIDE, DEPTH), :]
        out_ref[channel] = flat_chunk(rows).astype(jnp.bfloat16)


SCRATCH = pltpu.VMEM(((HIDDEN + 1) * STRIDE, LANES), jnp.float32)


def right_kernel(
    place_ref, valid_ref, pair_ref, gain_ref, bias_ref, weight_ref, normed_ref, right_ref, right_s
):
    columns = spread_columns(place_ref, valid_ref)

    def work(first, count):
        values = load_pairs(pair_ref, first, count)
        pieces = pad_rows(normalize(values, gain_ref[...], bias_ref[...]), count)
        for n in range(BATCH):
            normed_ref[first + n] = pieces[n]
        mask = mask_of(first, count, place_ref, valid_ref, columns)
        factor_rows(first, jnp.concatenate(pieces, axis=0), weight_ref, mask, right_s)

    batches(work)
    put_chunks(right_s, right_ref)


def project_right(place, valid, pair, gain, bias, weight):
    return call(
        right_kernel, [NORMED, CHUNKS], [SMEM, SMEM, VMEM, VMEM, VMEM, VMEM], [SCRATCH]
    )(place, valid, pair, gain, bias, weight)


def load_normed(normed_ref, first):
    return normed_ref[pl.ds(first, BATCH)].reshape(BATCH * LANES, WIDTH)


def left_kernel(place_ref, valid_ref, normed_ref, weight_ref, left_ref, left_s):
    columns = spread_columns(place_ref, valid_ref)

    def work(first, count):
        mask = mask_of(first, count, place_ref, valid_ref, columns)
        factor_rows(first, load_normed(normed_ref, first), weight_ref, mask, left_s)

    batches(work)
    put_chunks(left_s, left_ref)


def project_left(place, valid, normed, weight):
    return call(left_kernel, CHUNKS, [SMEM, SMEM, VMEM, VMEM], [SCRATCH])(
        place, valid, normed, weight
    )


def gate_kernel(place_ref, chain_ref, normed_ref, gate_ref, chain_bias_ref, out_ref):
    row = lax.broadcasted_iota(jnp.int32, (COLUMNS, WIDTH), 0)
    chain_columns = jnp.full((COLUMNS, WIDTH), -1, jnp.int32)
    for column in range(COLUMNS):
        chain_columns = jnp.where(row == column, chain_ref[place_ref[1] + column], chain_columns)

    def work(first, count):
        logit = jnp.dot(
            load_normed(normed_ref, first), gate_ref[...], preferred_element_type=jnp.float32
        )
        for n, rows in enumerate(block_rows(first, count)):
            for group, row in enumerate(rows):
                same = chain_columns == chain_ref[place_ref[0] + row]
                start = n * LANES + group * COLUMNS
                out_ref[first + n, pl.ds(group * COLUMNS, COLUMNS)] = jax.nn.sigmoid(
                    logit[start : start + COLUMNS] + jnp.where(same, chain_bias_ref[...], 0.0)
                )

    batches(work)


def gates(place, chain, normed, gate, chain_bias):
    return call(gate_kernel, GATES, [SMEM, SMEM, VMEM, VMEM, VMEM])(
        place, chain, normed, gate, chain_bias
    )


def finish_kernel(
    then,
    place_ref,
    valid_ref,
    out_gain_ref,
    pair_ref,
    gates_ref,
    product_ref,
    out_weight_ref,
    *rest,
):
    if then:
        gain_ref, bias_ref, weight_ref, out_ref, normed_ref, right_ref, hidden_s, right_s = rest
        columns = spread_columns(place_ref, valid_ref)
    else:
        out_ref, hidden_s = rest

    def channel(n):
        return product_ref[n].astype(jnp.float32)

    average = channel(0)
    for n in range(1, HIDDEN):
        average = average + channel(n)
    average = average / HIDDEN
    spread = jnp.zeros_like(average)
    for n in range(HIDDEN):
        centred = channel(n) - average
        spread = spread + centred * centred
    scale = lax.rsqrt(spread / HIDDEN + EPS)
    for n in range(HIDDEN):
        hidden = (channel(n) - average) * scale * out_gain_ref[n]
        for part in range(DEPTH // SUB):
            place = pl.ds(n * STRIDE + part * SUB, SUB)
            hidden_s[place, :] = hidden[:, part * LANES : (part + 1) * LANES]

    def work(first, count):
        size = count * COLUMNS
        values = load_pairs(pair_ref, first, count)
        hidden = jnp.concatenate(
            [hidden_s[pl.ds(first + n, HIDDEN, stride=STRIDE), :] for n in range(BATCH)], axis=1
        ).astype(jnp.bfloat16)
        branch = lax.dot_general(
            hidden,
            out_weight_ref[...],
            (((0,), (0,)), ((), ())),
            preferred_element_type=jnp.float32,
        )
        branch = jnp.concatenate(
            [
                branch[n * LANES : n * LANES + size] * gates_ref[first + n, pl.ds(0, size)]
                for n in range(BATCH)
            ],
            axis=0,
        )
        new = values + branch
        places = [row for rows in block_rows(first, count) for row in rows]
        for n, row in enumerate(places):
            out_ref[row] = new[n * COLUMNS : (n + 1) * COLUMNS].astype(jnp.bfloat16)
        if then:
            new = new.astype(jnp.bfloat16).astype(jnp.float32)
            pieces = pad_rows(normalize(new, gain_ref[...], bias_ref[...]), count)
            for n in range(BATCH):
                normed_ref[first + n] = pieces[n]
            mask = mask_of(first, count, place_ref, valid_ref, columns)
            factor_rows(first, jnp.concatenate(pieces, axis=0), weight_ref, mask, right_s)

    batches(work)
    if then:
        put_chunks(right_s, right_ref)


def finish(place, valid, out_gain, pair, gate, product, out_weight, then=()):
    out = jax.ShapeDtypeStruct(pair.shape, pair.dtype)
    return call(
        functools.partial(finish_kernel, bool(then)),
        [out, NORMED, CHUNKS] if then else [out],
        [SMEM] * 3 + [VMEM] * (4 + len(then)),
        [SCRATCH] * (2 if then else 1),
    )(place, valid, out_gain, pair, gate, product, out_weight, *then)


def gather_rows(chunks_ref, zh, group, part):
    start = part * LANES + group * COLUMNS
    return jnp.concatenate(
        [
            chunks_ref[span * ZH + zh].astype(jnp.float32)[:, start : start + COLUMNS]
            for span in range(SPAN)
        ],
        axis=1,
    )


def assemble_into(chunks_ref, put):
    for zh in range(ZH):
        for group, (start, size) in enumerate(GROUPS):
            for part in range(0, size // SUB, 2):
                rows = [gather_rows(chunks_ref, zh, group, part + n) for n in range(2)]
                put(zh * ROWS + start + part * SUB, jnp.concatenate(rows, axis=0))


def assemble_kernel(chunks_ref, out_ref):
    def put(start, values):
        out_ref[pl.ds(start, 2 * SUB), :] = values.astype(jnp.bfloat16)

    assemble_into(chunks_ref, put)


def assemble(chunks):
    out = jax.ShapeDtypeStruct((ZH * ROWS, SPAN * COLUMNS), jnp.bfloat16)
    return call(assemble_kernel, out, [VMEM])(chunks)


def assemble_turned_kernel(chunks_ref, out_ref, whole):
    def put(start, values):
        whole[pl.ds(start, 2 * SUB), :] = values

    assemble_into(chunks_ref, put)
    whole[pl.ds(ZH * ROWS, 64), :] = jnp.zeros((64, SPAN * COLUMNS), jnp.float32)
    for part in range(SPAN * COLUMNS // 128):
        turned = whole[:, part * 128 : (part + 1) * 128].T
        out_ref[pl.ds(part * 128, 128), :] = turned[:, : ZH * ROWS].astype(jnp.bfloat16)


def assemble_turned(chunks):
    out = jax.ShapeDtypeStruct((SPAN * COLUMNS, ZH * ROWS), jnp.bfloat16)
    scratch = [pltpu.VMEM((ZH * ROWS + 64, SPAN * COLUMNS), jnp.float32)]
    return call(assemble_turned_kernel, out, [VMEM], scratch)(chunks)


def chunk_of(total, zh, start):
    pieces = []
    for first, size in GROUPS:
        piece = total[pl.ds(zh * ROWS + first, size), :][:, start : start + COLUMNS]
        if size < DEPTH:
            piece = jnp.concatenate(
                [piece, jnp.zeros((DEPTH - size, COLUMNS), jnp.float32)], axis=0
            )
        pieces.append(piece)
    pieces.append(jnp.zeros((DEPTH, LANES - 3 * COLUMNS), jnp.float32))
    return flat_chunk(jnp.concatenate(pieces, axis=1)).astype(jnp.bfloat16)


def outgoing_kernel(core_ref, left_ref, right_ref, out_ref, left_s, total):
    assemble_kernel(left_ref, left_s)
    for x in range(X):
        total[:, x * ZH * ROWS : (x + 1) * ZH * ROWS] = lax.dot_general(
            left_s[...],
            right_ref[pl.ds(x * ZH * ROWS, ZH * ROWS), :],
            (((1,), (1,)), ((), ())),
            preferred_element_type=jnp.float32,
        )
    for half in range(2):
        slot = lax.rem(core_ref[0] + half, 2)
        for span in range(SPAN):
            for zh in range(ZH):
                out_ref[slot, span * ZH + zh] = chunk_of(total, zh, (2 * span + half) * COLUMNS)


def outgoing(core, left, right):
    out = jax.ShapeDtypeStruct((2,) + CHUNKS.shape, jnp.bfloat16)
    scratch = [
        pltpu.VMEM((ZH * ROWS, SPAN * COLUMNS), jnp.bfloat16),
        pltpu.VMEM((ZH * ROWS, X * ZH * ROWS), jnp.float32),
    ]
    return call(outgoing_kernel, out, [SMEM, VMEM, VMEM], scratch, 6 * 10**8)(core, left, right)


def incoming_kernel(core_ref, own_ref, other_ref, right_ref, out_ref, total):
    for n, left_ref in enumerate((own_ref, other_ref)):
        side = lax.rem(core_ref[0] + n, 2)
        product = jnp.zeros((ZH * COLUMNS, SPAN * COLUMNS), jnp.float32)
        for x in range(X):
            product = product + jnp.dot(
                left_ref[x],
                right_ref[pl.ds(x * ZH * ROWS, ZH * ROWS), :],
                preferred_element_type=jnp.float32,
            )
        for zh in range(ZH):
            start = pl.multiple_of(zh * ROWS + side * COLUMNS, 8)
            total[pl.ds(start, COLUMNS), :] = product[zh * COLUMNS : (zh + 1) * COLUMNS]
    for span in range(SPAN):
        for zh in range(ZH):
            out_ref[span * ZH + zh] = chunk_of(total, zh, span * COLUMNS)


def incoming(core, own, other, right):
    scratch = [pltpu.VMEM((ZH * ROWS, SPAN * COLUMNS), jnp.float32)]
    return call(incoming_kernel, CHUNKS, [SMEM, VMEM, VMEM, VMEM], scratch, 6 * 10**8)(
        core, own, other, right
    )


def exchange(values, axes):
    return lax.all_to_all(values, axes, split_axis=0, concat_axis=0, tiled=True)


def swap_cores(values):
    return lax.ppermute(values, "core", [(0, 1), (1, 0)])


def body(
    pair_acts,
    residue_valid,
    chain_index,
    norm_gain,
    norm_bias,
    projection,
    gate_weight,
    chain_bias,
    out_gain,
    out_weight,
):
    row_start = (lax.axis_index("x") * ZH + lax.axis_index("zh")) * ROWS
    core_index = lax.axis_index("core")
    column_block = (lax.axis_index("zl") * 8 + lax.axis_index("y")) * 2 + core_index
    place = jnp.stack([row_start, column_block * COLUMNS]).astype(jnp.int32)
    core = core_index.reshape(1).astype(jnp.int32)
    turned = projection.transpose(0, 2, 1)

    normed, right = project_right(
        place, residue_valid, pair_acts, norm_gain[:1], norm_bias[:1], turned[0, 2 * HIDDEN :]
    )
    right = assemble(exchange(right, PLANE))
    right = lax.all_gather(right, "x", axis=0, tiled=True)
    left = project_left(place, residue_valid, normed, turned[0, : 2 * HIDDEN])
    gate = gates(place, chain_index, normed, gate_weight[0], chain_bias[:1])
    halves = outgoing(core, exchange(left, PLANE), right)
    total = halves[0].astype(jnp.float32) + swap_cores(halves[1]).astype(jnp.float32)
    product = exchange(total.astype(jnp.bfloat16), PLANE)
    middle, normed, right = finish(
        place,
        residue_valid,
        out_gain[0],
        pair_acts,
        gate,
        product,
        out_weight[0],
        (norm_gain[1:], norm_bias[1:], turned[1, 2 * HIDDEN :]),
    )
    right = assemble(exchange(right, PLANE))
    right = lax.all_gather(right, "x", axis=0, tiled=True)
    left = project_left(place, residue_valid, normed, turned[1, : 2 * HIDDEN])
    gate = gates(place, chain_index, normed, gate_weight[1], chain_bias[1:])
    left = assemble_turned(exchange(left, PLANE)).reshape(X, ZH * COLUMNS, ZH * ROWS)
    left = exchange(left, "x")
    product = exchange(incoming(core, left, swap_cores(left), right), PLANE)
    return finish(
        place, residue_valid, out_gain[1], middle, gate, product, out_weight[1]
    )[0]


def solution(mesh):
    fine = Mesh(mesh.devices.reshape(SIZES), AXES)
    pairs = P(("x", "zh"), ("zl", "y", "core"), None)
    placed = (pairs, P(), P(), P(), P(), P(), P(), P(), P(), P())
    return jax.shard_map(body, mesh=fine, in_specs=placed, out_specs=pairs, check_vma=False)
```

```python
import functools

import jax
import jax.numpy as jnp
from jax import lax
from jax.experimental import pallas as pl
from jax.experimental.pallas import tpu as pltpu
from jax.sharding import Mesh
from jax.sharding import PartitionSpec as P

AXES = ("zl", "y", "core", "x", "zh")
SIZES = (2, 8, 2, 4, 4)
PLANE = ("y", "zh", "zl")
ROWS = 80
COLUMNS = 40
WIDTH = 128
HIDDEN = 64
X = 4
ZH = 4
SPAN = 16
EPS = 1e-05
DEPTH = 32
LANES = 128
SUB = 8
GROUPS = ((0, 32), (32, 32), (64, 16))
STRIDE = 40
BATCH = 8
CHUNKS = jax.ShapeDtypeStruct((HIDDEN, SUB, DEPTH // SUB * LANES), jnp.bfloat16)
NORMED = jax.ShapeDtypeStruct((DEPTH, LANES, WIDTH), jnp.bfloat16)
GATES = jax.ShapeDtypeStruct((DEPTH, LANES, WIDTH), jnp.float32)
VMEM = pl.BlockSpec(memory_space=pltpu.VMEM)
ANY = pl.BlockSpec(memory_space=pl.ANY)
SMEM = pl.BlockSpec(memory_space=pltpu.SMEM)


def spot(span, zh):
    zl, y = divmod(span, 8)
    return (y * ZH + zh) * 2 + zl


def call(kernel, out_shape, in_specs, scratch_shapes=(), flops=10**8, outs=None):
    outs = outs or jax.tree.map(lambda _: VMEM, out_shape)
    moved = 4 * 10**6
    return pl.pallas_call(
        kernel,
        out_shape=out_shape,
        in_specs=in_specs,
        out_specs=outs,
        scratch_shapes=scratch_shapes,
        compiler_params=pltpu.CompilerParams(vmem_limit_bytes=40 * 2**20),
        cost_estimate=pl.CostEstimate(flops=flops, bytes_accessed=moved, transcendentals=0),
    )


def normalize(values, gain, bias):
    average = jnp.mean(values, axis=-1, keepdims=True)
    centred = values - average
    spread = jnp.mean(centred * centred, axis=-1, keepdims=True)
    return centred * lax.rsqrt(spread + EPS) * gain + bias


def batches(work):
    half = DEPTH // 2 // BATCH
    pl.loop(0, half)(lambda step: work(step * BATCH, 3))
    pl.loop(half, 2 * half)(lambda step: work(step * BATCH, 2))


def block_rows(first, count):
    return [[first + n + DEPTH * group for group in range(count)] for n in range(BATCH)]


def load_pairs(pair_ref, first, count):
    rows = [row for rows in block_rows(first, count) for row in rows]
    return jnp.concatenate([pair_ref[row].astype(jnp.float32) for row in rows], axis=0)


def pad_rows(values, count):
    size = count * COLUMNS
    empty = jnp.zeros((LANES - size, WIDTH), jnp.float32)
    return [
        jnp.concatenate([values[n * size : (n + 1) * size], empty], axis=0).astype(jnp.bfloat16)
        for n in range(BATCH)
    ]


def spread_columns(place_ref, valid_ref):
    lane = lax.broadcasted_iota(jnp.int32, (1, LANES), 1)
    inside = lane % COLUMNS
    found = jnp.zeros((1, LANES), jnp.float32)
    for column in range(COLUMNS):
        value = valid_ref[place_ref[1] + column].astype(jnp.float32)
        found = jnp.where(inside == column, value, found)
    return jnp.where(lane < 3 * COLUMNS, found, 0.0)


def mask_of(first, count, place_ref, valid_ref, columns):
    lane = lax.broadcasted_iota(jnp.int32, (1, LANES), 1)
    masks = []
    for rows in block_rows(first, count):
        mask = jnp.zeros((1, LANES), jnp.float32)
        for group, row in enumerate(rows):
            value = valid_ref[place_ref[0] + row].astype(jnp.float32)
            inside = (lane >= group * COLUMNS) & (lane < (group + 1) * COLUMNS)
            mask = jnp.where(inside, value, mask)
        masks.append(mask * columns)
    return jnp.concatenate(masks, axis=1)


def weight_of(weight_ref, which, start):
    columns = weight_ref[which][:, start : start + 2 * HIDDEN]
    return columns.astype(jnp.float32).T.astype(jnp.bfloat16)


def factor_rows(first, normed, weight, mask, scratch):
    proj = lax.dot_general(
        weight, normed, (((1,), (1,)), ((), ())), preferred_element_type=jnp.float32
    )
    factor = jax.nn.sigmoid(proj[HIDDEN:]) * proj[:HIDDEN] * mask
    for n in range(BATCH):
        place = pl.ds(first + n, HIDDEN, stride=STRIDE)
        scratch[place, :] = factor[:, n * LANES : (n + 1) * LANES]


def flat_chunk(values):
    return jnp.concatenate([values[n : n + SUB] for n in range(0, DEPTH, SUB)], axis=1)


def put_chunks(scratch, out_ref):
    for channel in range(HIDDEN):
        rows = scratch[pl.ds(channel * STRIDE, DEPTH), :]
        out_ref[channel] = flat_chunk(rows).astype(jnp.bfloat16)


SCRATCH = pltpu.VMEM(((HIDDEN + 1) * STRIDE, LANES), jnp.float32)


def right_kernel(
    place_ref, valid_ref, pair_ref, gain_ref, bias_ref, weight_ref, normed_ref, right_ref, right_s
):
    columns = spread_columns(place_ref, valid_ref)
    weight = weight_of(weight_ref, 0, 2 * HIDDEN)

    def work(first, count):
        values = load_pairs(pair_ref, first, count)
        pieces = pad_rows(normalize(values, gain_ref[0:1], bias_ref[0:1]), count)
        for n in range(BATCH):
            normed_ref[first + n] = pieces[n]
        mask = mask_of(first, count, place_ref, valid_ref, columns)
        factor_rows(first, jnp.concatenate(pieces, axis=0), weight, mask, right_s)

    batches(work)
    put_chunks(right_s, right_ref)


def project_right(place, valid, pair, gain, bias, weight):
    return call(
        right_kernel, [NORMED, CHUNKS], [SMEM, SMEM, VMEM, VMEM, VMEM, VMEM], [SCRATCH]
    )(place, valid, pair, gain, bias, weight)


def load_normed(normed_ref, first):
    return normed_ref[pl.ds(first, BATCH)].reshape(BATCH * LANES, WIDTH)


def left_work(which, place_ref, valid_ref, normed_ref, weight_ref, left_s):
    columns = spread_columns(place_ref, valid_ref)
    weight = weight_of(weight_ref, which, 0)

    def work(first, count):
        mask = mask_of(first, count, place_ref, valid_ref, columns)
        factor_rows(first, load_normed(normed_ref, first), weight, mask, left_s)

    return work


def gate_work(which, place_ref, chain_ref, normed_ref, gate_ref, chain_bias_ref, out_ref):
    row = lax.broadcasted_iota(jnp.int32, (COLUMNS, WIDTH), 0)
    chain_columns = jnp.full((COLUMNS, WIDTH), -1, jnp.int32)
    for column in range(COLUMNS):
        chain_columns = jnp.where(row == column, chain_ref[place_ref[1] + column], chain_columns)
    offset = chain_bias_ref[which : which + 1]

    def work(first, count):
        logit = jnp.dot(
            load_normed(normed_ref, first), gate_ref[which], preferred_element_type=jnp.float32
        )
        for n, rows in enumerate(block_rows(first, count)):
            for group, row in enumerate(rows):
                same = chain_columns == chain_ref[place_ref[0] + row]
                start = n * LANES + group * COLUMNS
                out_ref[first + n, pl.ds(group * COLUMNS, COLUMNS)] = jax.nn.sigmoid(
                    logit[start : start + COLUMNS] + jnp.where(same, offset, 0.0)
                )

    return work


def left_kernel(which, place_ref, valid_ref, normed_ref, weight_ref, left_ref, left_s):
    batches(left_work(which, place_ref, valid_ref, normed_ref, weight_ref, left_s))
    put_chunks(left_s, left_ref)


def project_left(which, place, valid, normed, weight):
    kernel = functools.partial(left_kernel, which)
    return call(kernel, CHUNKS, [SMEM, SMEM, VMEM, VMEM], [SCRATCH])(place, valid, normed, weight)


def gate_kernel(
    which,
    place_ref,
    chain_ref,
    normed_ref,
    gate_ref,
    chain_bias_ref,
    pair_ref,
    out_ref,
    kept_ref,
    sem,
):
    keep = pltpu.make_async_copy(pair_ref, kept_ref, sem)
    keep.start()
    batches(
        gate_work(which, place_ref, chain_ref, normed_ref, gate_ref, chain_bias_ref, out_ref)
    )
    keep.wait()


def gates(which, place, chain, normed, gate, chain_bias, pair):
    kernel = functools.partial(gate_kernel, which)
    return call(
        kernel,
        [GATES, jax.ShapeDtypeStruct(pair.shape, pair.dtype)],
        [SMEM, SMEM, VMEM, VMEM, VMEM, ANY],
        [pltpu.SemaphoreType.DMA],
    )(place, chain, normed, gate, chain_bias, pair)


def left_and_gate_kernel(
    which,
    place_ref,
    valid_ref,
    chain_ref,
    normed_ref,
    weight_ref,
    gate_ref,
    chain_bias_ref,
    left_ref,
    out_ref,
    left_s,
):
    left = left_work(which, place_ref, valid_ref, normed_ref, weight_ref, left_s)
    gate = gate_work(which, place_ref, chain_ref, normed_ref, gate_ref, chain_bias_ref, out_ref)

    def work(first, count):
        left(first, count)
        gate(first, count)

    batches(work)
    put_chunks(left_s, left_ref)


def left_and_gates(which, place, valid, chain, normed, weight, gate, chain_bias):
    kernel = functools.partial(left_and_gate_kernel, which)
    return call(kernel, [CHUNKS, GATES], [SMEM] * 3 + [VMEM] * 4, [SCRATCH])(
        place, valid, chain, normed, weight, gate, chain_bias
    )


def finish_kernel(
    which,
    place_ref,
    valid_ref,
    out_gain_ref,
    pair_ref,
    gates_ref,
    product_ref,
    out_weight_ref,
    *rest,
):
    then = which == 0
    if then:
        gain_ref, bias_ref, weight_ref, out_ref, normed_ref, right_ref = rest[:6]
        hidden_s, right_s = rest[6:]
        new_s = out_ref
        columns = spread_columns(place_ref, valid_ref)
        weight = weight_of(weight_ref, 1, 2 * HIDDEN)
    else:
        out_ref, hidden_s, new_s, out_sem = rest

    def channel(n):
        return product_ref[n].astype(jnp.float32)

    average = channel(0)
    for n in range(1, HIDDEN):
        average = average + channel(n)
    average = average / HIDDEN
    spread = jnp.zeros_like(average)
    for n in range(HIDDEN):
        centred = channel(n) - average
        spread = spread + centred * centred
    scale = lax.rsqrt(spread / HIDDEN + EPS)
    for n in range(HIDDEN):
        hidden = (channel(n) - average) * scale * out_gain_ref[which, n]
        for part in range(DEPTH // SUB):
            place = pl.ds(n * STRIDE + part * SUB, SUB)
            hidden_s[place, :] = hidden[:, part * LANES : (part + 1) * LANES]

    def work(first, count):
        size = count * COLUMNS
        values = load_pairs(pair_ref, first, count)
        hidden = jnp.concatenate(
            [hidden_s[pl.ds(first + n, HIDDEN, stride=STRIDE), :] for n in range(BATCH)], axis=1
        ).astype(jnp.bfloat16)
        branch = lax.dot_general(
            hidden,
            out_weight_ref[which],
            (((0,), (0,)), ((), ())),
            preferred_element_type=jnp.float32,
        )
        branch = jnp.concatenate(
            [
                branch[n * LANES : n * LANES + size] * gates_ref[first + n, pl.ds(0, size)]
                for n in range(BATCH)
            ],
            axis=0,
        )
        new = values + branch
        places = [row for rows in block_rows(first, count) for row in rows]
        for n, row in enumerate(places):
            new_s[row] = new[n * COLUMNS : (n + 1) * COLUMNS].astype(jnp.bfloat16)
        if not then:
            for group in range(count):
                span = pl.ds(first + DEPTH * group, BATCH)
                pltpu.make_async_copy(new_s.at[span], out_ref.at[span], out_sem).start()
        if then:
            new = new.astype(jnp.bfloat16).astype(jnp.float32)
            pieces = pad_rows(normalize(new, gain_ref[1:2], bias_ref[1:2]), count)
            for n in range(BATCH):
                normed_ref[first + n] = pieces[n]
            mask = mask_of(first, count, place_ref, valid_ref, columns)
            factor_rows(first, jnp.concatenate(pieces, axis=0), weight, mask, right_s)

    batches(work)
    if then:
        put_chunks(right_s, right_ref)
    else:
        pltpu.make_async_copy(new_s, out_ref, out_sem).wait()


def finish(which, place, valid, out_gain, pair, gate, product, out_weight, then=()):
    out = jax.ShapeDtypeStruct(pair.shape, pair.dtype)
    last = [pltpu.VMEM(pair.shape, pair.dtype), pltpu.SemaphoreType.DMA]
    return call(
        functools.partial(finish_kernel, which),
        [out, NORMED, CHUNKS] if then else [out],
        [SMEM] * 3 + [VMEM] * (4 + len(then)),
        [SCRATCH] + ([SCRATCH] if then else last),
        outs=None if then else [ANY],
    )(place, valid, out_gain, pair, gate, product, out_weight, *then)


def gather_rows(chunks_ref, zh, group, part):
    start = part * LANES + group * COLUMNS
    return jnp.concatenate(
        [
            chunks_ref[spot(span, zh)].astype(jnp.float32)[:, start : start + COLUMNS]
            for span in range(SPAN)
        ],
        axis=1,
    )


def assemble_into(chunks_ref, put):
    for zh in range(ZH):
        for group, (start, size) in enumerate(GROUPS):
            for part in range(0, size // SUB, 2):
                rows = [gather_rows(chunks_ref, zh, group, part + n) for n in range(2)]
                put(zh * ROWS + start + part * SUB, jnp.concatenate(rows, axis=0))


def assemble_kernel(chunks_ref, out_ref):
    def put(start, values):
        out_ref[pl.ds(start, 2 * SUB), :] = values.astype(jnp.bfloat16)

    assemble_into(chunks_ref, put)


def assemble(chunks):
    out = jax.ShapeDtypeStruct((ZH * ROWS, SPAN * COLUMNS), jnp.bfloat16)
    return call(assemble_kernel, out, [VMEM])(chunks)


def assemble_turned_kernel(chunks_ref, out_ref, whole):
    def put(start, values):
        whole[pl.ds(start, 2 * SUB), :] = values

    assemble_into(chunks_ref, put)
    whole[pl.ds(ZH * ROWS, 64), :] = jnp.zeros((64, SPAN * COLUMNS), jnp.float32)
    for part in range(SPAN * COLUMNS // 128):
        turned = whole[:, part * 128 : (part + 1) * 128].T
        out_ref[pl.ds(part * 128, 128), :] = turned[:, : ZH * ROWS].astype(jnp.bfloat16)


def assemble_turned(chunks):
    out = jax.ShapeDtypeStruct((SPAN * COLUMNS, ZH * ROWS), jnp.bfloat16)
    scratch = [pltpu.VMEM((ZH * ROWS + 64, SPAN * COLUMNS), jnp.float32)]
    return call(assemble_turned_kernel, out, [VMEM], scratch)(chunks)


def chunk_of(total, zh, start):
    pieces = []
    for first, size in GROUPS:
        piece = total[pl.ds(zh * ROWS + first, size), :][:, start : start + COLUMNS]
        if size < DEPTH:
            piece = jnp.concatenate(
                [piece, jnp.zeros((DEPTH - size, COLUMNS), jnp.float32)], axis=0
            )
        pieces.append(piece)
    pieces.append(jnp.zeros((DEPTH, LANES - 3 * COLUMNS), jnp.float32))
    return flat_chunk(jnp.concatenate(pieces, axis=1)).astype(jnp.bfloat16)


def outgoing_kernel(core_ref, left_ref, right_ref, out_ref, left_s, total):
    assemble_kernel(left_ref, left_s)
    for x in range(X):
        total[:, x * ZH * ROWS : (x + 1) * ZH * ROWS] = lax.dot_general(
            left_s[...],
            right_ref[pl.ds(x * ZH * ROWS, ZH * ROWS), :],
            (((1,), (1,)), ((), ())),
            preferred_element_type=jnp.float32,
        )
    for half in range(2):
        slot = lax.rem(core_ref[0] + half, 2)
        for span in range(SPAN):
            for zh in range(ZH):
                out_ref[slot, spot(span, zh)] = chunk_of(total, zh, (2 * span + half) * COLUMNS)


def outgoing(core, left, right):
    out = jax.ShapeDtypeStruct((2,) + CHUNKS.shape, jnp.bfloat16)
    scratch = [
        pltpu.VMEM((ZH * ROWS, SPAN * COLUMNS), jnp.bfloat16),
        pltpu.VMEM((ZH * ROWS, X * ZH * ROWS), jnp.float32),
    ]
    return call(outgoing_kernel, out, [SMEM, VMEM, VMEM], scratch, 6 * 10**8)(core, left, right)


def incoming_kernel(core_ref, own_ref, other_ref, right_ref, out_ref, total):
    for n, left_ref in enumerate((own_ref, other_ref)):
        side = lax.rem(core_ref[0] + n, 2)
        product = jnp.zeros((ZH * COLUMNS, SPAN * COLUMNS), jnp.float32)
        for x in range(X):
            product = product + jnp.dot(
                left_ref[x],
                right_ref[pl.ds(x * ZH * ROWS, ZH * ROWS), :],
                preferred_element_type=jnp.float32,
            )
        for zh in range(ZH):
            start = pl.multiple_of(zh * ROWS + side * COLUMNS, 8)
            total[pl.ds(start, COLUMNS), :] = product[zh * COLUMNS : (zh + 1) * COLUMNS]
    for span in range(SPAN):
        for zh in range(ZH):
            out_ref[spot(span, zh)] = chunk_of(total, zh, span * COLUMNS)


def incoming(core, own, other, right):
    scratch = [pltpu.VMEM((ZH * ROWS, SPAN * COLUMNS), jnp.float32)]
    return call(incoming_kernel, CHUNKS, [SMEM, VMEM, VMEM, VMEM], scratch, 6 * 10**8)(
        core, own, other, right
    )


def exchange(values, axes):
    return lax.all_to_all(values, axes, split_axis=0, concat_axis=0, tiled=True)


def swap_cores(values):
    return lax.ppermute(values, "core", [(0, 1), (1, 0)])


def body(
    pair_acts,
    residue_valid,
    chain_index,
    norm_gain,
    norm_bias,
    projection,
    gate_weight,
    chain_bias,
    out_gain,
    out_weight,
):
    row_start = (lax.axis_index("x") * ZH + lax.axis_index("zh")) * ROWS
    core_index = lax.axis_index("core")
    column_block = (lax.axis_index("zl") * 8 + lax.axis_index("y")) * 2 + core_index
    place = jnp.stack([row_start, column_block * COLUMNS]).astype(jnp.int32)
    core = core_index.reshape(1).astype(jnp.int32)

    normed, right = project_right(
        place, residue_valid, pair_acts, norm_gain, norm_bias, projection
    )
    right = assemble(exchange(right, PLANE))
    right = lax.all_gather(right, "x", axis=0, tiled=True)
    left, gate = left_and_gates(
        0, place, residue_valid, chain_index, normed, projection, gate_weight, chain_bias
    )
    halves = outgoing(core, exchange(left, PLANE), right)
    total = halves[0].astype(jnp.float32) + swap_cores(halves[1]).astype(jnp.float32)
    product = exchange(total.astype(jnp.bfloat16), PLANE)
    middle, normed, right = finish(
        0,
        place,
        residue_valid,
        out_gain,
        pair_acts,
        gate,
        product,
        out_weight,
        (norm_gain, norm_bias, projection),
    )
    right = assemble(exchange(right, PLANE))
    right = lax.all_gather(right, "x", axis=0, tiled=True)
    left = project_left(1, place, residue_valid, normed, projection)
    gate, middle = gates(1, place, chain_index, normed, gate_weight, chain_bias, middle)
    left = assemble_turned(exchange(left, PLANE)).reshape(X, ZH * COLUMNS, ZH * ROWS)
    left = exchange(left, "x")
    product = exchange(incoming(core, left, swap_cores(left), right), PLANE)
    return finish(1, place, residue_valid, out_gain, middle, gate, product, out_weight)[0]


def solution(mesh):
    fine = Mesh(mesh.devices.reshape(SIZES), AXES)
    pairs = P(("x", "zh"), ("zl", "y", "core"), None)
    placed = (pairs, P(), P(), P(), P(), P(), P(), P(), P(), P())
    return jax.shard_map(body, mesh=fine, in_specs=placed, out_specs=pairs, check_vma=False)
```

```python
import functools

import jax
import jax.numpy as jnp
from jax import lax
from jax.experimental import pallas as pl
from jax.experimental.pallas import tpu as pltpu
from jax.sharding import Mesh
from jax.sharding import PartitionSpec as P

AXES = ("zl", "y", "core", "x", "zh")
SIZES = (2, 8, 2, 4, 4)
PLANE = ("y", "zh", "zl")
ROWS = 80
COLUMNS = 40
WIDTH = 128
HIDDEN = 64
X = 4
ZH = 4
SPAN = 16
EPS = 1e-05
DEPTH = 32
LANES = 128
SUB = 8
WHOLE = 3
TAIL = 8 * 9
STRIDE = 40
BOTH = 56
BATCH = 8
CHUNKS = jax.ShapeDtypeStruct((HIDDEN, SUB, DEPTH // SUB * LANES), jnp.bfloat16)
BOTH_CHUNKS = jax.ShapeDtypeStruct((HIDDEN, SUB, BOTH // SUB * LANES), jnp.bfloat16)
NORMED = jax.ShapeDtypeStruct((DEPTH, LANES, WIDTH), jnp.bfloat16)
GATES = jax.ShapeDtypeStruct((2, DEPTH, LANES, WIDTH), jnp.float32)
VMEM = pl.BlockSpec(memory_space=pltpu.VMEM)
ANY = pl.BlockSpec(memory_space=pl.ANY)
SMEM = pl.BlockSpec(memory_space=pltpu.SMEM)


def spot(span, zh):
    zl, y = divmod(span, 8)
    return (y * ZH + zh) * 2 + zl


def call(kernel, out_shape, in_specs, scratch_shapes=(), flops=10**8, outs=None, grant=40):
    outs = outs or jax.tree.map(lambda _: VMEM, out_shape)
    moved = 4 * 10**6
    return pl.pallas_call(
        kernel,
        out_shape=out_shape,
        in_specs=in_specs,
        out_specs=outs,
        scratch_shapes=scratch_shapes,
        compiler_params=pltpu.CompilerParams(vmem_limit_bytes=grant * 2**20),
        cost_estimate=pl.CostEstimate(flops=flops, bytes_accessed=moved, transcendentals=0),
    )


def normalize(values, gain, bias):
    average = jnp.mean(values, axis=-1, keepdims=True)
    centred = values - average
    spread = jnp.mean(centred * centred, axis=-1, keepdims=True)
    return centred * lax.rsqrt(spread + EPS) * gain + bias


def batches(work):
    pl.loop(0, WHOLE)(lambda step: work(step * BATCH, 3))
    work(WHOLE * BATCH, 1)


def block_rows(first, count):
    if count == 1:
        return [[TAIL + n] for n in range(BATCH)]
    return [[first + n + WHOLE * SUB * group for group in range(count)] for n in range(BATCH)]


def load_pairs(pair_ref, first, count):
    rows = [row for rows in block_rows(first, count) for row in rows]
    return jnp.concatenate([pair_ref[row].astype(jnp.float32) for row in rows], axis=0)


def pad_rows(values, count):
    size = count * COLUMNS
    empty = jnp.zeros((LANES - size, WIDTH), jnp.float32)
    return [
        jnp.concatenate([values[n * size : (n + 1) * size], empty], axis=0).astype(jnp.bfloat16)
        for n in range(BATCH)
    ]


def spread_columns(place_ref, valid_ref):
    lane = lax.broadcasted_iota(jnp.int32, (1, LANES), 1)
    inside = lane % COLUMNS
    found = jnp.zeros((1, LANES), jnp.float32)
    for column in range(COLUMNS):
        value = valid_ref[place_ref[1] + column].astype(jnp.float32)
        found = jnp.where(inside == column, value, found)
    return jnp.where(lane < 3 * COLUMNS, found, 0.0)


def mask_of(first, count, place_ref, valid_ref, columns, shift=0):
    lane = lax.broadcasted_iota(jnp.int32, (1, LANES), 1)
    masks = []
    for rows in block_rows(first, count):
        mask = jnp.zeros((1, LANES), jnp.float32)
        for group, row in enumerate(rows):
            value = valid_ref[place_ref[0] + row].astype(jnp.float32)
            start = (group + shift) * COLUMNS
            inside = (lane >= start) & (lane < start + COLUMNS)
            mask = jnp.where(inside, value, mask)
        masks.append(mask * columns)
    return jnp.concatenate(masks, axis=1)


def weight_of(weight_ref, which, start):
    columns = weight_ref[which][:, start : start + 2 * HIDDEN]
    return columns.astype(jnp.float32).T.astype(jnp.bfloat16)


def factor_of(normed, weight, mask):
    proj = lax.dot_general(
        weight, normed, (((1,), (1,)), ((), ())), preferred_element_type=jnp.float32
    )
    return jax.nn.sigmoid(proj[HIDDEN:]) * proj[:HIDDEN] * mask


def keep_rows(factor, scratch, first, stride):
    for n in range(BATCH):
        place = pl.ds(first + n, HIDDEN, stride=stride)
        scratch[place, :] = factor[:, n * LANES : (n + 1) * LANES]


def put_chunks(scratch, out_ref, stride, depth):
    for channel in range(HIDDEN):
        rows = scratch[pl.ds(channel * stride, depth), :]
        tiles = [rows[n : n + SUB] for n in range(0, depth, SUB)]
        out_ref[channel] = jnp.concatenate(tiles, axis=1).astype(jnp.bfloat16)


SCRATCH = pltpu.VMEM(((HIDDEN + 1) * STRIDE, LANES), jnp.float32)


def right_kernel(
    place_ref,
    valid_ref,
    pair_any,
    gain_any,
    bias_any,
    weight_any,
    normed_ref,
    right_ref,
    right_s,
    pair_ref,
    gain_ref,
    bias_ref,
    weight_ref,
    sems,
):
    moves = ((pair_any, pair_ref), (gain_any, gain_ref), (bias_any, bias_ref), (weight_any, weight_ref))
    copies = [pltpu.make_async_copy(a, b, sems.at[n]) for n, (a, b) in enumerate(moves)]
    for copy in copies:
        copy.start()
    columns = spread_columns(place_ref, valid_ref)
    for copy in copies:
        copy.wait()
    weight = weight_of(weight_ref, 0, 2 * HIDDEN)

    def work(first, count):
        values = load_pairs(pair_ref, first, count)
        pieces = pad_rows(normalize(values, gain_ref[0:1], bias_ref[0:1]), count)
        for n in range(BATCH):
            normed_ref[first + n] = pieces[n]
        mask = mask_of(first, count, place_ref, valid_ref, columns)
        factor = factor_of(jnp.concatenate(pieces, axis=0), weight, mask)
        keep_rows(factor, right_s, first, STRIDE)

    batches(work)
    put_chunks(right_s, right_ref, STRIDE, DEPTH)


def project_right(place, valid, *operands):
    scratch = [pltpu.VMEM(each.shape, each.dtype) for each in operands]
    return call(
        right_kernel,
        [NORMED, CHUNKS],
        [SMEM, SMEM] + [ANY] * 4,
        [SCRATCH] + scratch + [pltpu.SemaphoreType.DMA((4,))],
        grant=60,
    )(place, valid, *operands)


def load_normed(normed_ref, first):
    return normed_ref[pl.ds(first, BATCH)].reshape(BATCH * LANES, WIDTH)


def gate_work(
    which, place_ref, chain_ref, normed_ref, gate_ref, chain_bias_ref, pair_ref, out_ref
):
    row = lax.broadcasted_iota(jnp.int32, (COLUMNS, WIDTH), 0)
    chain_columns = jnp.full((COLUMNS, WIDTH), -1, jnp.int32)
    for column in range(COLUMNS):
        chain_columns = jnp.where(row == column, chain_ref[place_ref[1] + column], chain_columns)
    offset = chain_bias_ref[which : which + 1]

    def work(first, count):
        logit = jnp.dot(
            load_normed(normed_ref, first), gate_ref[which], preferred_element_type=jnp.float32
        )
        for n, rows in enumerate(block_rows(first, count)):
            for group, row in enumerate(rows):
                same = chain_columns == chain_ref[place_ref[0] + row]
                start = n * LANES + group * COLUMNS
                place = pl.ds(group * COLUMNS, COLUMNS)
                out_ref[0, first + n, place] = jax.nn.sigmoid(
                    logit[start : start + COLUMNS] + jnp.where(same, offset, 0.0)
                )
                out_ref[1, first + n, place] = pair_ref[row].astype(jnp.float32)

    return work


def gate_kernel(which, *refs):
    batches(gate_work(which, *refs))


def gates(which, place, chain, normed, gate, chain_bias, pair):
    kernel = functools.partial(gate_kernel, which)
    return call(kernel, GATES, [SMEM, SMEM, VMEM, VMEM, VMEM, VMEM])(
        place, chain, normed, gate, chain_bias, pair
    )


def left_and_gate_kernel(
    place_ref,
    valid_ref,
    chain_ref,
    normed_ref,
    weight_ref,
    gate_ref,
    chain_bias_ref,
    pair_ref,
    left_ref,
    out_ref,
    left_s,
):
    columns = spread_columns(place_ref, valid_ref)
    weight = weight_of(weight_ref, 0, 0)
    gate = gate_work(
        0, place_ref, chain_ref, normed_ref, gate_ref, chain_bias_ref, pair_ref, out_ref
    )

    def work(first, count):
        mask = mask_of(first, count, place_ref, valid_ref, columns)
        keep_rows(factor_of(load_normed(normed_ref, first), weight, mask), left_s, first, STRIDE)
        gate(first, count)

    batches(work)
    put_chunks(left_s, left_ref, STRIDE, DEPTH)


def left_and_gates(place, valid, chain, normed, weight, gate, chain_bias, pair):
    return call(left_and_gate_kernel, [CHUNKS, GATES], [SMEM] * 3 + [VMEM] * 5, [SCRATCH])(
        place, valid, chain, normed, weight, gate, chain_bias, pair
    )


def finish_kernel(which, place_ref, valid_ref, out_gain_ref, gates_ref, product_ref, out_weight_ref, *rest):
    then = which == 0
    if then:
        gain_ref, bias_ref, weight_ref, out_ref, normed_ref, both_ref, hidden_s, both_s = rest
        new_s = out_ref
        columns = spread_columns(place_ref, valid_ref)
        left_weight = weight_of(weight_ref, 1, 0)
        right_weight = weight_of(weight_ref, 1, 2 * HIDDEN)
    else:
        out_ref, hidden_s, new_s, out_sem = rest

    def channel(n):
        return product_ref[n].astype(jnp.float32)

    average = channel(0)
    for n in range(1, HIDDEN):
        average = average + channel(n)
    average = average / HIDDEN
    spread = jnp.zeros_like(average)
    for n in range(HIDDEN):
        centred = channel(n) - average
        spread = spread + centred * centred
    scale = lax.rsqrt(spread / HIDDEN + EPS)
    for n in range(HIDDEN):
        hidden = (channel(n) - average) * scale * out_gain_ref[which, n]
        for part in range(DEPTH // SUB):
            place = pl.ds(n * STRIDE + part * SUB, SUB)
            hidden_s[place, :] = hidden[:, part * LANES : (part + 1) * LANES]

    def work(first, count):
        size = count * COLUMNS
        hidden = jnp.concatenate(
            [hidden_s[pl.ds(first + n, HIDDEN, stride=STRIDE), :] for n in range(BATCH)], axis=1
        ).astype(jnp.bfloat16)
        branch = lax.dot_general(
            hidden,
            out_weight_ref[which],
            (((0,), (0,)), ((), ())),
            preferred_element_type=jnp.float32,
        )
        new = jnp.concatenate(
            [
                gates_ref[1, first + n, pl.ds(0, size)]
                + gates_ref[0, first + n, pl.ds(0, size)] * branch[n * LANES : n * LANES + size]
                for n in range(BATCH)
            ],
            axis=0,
        )
        places = [row for rows in block_rows(first, count) for row in rows]
        for n, row in enumerate(places):
            new_s[row] = new[n * COLUMNS : (n + 1) * COLUMNS].astype(jnp.bfloat16)
        if not then:
            for group in range(count):
                span = pl.ds(block_rows(first, count)[0][group], BATCH)
                pltpu.make_async_copy(new_s.at[span], out_ref.at[span], out_sem).start()
            return
        new = new.astype(jnp.bfloat16).astype(jnp.float32)
        values = normalize(new, gain_ref[1:2], bias_ref[1:2])
        pieces = pad_rows(values, count)
        for n in range(BATCH):
            normed_ref[first + n] = pieces[n]
        mask = mask_of(first, count, place_ref, valid_ref, columns)
        if count == 3:
            normed = jnp.concatenate(pieces, axis=0)
            keep_rows(factor_of(normed, left_weight, mask), both_s, first, BOTH)
            right_first = first + WHOLE * SUB
            keep_rows(factor_of(normed, right_weight, mask), both_s, right_first, BOTH)
        else:
            twice = [values[n * size : (n + 1) * size] for n in range(BATCH) for _ in range(2)]
            normed = jnp.concatenate(
                [
                    each
                    for n in range(BATCH)
                    for each in twice[2 * n : 2 * n + 2]
                    + [jnp.zeros((LANES - 2 * size, WIDTH), jnp.float32)]
                ],
                axis=0,
            ).astype(jnp.bfloat16)
            other = mask_of(first, count, place_ref, valid_ref, columns, 1)
            factor = factor_of(normed, left_weight, mask) + factor_of(normed, right_weight, other)
            keep_rows(factor, both_s, 2 * WHOLE * SUB, BOTH)

    batches(work)
    if then:
        put_chunks(both_s, both_ref, BOTH, BOTH)
    else:
        pltpu.make_async_copy(new_s, out_ref, out_sem).wait()


def finish(which, place, valid, out_gain, gate, product, out_weight, *then):
    shape = (ROWS, COLUMNS, WIDTH)
    out = jax.ShapeDtypeStruct(shape, jnp.bfloat16)
    both = [pltpu.VMEM(((HIDDEN + 1) * BOTH, LANES), jnp.float32)]
    last = [pltpu.VMEM(shape, jnp.bfloat16), pltpu.SemaphoreType.DMA]
    return call(
        functools.partial(finish_kernel, which),
        [out, NORMED, BOTH_CHUNKS] if then else [out],
        [SMEM] * 3 + [VMEM] * (3 + len(then)),
        [SCRATCH] + (both if then else last),
        outs=None if then else [ANY],
    )(place, valid, out_gain, gate, product, out_weight, *then)


ALONE = (0, 3, 0)
LEFT = (0, 6, 0)
RIGHT = (3, 6, COLUMNS)


def gather_rows(chunks_ref, zh, block, layout):
    tile, last_tile, last_lane = layout
    start = last_tile * LANES + last_lane
    if block < 9:
        start = (tile + block % 3) * LANES + block // 3 * COLUMNS
    return jnp.concatenate(
        [
            chunks_ref[spot(span, zh)].astype(jnp.float32)[:, start : start + COLUMNS]
            for span in range(SPAN)
        ],
        axis=1,
    )


def assemble_into(chunks_ref, layout, put):
    for zh in range(ZH):
        for block in range(0, ROWS // SUB, 2):
            rows = [gather_rows(chunks_ref, zh, block + n, layout) for n in range(2)]
            put(zh * ROWS + block * SUB, jnp.concatenate(rows, axis=0))


def assemble_kernel(layout, chunks_ref, out_ref):
    def put(start, values):
        out_ref[pl.ds(start, 2 * SUB), :] = values.astype(jnp.bfloat16)

    assemble_into(chunks_ref, layout, put)


def assemble(chunks, layout):
    out = jax.ShapeDtypeStruct((ZH * ROWS, SPAN * COLUMNS), jnp.bfloat16)
    return call(functools.partial(assemble_kernel, layout), out, [VMEM])(chunks)


def assemble_turned_kernel(layout, chunks_ref, out_ref, whole):
    def put(start, values):
        whole[pl.ds(start, 2 * SUB), :] = values

    assemble_into(chunks_ref, layout, put)
    whole[pl.ds(ZH * ROWS, 64), :] = jnp.zeros((64, SPAN * COLUMNS), jnp.float32)
    for part in range(SPAN * COLUMNS // 128):
        turned = whole[:, part * 128 : (part + 1) * 128].T
        out_ref[pl.ds(part * 128, 128), :] = turned[:, : ZH * ROWS].astype(jnp.bfloat16)


def assemble_turned(chunks, layout):
    out = jax.ShapeDtypeStruct((SPAN * COLUMNS, ZH * ROWS), jnp.bfloat16)
    scratch = [pltpu.VMEM((ZH * ROWS + 64, SPAN * COLUMNS), jnp.float32)]
    kernel = functools.partial(assemble_turned_kernel, layout)
    return call(kernel, out, [VMEM], scratch)(chunks)


def chunk_of(total, zh, start):
    pieces = [
        total[pl.ds(zh * ROWS + block * SUB, SUB), :][:, start : start + COLUMNS]
        for block in range(ROWS // SUB)
    ]
    lanes = []
    for tile in range(WHOLE):
        lanes += pieces[tile:9:3] + [jnp.zeros((SUB, LANES - 3 * COLUMNS), jnp.float32)]
    lanes += [pieces[9], jnp.zeros((SUB, LANES - COLUMNS), jnp.float32)]
    return jnp.concatenate(lanes, axis=1).astype(jnp.bfloat16)


def outgoing_kernel(core_ref, left_ref, right_ref, out_ref, left_s, total):
    assemble_kernel(ALONE, left_ref, left_s)
    for x in range(X):
        total[:, x * ZH * ROWS : (x + 1) * ZH * ROWS] = lax.dot_general(
            left_s[...],
            right_ref[pl.ds(x * ZH * ROWS, ZH * ROWS), :],
            (((1,), (1,)), ((), ())),
            preferred_element_type=jnp.float32,
        )
    for half in range(2):
        slot = lax.rem(core_ref[0] + half, 2)
        for span in range(SPAN):
            for zh in range(ZH):
                out_ref[slot, spot(span, zh)] = chunk_of(total, zh, (2 * span + half) * COLUMNS)


def outgoing(core, left, right):
    out = jax.ShapeDtypeStruct((2,) + CHUNKS.shape, jnp.bfloat16)
    scratch = [
        pltpu.VMEM((ZH * ROWS, SPAN * COLUMNS), jnp.bfloat16),
        pltpu.VMEM((ZH * ROWS, X * ZH * ROWS), jnp.float32),
    ]
    return call(outgoing_kernel, out, [SMEM, VMEM, VMEM], scratch, 6 * 10**8)(core, left, right)


def incoming_kernel(core_ref, own_ref, other_ref, right_ref, out_ref, total):
    for n, left_ref in enumerate((own_ref, other_ref)):
        side = lax.rem(core_ref[0] + n, 2)
        product = jnp.zeros((ZH * COLUMNS, SPAN * COLUMNS), jnp.float32)
        for x in range(X):
            product = product + jnp.dot(
                left_ref[x],
                right_ref[pl.ds(x * ZH * ROWS, ZH * ROWS), :],
                preferred_element_type=jnp.float32,
            )
        for zh in range(ZH):
            start = pl.multiple_of(zh * ROWS + side * COLUMNS, 8)
            total[pl.ds(start, COLUMNS), :] = product[zh * COLUMNS : (zh + 1) * COLUMNS]
    for span in range(SPAN):
        for zh in range(ZH):
            out_ref[spot(span, zh)] = chunk_of(total, zh, span * COLUMNS)


def incoming(core, own, other, right):
    scratch = [pltpu.VMEM((ZH * ROWS, SPAN * COLUMNS), jnp.float32)]
    return call(incoming_kernel, CHUNKS, [SMEM, VMEM, VMEM, VMEM], scratch, 6 * 10**8)(
        core, own, other, right
    )


def exchange(values, axes):
    return lax.all_to_all(values, axes, split_axis=0, concat_axis=0, tiled=True)


def swap_cores(values):
    return lax.ppermute(values, "core", [(0, 1), (1, 0)])


def body(
    pair_acts,
    residue_valid,
    chain_index,
    norm_gain,
    norm_bias,
    projection,
    gate_weight,
    chain_bias,
    out_gain,
    out_weight,
):
    row_start = (lax.axis_index("x") * ZH + lax.axis_index("zh")) * ROWS
    core_index = lax.axis_index("core")
    column_block = (lax.axis_index("zl") * 8 + lax.axis_index("y")) * 2 + core_index
    place = jnp.stack([row_start, column_block * COLUMNS]).astype(jnp.int32)
    core = core_index.reshape(1).astype(jnp.int32)

    normed, right = project_right(
        place, residue_valid, pair_acts, norm_gain, norm_bias, projection
    )
    right = assemble(exchange(right, PLANE), ALONE)
    right = lax.all_gather(right, "x", axis=0, tiled=True)
    left, gate = left_and_gates(
        place,
        residue_valid,
        chain_index,
        normed,
        projection,
        gate_weight,
        chain_bias,
        pair_acts,
    )
    halves = outgoing(core, exchange(left, PLANE), right)
    total = halves[0].astype(jnp.float32) + swap_cores(halves[1]).astype(jnp.float32)
    product = exchange(total.astype(jnp.bfloat16), PLANE)
    middle, normed, both = finish(
        0,
        place,
        residue_valid,
        out_gain,
        gate,
        product,
        out_weight,
        norm_gain,
        norm_bias,
        projection,
    )
    both = exchange(both, PLANE)
    right = assemble(both, RIGHT)
    right = lax.all_gather(right, "x", axis=0, tiled=True)
    left = assemble_turned(both, LEFT).reshape(X, ZH * COLUMNS, ZH * ROWS)
    left = exchange(left, "x")
    product = exchange(incoming(core, left, swap_cores(left), right), PLANE)
    gate = gates(1, place, chain_index, normed, gate_weight, chain_bias, middle)
    return finish(1, place, residue_valid, out_gain, gate, product, out_weight)[0]


def solution(mesh):
    fine = Mesh(mesh.devices.reshape(SIZES), AXES)
    pairs = P(("x", "zh"), ("zl", "y", "core"), None)
    placed = (pairs, P(), P(), P(), P(), P(), P(), P(), P(), P())
    return jax.shard_map(body, mesh=fine, in_specs=placed, out_specs=pairs, check_vma=False)
```

```python
import functools

import jax
import jax.numpy as jnp
from jax import lax
from jax.experimental import pallas as pl
from jax.experimental.pallas import tpu as pltpu
from jax.sharding import Mesh
from jax.sharding import PartitionSpec as P

AXES = ("zl", "y", "core", "x", "zh")
SIZES = (2, 8, 2, 4, 4)
PLANE = ("y", "zh", "zl")
ROWS = 80
COLUMNS = 40
WIDTH = 128
HIDDEN = 64
X = 4
ZH = 4
SPAN = 16
EPS = 1e-05
DEPTH = 32
LANES = 128
SUB = 8
WHOLE = 3
TAIL = 8 * 9
STRIDE = 40
BOTH = 56
BATCH = 8
CHUNKS = jax.ShapeDtypeStruct((HIDDEN, SUB, DEPTH // SUB * LANES), jnp.bfloat16)
BOTH_CHUNKS = jax.ShapeDtypeStruct((HIDDEN, SUB, BOTH // SUB * LANES), jnp.bfloat16)
NORMED = jax.ShapeDtypeStruct((DEPTH, LANES, WIDTH), jnp.bfloat16)
GATES = jax.ShapeDtypeStruct((2, DEPTH, LANES, WIDTH), jnp.float32)
VMEM = pl.BlockSpec(memory_space=pltpu.VMEM)
ANY = pl.BlockSpec(memory_space=pl.ANY)
SMEM = pl.BlockSpec(memory_space=pltpu.SMEM)


def spot(span, zh):
    zl, y = divmod(span, 8)
    return (y * ZH + zh) * 2 + zl


def call(kernel, out_shape, in_specs, scratch_shapes=(), flops=10**8, outs=None):
    outs = outs or jax.tree.map(lambda _: VMEM, out_shape)
    moved = 4 * 10**6
    return pl.pallas_call(
        kernel,
        out_shape=out_shape,
        in_specs=in_specs,
        out_specs=outs,
        scratch_shapes=scratch_shapes,
        compiler_params=pltpu.CompilerParams(vmem_limit_bytes=40 * 2**20),
        cost_estimate=pl.CostEstimate(flops=flops, bytes_accessed=moved, transcendentals=0),
    )


def normalize(values, gain, bias):
    average = jnp.mean(values, axis=-1, keepdims=True)
    centred = values - average
    spread = jnp.mean(centred * centred, axis=-1, keepdims=True)
    return centred * lax.rsqrt(spread + EPS) * gain + bias


def batches(work):
    pl.loop(0, WHOLE)(lambda step: work(step * BATCH, 3))
    work(WHOLE * BATCH, 1)


def block_rows(first, count):
    if count == 1:
        return [[TAIL + n] for n in range(BATCH)]
    return [[first + n + WHOLE * SUB * group for group in range(count)] for n in range(BATCH)]


def load_pairs(pair_ref, first, count):
    rows = [row for rows in block_rows(first, count) for row in rows]
    return jnp.concatenate([pair_ref[row].astype(jnp.float32) for row in rows], axis=0)


def pad_rows(values, count):
    size = count * COLUMNS
    empty = jnp.zeros((LANES - size, WIDTH), jnp.float32)
    return [
        jnp.concatenate([values[n * size : (n + 1) * size], empty], axis=0).astype(jnp.bfloat16)
        for n in range(BATCH)
    ]


def spread_columns(place_ref, valid_ref):
    lane = lax.broadcasted_iota(jnp.int32, (1, LANES), 1)
    inside = lane % COLUMNS
    found = jnp.zeros((1, LANES), jnp.float32)
    for column in range(COLUMNS):
        value = valid_ref[place_ref[1] + column].astype(jnp.float32)
        found = jnp.where(inside == column, value, found)
    return jnp.where(lane < 3 * COLUMNS, found, 0.0)


def mask_of(first, count, place_ref, valid_ref, columns, shift=0):
    lane = lax.broadcasted_iota(jnp.int32, (1, LANES), 1)
    masks = []
    for rows in block_rows(first, count):
        mask = jnp.zeros((1, LANES), jnp.float32)
        for group, row in enumerate(rows):
            value = valid_ref[place_ref[0] + row].astype(jnp.float32)
            start = (group + shift) * COLUMNS
            inside = (lane >= start) & (lane < start + COLUMNS)
            mask = jnp.where(inside, value, mask)
        masks.append(mask * columns)
    return jnp.concatenate(masks, axis=1)


def weight_of(weight_ref, which, start):
    columns = weight_ref[which][:, start : start + 2 * HIDDEN]
    return columns.astype(jnp.float32).T.astype(jnp.bfloat16)


def factor_of(normed, weight, mask):
    proj = lax.dot_general(
        weight, normed, (((1,), (1,)), ((), ())), preferred_element_type=jnp.float32
    )
    return jax.nn.sigmoid(proj[HIDDEN:]) * proj[:HIDDEN] * mask


def keep_rows(factor, scratch, first, stride):
    for n in range(BATCH):
        place = pl.ds(first + n, HIDDEN, stride=stride)
        scratch[place, :] = factor[:, n * LANES : (n + 1) * LANES]


def put_chunks(scratch, out_ref, stride, depth):
    for channel in range(HIDDEN):
        rows = scratch[pl.ds(channel * stride, depth), :]
        tiles = [rows[n : n + SUB] for n in range(0, depth, SUB)]
        out_ref[channel] = jnp.concatenate(tiles, axis=1).astype(jnp.bfloat16)


SCRATCH = pltpu.VMEM(((HIDDEN + 1) * STRIDE, LANES), jnp.float32)


def right_kernel(
    place_ref, valid_ref, pair_ref, vectors_ref, weight_ref, normed_ref, right_ref, right_s
):
    columns = spread_columns(place_ref, valid_ref)
    weight = weight_of(weight_ref, 0, 2 * HIDDEN)

    def work(first, count):
        values = load_pairs(pair_ref, first, count)
        pieces = pad_rows(normalize(values, vectors_ref[0:1], vectors_ref[2:3]), count)
        for n in range(BATCH):
            normed_ref[first + n] = pieces[n]
        mask = mask_of(first, count, place_ref, valid_ref, columns)
        factor = factor_of(jnp.concatenate(pieces, axis=0), weight, mask)
        keep_rows(factor, right_s, first, STRIDE)

    batches(work)
    put_chunks(right_s, right_ref, STRIDE, DEPTH)


def project_right(place, valid, pair, vectors, weight):
    return call(right_kernel, [NORMED, CHUNKS], [SMEM, SMEM, VMEM, VMEM, VMEM], [SCRATCH])(
        place, valid, pair, vectors, weight
    )


def load_normed(normed_ref, first):
    return normed_ref[pl.ds(first, BATCH)].reshape(BATCH * LANES, WIDTH)


def gate_work(
    which, place_ref, chain_ref, normed_ref, gate_ref, vectors_ref, pair_ref, out_ref
):
    row = lax.broadcasted_iota(jnp.int32, (COLUMNS, WIDTH), 0)
    chain_columns = jnp.full((COLUMNS, WIDTH), -1, jnp.int32)
    for column in range(COLUMNS):
        chain_columns = jnp.where(row == column, chain_ref[place_ref[1] + column], chain_columns)
    offset = vectors_ref[4 + which : 5 + which]

    def work(first, count):
        logit = jnp.dot(
            load_normed(normed_ref, first), gate_ref[which], preferred_element_type=jnp.float32
        )
        for n, rows in enumerate(block_rows(first, count)):
            for group, row in enumerate(rows):
                same = chain_columns == chain_ref[place_ref[0] + row]
                start = n * LANES + group * COLUMNS
                place = pl.ds(group * COLUMNS, COLUMNS)
                out_ref[0, first + n, place] = jax.nn.sigmoid(
                    logit[start : start + COLUMNS] + jnp.where(same, offset, 0.0)
                )
                out_ref[1, first + n, place] = pair_ref[row].astype(jnp.float32)

    return work


def gate_kernel(which, *refs):
    batches(gate_work(which, *refs))


def gates(which, place, chain, normed, gate, vectors, pair):
    kernel = functools.partial(gate_kernel, which)
    return call(kernel, GATES, [SMEM, SMEM, VMEM, VMEM, VMEM, VMEM])(
        place, chain, normed, gate, vectors, pair
    )


def left_and_gate_kernel(
    place_ref,
    valid_ref,
    chain_ref,
    normed_ref,
    weight_ref,
    gate_ref,
    vectors_ref,
    pair_ref,
    left_ref,
    out_ref,
    left_s,
):
    columns = spread_columns(place_ref, valid_ref)
    weight = weight_of(weight_ref, 0, 0)
    gate = gate_work(
        0, place_ref, chain_ref, normed_ref, gate_ref, vectors_ref, pair_ref, out_ref
    )

    def work(first, count):
        mask = mask_of(first, count, place_ref, valid_ref, columns)
        keep_rows(factor_of(load_normed(normed_ref, first), weight, mask), left_s, first, STRIDE)
        gate(first, count)

    batches(work)
    put_chunks(left_s, left_ref, STRIDE, DEPTH)


def left_and_gates(place, valid, chain, normed, weight, gate, vectors, pair):
    return call(left_and_gate_kernel, [CHUNKS, GATES], [SMEM] * 3 + [VMEM] * 5, [SCRATCH])(
        place, valid, chain, normed, weight, gate, vectors, pair
    )


def finish_kernel(which, place_ref, valid_ref, out_gain_ref, gates_ref, product_ref, out_weight_ref, *rest):
    then = which == 0
    if then:
        vectors_ref, weight_ref, out_ref, normed_ref, both_ref, hidden_s, both_s = rest
        new_s = out_ref
        columns = spread_columns(place_ref, valid_ref)
        left_weight = weight_of(weight_ref, 1, 0)
        right_weight = weight_of(weight_ref, 1, 2 * HIDDEN)
    else:
        out_ref, hidden_s, new_s, out_sem = rest

    def channel(n):
        return product_ref[n].astype(jnp.float32)

    average = channel(0)
    for n in range(1, HIDDEN):
        average = average + channel(n)
    average = average / HIDDEN
    spread = jnp.zeros_like(average)
    for n in range(HIDDEN):
        centred = channel(n) - average
        spread = spread + centred * centred
    scale = lax.rsqrt(spread / HIDDEN + EPS)
    for n in range(HIDDEN):
        hidden = (channel(n) - average) * scale * out_gain_ref[which, n]
        for part in range(DEPTH // SUB):
            place = pl.ds(n * STRIDE + part * SUB, SUB)
            hidden_s[place, :] = hidden[:, part * LANES : (part + 1) * LANES]

    def work(first, count):
        size = count * COLUMNS
        hidden = jnp.concatenate(
            [hidden_s[pl.ds(first + n, HIDDEN, stride=STRIDE), :] for n in range(BATCH)], axis=1
        ).astype(jnp.bfloat16)
        branch = lax.dot_general(
            hidden,
            out_weight_ref[which],
            (((0,), (0,)), ((), ())),
            preferred_element_type=jnp.float32,
        )
        new = jnp.concatenate(
            [
                gates_ref[1, first + n, pl.ds(0, size)]
                + gates_ref[0, first + n, pl.ds(0, size)] * branch[n * LANES : n * LANES + size]
                for n in range(BATCH)
            ],
            axis=0,
        )
        places = [row for rows in block_rows(first, count) for row in rows]
        for n, row in enumerate(places):
            new_s[row] = new[n * COLUMNS : (n + 1) * COLUMNS].astype(jnp.bfloat16)
        if not then:
            for group in range(count):
                span = pl.ds(block_rows(first, count)[0][group], BATCH)
                pltpu.make_async_copy(new_s.at[span], out_ref.at[span], out_sem).start()
            return
        new = new.astype(jnp.bfloat16).astype(jnp.float32)
        values = normalize(new, vectors_ref[1:2], vectors_ref[3:4])
        pieces = pad_rows(values, count)
        for n in range(BATCH):
            normed_ref[first + n] = pieces[n]
        mask = mask_of(first, count, place_ref, valid_ref, columns)
        if count == 3:
            normed = jnp.concatenate(pieces, axis=0)
            keep_rows(factor_of(normed, left_weight, mask), both_s, first, BOTH)
            right_first = first + WHOLE * SUB
            keep_rows(factor_of(normed, right_weight, mask), both_s, right_first, BOTH)
        else:
            twice = [values[n * size : (n + 1) * size] for n in range(BATCH) for _ in range(2)]
            normed = jnp.concatenate(
                [
                    each
                    for n in range(BATCH)
                    for each in twice[2 * n : 2 * n + 2]
                    + [jnp.zeros((LANES - 2 * size, WIDTH), jnp.float32)]
                ],
                axis=0,
            ).astype(jnp.bfloat16)
            other = mask_of(first, count, place_ref, valid_ref, columns, 1)
            factor = factor_of(normed, left_weight, mask) + factor_of(normed, right_weight, other)
            keep_rows(factor, both_s, 2 * WHOLE * SUB, BOTH)

    batches(work)
    if then:
        put_chunks(both_s, both_ref, BOTH, BOTH)
    else:
        pltpu.make_async_copy(new_s, out_ref, out_sem).wait()


def finish(which, place, valid, out_gain, gate, product, out_weight, *then):
    shape = (ROWS, COLUMNS, WIDTH)
    out = jax.ShapeDtypeStruct(shape, jnp.bfloat16)
    both = [pltpu.VMEM(((HIDDEN + 1) * BOTH, LANES), jnp.float32)]
    last = [pltpu.VMEM(shape, jnp.bfloat16), pltpu.SemaphoreType.DMA]
    return call(
        functools.partial(finish_kernel, which),
        [out, NORMED, BOTH_CHUNKS] if then else [out],
        [SMEM] * 3 + [VMEM] * (3 + len(then)),
        [SCRATCH] + (both if then else last),
        outs=None if then else [ANY],
    )(place, valid, out_gain, gate, product, out_weight, *then)


ALONE = (0, 3, 0)
LEFT = (0, 6, 0)
RIGHT = (3, 6, COLUMNS)


def gather_rows(chunks_ref, zh, block, layout):
    tile, last_tile, last_lane = layout
    start = last_tile * LANES + last_lane
    if block < 9:
        start = (tile + block % 3) * LANES + block // 3 * COLUMNS
    return jnp.concatenate(
        [
            chunks_ref[spot(span, zh)].astype(jnp.float32)[:, start : start + COLUMNS]
            for span in range(SPAN)
        ],
        axis=1,
    )


def assemble_into(chunks_ref, layout, put):
    for zh in range(ZH):
        for block in range(0, ROWS // SUB, 2):
            rows = [gather_rows(chunks_ref, zh, block + n, layout) for n in range(2)]
            put(zh * ROWS + block * SUB, jnp.concatenate(rows, axis=0))


def assemble_kernel(layout, chunks_ref, out_ref):
    def put(start, values):
        out_ref[pl.ds(start, 2 * SUB), :] = values.astype(jnp.bfloat16)

    assemble_into(chunks_ref, layout, put)


def assemble(chunks, layout):
    out = jax.ShapeDtypeStruct((ZH * ROWS, SPAN * COLUMNS), jnp.bfloat16)
    return call(functools.partial(assemble_kernel, layout), out, [VMEM])(chunks)


def assemble_turned_kernel(layout, chunks_ref, out_ref, whole):
    def put(start, values):
        whole[pl.ds(start, 2 * SUB), :] = values

    assemble_into(chunks_ref, layout, put)
    whole[pl.ds(ZH * ROWS, 64), :] = jnp.zeros((64, SPAN * COLUMNS), jnp.float32)
    for part in range(SPAN * COLUMNS // 128):
        turned = whole[:, part * 128 : (part + 1) * 128].T
        out_ref[pl.ds(part * 128, 128), :] = turned[:, : ZH * ROWS].astype(jnp.bfloat16)


def assemble_turned(chunks, layout):
    out = jax.ShapeDtypeStruct((SPAN * COLUMNS, ZH * ROWS), jnp.bfloat16)
    scratch = [pltpu.VMEM((ZH * ROWS + 64, SPAN * COLUMNS), jnp.float32)]
    kernel = functools.partial(assemble_turned_kernel, layout)
    return call(kernel, out, [VMEM], scratch)(chunks)


def chunk_of(total, zh, start):
    pieces = [
        total[pl.ds(zh * ROWS + block * SUB, SUB), :][:, start : start + COLUMNS]
        for block in range(ROWS // SUB)
    ]
    lanes = []
    for tile in range(WHOLE):
        lanes += pieces[tile:9:3] + [jnp.zeros((SUB, LANES - 3 * COLUMNS), jnp.float32)]
    lanes += [pieces[9], jnp.zeros((SUB, LANES - COLUMNS), jnp.float32)]
    return jnp.concatenate(lanes, axis=1).astype(jnp.bfloat16)


def outgoing_kernel(core_ref, left_ref, *rest):
    rights, (out_ref, left_s, total) = rest[:X], rest[X:]
    assemble_kernel(ALONE, left_ref, left_s)
    for n, right_ref in enumerate(rights):
        total[:, n * ZH * ROWS : (n + 1) * ZH * ROWS] = lax.dot_general(
            left_s[...],
            right_ref[...],
            (((1,), (1,)), ((), ())),
            preferred_element_type=jnp.float32,
        )
    for half in range(2):
        slot = lax.rem(core_ref[0] + half, 2)
        for n in range(X):
            x = lax.rem(core_ref[1] + n, X)
            for low in range(ZH):
                span = ((lax.rem(x, 2) * ZH + low) * ZH) * 2 + x // 2
                for zh in range(ZH):
                    start = ((n * ZH + low) * 2 + half) * COLUMNS
                    out_ref[slot, span + zh * 2] = chunk_of(total, zh, start)


def outgoing(core, left, rights):
    out = jax.ShapeDtypeStruct((2,) + CHUNKS.shape, jnp.bfloat16)
    scratch = [
        pltpu.VMEM((ZH * ROWS, SPAN * COLUMNS), jnp.bfloat16),
        pltpu.VMEM((ZH * ROWS, X * ZH * ROWS), jnp.float32),
    ]
    return call(outgoing_kernel, out, [SMEM] + [VMEM] * (1 + X), scratch, 6 * 10**8)(
        core, left, *rights
    )


def incoming_kernel(core_ref, own_ref, other_ref, *rest):
    rights, (_, out_ref, total) = rest[:X], rest[X:]
    for n, left_ref in enumerate((own_ref, other_ref)):
        side = lax.rem(core_ref[0] + n, 2)
        product = jnp.zeros((ZH * COLUMNS, SPAN * COLUMNS), jnp.float32)
        for m, right_ref in enumerate(rights):
            product = product + jnp.dot(
                left_ref[lax.rem(core_ref[1] + m, X)],
                right_ref[...],
                preferred_element_type=jnp.float32,
            )
        for zh in range(ZH):
            start = pl.multiple_of(zh * ROWS + side * COLUMNS, 8)
            total[pl.ds(start, COLUMNS), :] = product[zh * COLUMNS : (zh + 1) * COLUMNS]
    for span in range(SPAN):
        for zh in range(ZH):
            out_ref[spot(span, zh)] = chunk_of(total, zh, span * COLUMNS)


def incoming(core, own, other, rights, gate):
    scratch = [pltpu.VMEM((ZH * ROWS, SPAN * COLUMNS), jnp.float32)]
    return call(
        incoming_kernel, CHUNKS, [SMEM] + [VMEM] * (2 + X) + [ANY], scratch, 6 * 10**8
    )(core, own, other, *rights, gate)


def gather_x(block):
    def shift(by):
        return lax.ppermute(block, "x", [(x, (x + by) % X) for x in range(X)])

    return [block] + [shift(-n) for n in range(1, X)]


def exchange(values, axes):
    return lax.all_to_all(values, axes, split_axis=0, concat_axis=0, tiled=True)


def swap_cores(values):
    return lax.ppermute(values, "core", [(0, 1), (1, 0)])


def body(
    pair_acts,
    residue_valid,
    chain_index,
    norm_gain,
    norm_bias,
    projection,
    gate_weight,
    chain_bias,
    out_gain,
    out_weight,
):
    row_start = (lax.axis_index("x") * ZH + lax.axis_index("zh")) * ROWS
    core_index = lax.axis_index("core")
    column_block = (lax.axis_index("zl") * 8 + lax.axis_index("y")) * 2 + core_index
    place = jnp.stack([row_start, column_block * COLUMNS]).astype(jnp.int32)
    core = jnp.stack([core_index, lax.axis_index("x")]).astype(jnp.int32)

    vectors = jnp.concatenate([norm_gain, norm_bias, chain_bias], axis=0)
    normed, right = project_right(place, residue_valid, pair_acts, vectors, projection)
    rights = gather_x(assemble(exchange(right, PLANE), ALONE))
    left, gate = left_and_gates(
        place, residue_valid, chain_index, normed, projection, gate_weight, vectors, pair_acts
    )
    halves = outgoing(core, exchange(left, PLANE), rights)
    total = halves[0].astype(jnp.float32) + swap_cores(halves[1]).astype(jnp.float32)
    product = exchange(total.astype(jnp.bfloat16), PLANE)
    middle, normed, both = finish(
        0, place, residue_valid, out_gain, gate, product, out_weight, vectors, projection
    )
    both = exchange(both, PLANE)
    rights = gather_x(assemble(both, RIGHT))
    gate = gates(1, place, chain_index, normed, gate_weight, vectors, middle)
    left = assemble_turned(both, LEFT).reshape(X, ZH * COLUMNS, ZH * ROWS)
    left = exchange(left, "x")
    product = exchange(incoming(core, left, swap_cores(left), rights, gate), PLANE)
    return finish(1, place, residue_valid, out_gain, gate, product, out_weight)[0]


def solution(mesh):
    fine = Mesh(mesh.devices.reshape(SIZES), AXES)
    pairs = P(("x", "zh"), ("zl", "y", "core"), None)
    placed = (pairs, P(), P(), P(), P(), P(), P(), P(), P(), P())
    return jax.shard_map(body, mesh=fine, in_specs=placed, out_specs=pairs, check_vma=False)
```

```python
import functools

import jax
import jax.numpy as jnp
from jax import lax
from jax.experimental import pallas as pl
from jax.experimental.pallas import tpu as pltpu
from jax.sharding import Mesh
from jax.sharding import PartitionSpec as P

AXES = ("zl", "y", "core", "x", "zh")
SIZES = (2, 8, 2, 4, 4)
PLANE = ("y", "zh", "zl")
ROWS = 80
COLUMNS = 40
WIDTH = 128
HIDDEN = 64
X = 4
ZH = 4
SPAN = 16
EPS = 1e-05
DEPTH = 32
LANES = 128
SUB = 8
WHOLE = 3
TAIL = 8 * 9
STRIDE = 40
BOTH = 56
BATCH = 8
CHUNKS = jax.ShapeDtypeStruct((HIDDEN, SUB, DEPTH // SUB * LANES), jnp.bfloat16)
BOTH_CHUNKS = jax.ShapeDtypeStruct((HIDDEN, SUB, BOTH // SUB * LANES), jnp.bfloat16)
NORMED = jax.ShapeDtypeStruct((DEPTH, LANES, WIDTH), jnp.bfloat16)
GATES = jax.ShapeDtypeStruct((2, DEPTH, LANES, WIDTH), jnp.float32)
VMEM = pl.BlockSpec(memory_space=pltpu.VMEM)
ANY = pl.BlockSpec(memory_space=pl.ANY)
SMEM = pl.BlockSpec(memory_space=pltpu.SMEM)


def spot(span, zh):
    zl, y = divmod(span, 8)
    return (y * ZH + zh) * 2 + zl


def call(kernel, out_shape, in_specs, scratch_shapes=(), flops=10**8, outs=None, grant=40):
    outs = outs or jax.tree.map(lambda _: VMEM, out_shape)
    moved = 4 * 10**6
    return pl.pallas_call(
        kernel,
        out_shape=out_shape,
        in_specs=in_specs,
        out_specs=outs,
        scratch_shapes=scratch_shapes,
        compiler_params=pltpu.CompilerParams(vmem_limit_bytes=grant * 2**20),
        cost_estimate=pl.CostEstimate(flops=flops, bytes_accessed=moved, transcendentals=0),
    )


def normalize(values, gain, bias):
    average = jnp.mean(values, axis=-1, keepdims=True)
    centred = values - average
    spread = jnp.mean(centred * centred, axis=-1, keepdims=True)
    return centred * lax.rsqrt(spread + EPS) * gain + bias


def batches(work):
    pl.loop(0, WHOLE)(lambda step: work(step * BATCH, 3))
    work(WHOLE * BATCH, 1)


def block_rows(first, count):
    if count == 1:
        return [[TAIL + n] for n in range(BATCH)]
    return [[first + n + WHOLE * SUB * group for group in range(count)] for n in range(BATCH)]


def load_pairs(pair_ref, first, count):
    rows = [row for rows in block_rows(first, count) for row in rows]
    return jnp.concatenate([pair_ref[row].astype(jnp.float32) for row in rows], axis=0)


def pad_rows(values, count):
    size = count * COLUMNS
    empty = jnp.zeros((LANES - size, WIDTH), jnp.float32)
    return [
        jnp.concatenate([values[n * size : (n + 1) * size], empty], axis=0).astype(jnp.bfloat16)
        for n in range(BATCH)
    ]


def spread_columns(place_ref, valid_ref):
    lane = lax.broadcasted_iota(jnp.int32, (1, LANES), 1)
    inside = lane % COLUMNS
    found = jnp.zeros((1, LANES), jnp.float32)
    for column in range(COLUMNS):
        value = valid_ref[place_ref[1] + column].astype(jnp.float32)
        found = jnp.where(inside == column, value, found)
    return jnp.where(lane < 3 * COLUMNS, found, 0.0)


def mask_of(first, count, place_ref, valid_ref, columns, shift=0):
    lane = lax.broadcasted_iota(jnp.int32, (1, LANES), 1)
    masks = []
    for rows in block_rows(first, count):
        mask = jnp.zeros((1, LANES), jnp.float32)
        for group, row in enumerate(rows):
            value = valid_ref[place_ref[0] + row].astype(jnp.float32)
            start = (group + shift) * COLUMNS
            inside = (lane >= start) & (lane < start + COLUMNS)
            mask = jnp.where(inside, value, mask)
        masks.append(mask * columns)
    return jnp.concatenate(masks, axis=1)


def weight_of(weight_ref, which, start):
    columns = weight_ref[which][:, start : start + 2 * HIDDEN]
    return columns.astype(jnp.float32).T.astype(jnp.bfloat16)


def factor_of(normed, weight, mask):
    proj = lax.dot_general(
        weight, normed, (((1,), (1,)), ((), ())), preferred_element_type=jnp.float32
    )
    return jax.nn.sigmoid(proj[HIDDEN:]) * proj[:HIDDEN] * mask


def keep_rows(factor, scratch, first, stride):
    for n in range(BATCH):
        place = pl.ds(first + n, HIDDEN, stride=stride)
        scratch[place, :] = factor[:, n * LANES : (n + 1) * LANES]


def put_chunks(scratch, out_ref, stride, depth):
    for channel in range(HIDDEN):
        rows = scratch[pl.ds(channel * stride, depth), :]
        tiles = [rows[n : n + SUB] for n in range(0, depth, SUB)]
        out_ref[channel] = jnp.concatenate(tiles, axis=1).astype(jnp.bfloat16)


SCRATCH = pltpu.VMEM(((HIDDEN + 1) * STRIDE, LANES), jnp.float32)


def right_kernel(
    place_ref,
    valid_ref,
    pair_any,
    vectors_any,
    weight_any,
    normed_ref,
    right_ref,
    right_s,
    pair_ref,
    vectors_ref,
    weight_ref,
    sems,
):
    moves = ((pair_any, pair_ref), (vectors_any, vectors_ref), (weight_any, weight_ref))
    copies = [pltpu.make_async_copy(a, b, sems.at[n]) for n, (a, b) in enumerate(moves)]
    for copy in copies:
        copy.start()
    columns = spread_columns(place_ref, valid_ref)
    for copy in copies:
        copy.wait()
    weight = weight_of(weight_ref, 0, 2 * HIDDEN)

    def work(first, count):
        values = load_pairs(pair_ref, first, count)
        pieces = pad_rows(normalize(values, vectors_ref[0:1], vectors_ref[2:3]), count)
        for n in range(BATCH):
            normed_ref[first + n] = pieces[n]
        mask = mask_of(first, count, place_ref, valid_ref, columns)
        factor = factor_of(jnp.concatenate(pieces, axis=0), weight, mask)
        keep_rows(factor, right_s, first, STRIDE)

    batches(work)
    put_chunks(right_s, right_ref, STRIDE, DEPTH)


def project_right(place, valid, *operands):
    scratch = [pltpu.VMEM(each.shape, each.dtype) for each in operands]
    return call(
        right_kernel,
        [NORMED, CHUNKS],
        [SMEM, SMEM] + [ANY] * 3,
        [SCRATCH] + scratch + [pltpu.SemaphoreType.DMA((3,))],
        grant=60,
    )(place, valid, *operands)


def load_normed(normed_ref, first):
    return normed_ref[pl.ds(first, BATCH)].reshape(BATCH * LANES, WIDTH)


def gate_work(
    which, place_ref, chain_ref, normed_ref, gate_ref, vectors_ref, pair_ref, out_ref
):
    row = lax.broadcasted_iota(jnp.int32, (COLUMNS, WIDTH), 0)
    chain_columns = jnp.full((COLUMNS, WIDTH), -1, jnp.int32)
    for column in range(COLUMNS):
        chain_columns = jnp.where(row == column, chain_ref[place_ref[1] + column], chain_columns)
    offset = vectors_ref[4 + which : 5 + which]

    def work(first, count):
        logit = jnp.dot(
            load_normed(normed_ref, first), gate_ref[which], preferred_element_type=jnp.float32
        )
        for n, rows in enumerate(block_rows(first, count)):
            for group, row in enumerate(rows):
                same = chain_columns == chain_ref[place_ref[0] + row]
                start = n * LANES + group * COLUMNS
                place = pl.ds(group * COLUMNS, COLUMNS)
                out_ref[0, first + n, place] = jax.nn.sigmoid(
                    logit[start : start + COLUMNS] + jnp.where(same, offset, 0.0)
                )
                out_ref[1, first + n, place] = pair_ref[row].astype(jnp.float32)

    return work


def gate_kernel(which, *refs):
    batches(gate_work(which, *refs))


def gates(which, place, chain, normed, gate, vectors, pair):
    kernel = functools.partial(gate_kernel, which)
    return call(kernel, GATES, [SMEM, SMEM, VMEM, VMEM, VMEM, VMEM])(
        place, chain, normed, gate, vectors, pair
    )


def left_and_gate_kernel(
    place_ref,
    valid_ref,
    chain_ref,
    normed_ref,
    weight_ref,
    gate_ref,
    vectors_ref,
    pair_ref,
    left_ref,
    out_ref,
    left_s,
):
    columns = spread_columns(place_ref, valid_ref)
    weight = weight_of(weight_ref, 0, 0)
    gate = gate_work(
        0, place_ref, chain_ref, normed_ref, gate_ref, vectors_ref, pair_ref, out_ref
    )

    def work(first, count):
        mask = mask_of(first, count, place_ref, valid_ref, columns)
        keep_rows(factor_of(load_normed(normed_ref, first), weight, mask), left_s, first, STRIDE)
        gate(first, count)

    batches(work)
    put_chunks(left_s, left_ref, STRIDE, DEPTH)


def left_and_gates(place, valid, chain, normed, weight, gate, vectors, pair):
    return call(left_and_gate_kernel, [CHUNKS, GATES], [SMEM] * 3 + [VMEM] * 5, [SCRATCH])(
        place, valid, chain, normed, weight, gate, vectors, pair
    )


def finish_kernel(which, place_ref, valid_ref, out_gain_ref, gates_ref, product_ref, out_weight_ref, *rest):
    then = which == 0
    if then:
        vectors_ref, weight_ref, out_ref, normed_ref, both_ref, hidden_s, both_s = rest
        new_s = out_ref
        columns = spread_columns(place_ref, valid_ref)
        left_weight = weight_of(weight_ref, 1, 0)
        right_weight = weight_of(weight_ref, 1, 2 * HIDDEN)
    else:
        out_ref, hidden_s, new_s, out_sem = rest

    def channel(n):
        return product_ref[n].astype(jnp.float32)

    average = channel(0)
    for n in range(1, HIDDEN):
        average = average + channel(n)
    average = average / HIDDEN
    spread = jnp.zeros_like(average)
    for n in range(HIDDEN):
        centred = channel(n) - average
        spread = spread + centred * centred
    scale = lax.rsqrt(spread / HIDDEN + EPS)
    for n in range(HIDDEN):
        hidden = (channel(n) - average) * scale * out_gain_ref[which, n]
        for part in range(DEPTH // SUB):
            place = pl.ds(n * STRIDE + part * SUB, SUB)
            hidden_s[place, :] = hidden[:, part * LANES : (part + 1) * LANES]

    def work(first, count):
        size = count * COLUMNS
        hidden = jnp.concatenate(
            [hidden_s[pl.ds(first + n, HIDDEN, stride=STRIDE), :] for n in range(BATCH)], axis=1
        ).astype(jnp.bfloat16)
        branch = lax.dot_general(
            hidden,
            out_weight_ref[which],
            (((0,), (0,)), ((), ())),
            preferred_element_type=jnp.float32,
        )
        new = jnp.concatenate(
            [
                gates_ref[1, first + n, pl.ds(0, size)]
                + gates_ref[0, first + n, pl.ds(0, size)] * branch[n * LANES : n * LANES + size]
                for n in range(BATCH)
            ],
            axis=0,
        )
        places = [row for rows in block_rows(first, count) for row in rows]
        for n, row in enumerate(places):
            new_s[row] = new[n * COLUMNS : (n + 1) * COLUMNS].astype(jnp.bfloat16)
        if not then:
            for group in range(count):
                span = pl.ds(block_rows(first, count)[0][group], BATCH)
                pltpu.make_async_copy(new_s.at[span], out_ref.at[span], out_sem).start()
            return
        new = new.astype(jnp.bfloat16).astype(jnp.float32)
        values = normalize(new, vectors_ref[1:2], vectors_ref[3:4])
        pieces = pad_rows(values, count)
        for n in range(BATCH):
            normed_ref[first + n] = pieces[n]
        mask = mask_of(first, count, place_ref, valid_ref, columns)
        if count == 3:
            normed = jnp.concatenate(pieces, axis=0)
            keep_rows(factor_of(normed, left_weight, mask), both_s, first, BOTH)
            right_first = first + WHOLE * SUB
            keep_rows(factor_of(normed, right_weight, mask), both_s, right_first, BOTH)
        else:
            twice = [values[n * size : (n + 1) * size] for n in range(BATCH) for _ in range(2)]
            normed = jnp.concatenate(
                [
                    each
                    for n in range(BATCH)
                    for each in twice[2 * n : 2 * n + 2]
                    + [jnp.zeros((LANES - 2 * size, WIDTH), jnp.float32)]
                ],
                axis=0,
            ).astype(jnp.bfloat16)
            other = mask_of(first, count, place_ref, valid_ref, columns, 1)
            factor = factor_of(normed, left_weight, mask) + factor_of(normed, right_weight, other)
            keep_rows(factor, both_s, 2 * WHOLE * SUB, BOTH)

    batches(work)
    if then:
        put_chunks(both_s, both_ref, BOTH, BOTH)
    else:
        pltpu.make_async_copy(new_s, out_ref, out_sem).wait()


def finish(which, place, valid, out_gain, gate, product, out_weight, *then):
    shape = (ROWS, COLUMNS, WIDTH)
    out = jax.ShapeDtypeStruct(shape, jnp.bfloat16)
    both = [pltpu.VMEM(((HIDDEN + 1) * BOTH, LANES), jnp.float32)]
    last = [pltpu.VMEM(shape, jnp.bfloat16), pltpu.SemaphoreType.DMA]
    return call(
        functools.partial(finish_kernel, which),
        [out, NORMED, BOTH_CHUNKS] if then else [out],
        [SMEM] * 3 + [VMEM] * (3 + len(then)),
        [SCRATCH] + (both if then else last),
        outs=None if then else [ANY],
    )(place, valid, out_gain, gate, product, out_weight, *then)


ALONE = (0, 3, 0)
LEFT = (0, 6, 0)
RIGHT = (3, 6, COLUMNS)


def gather_rows(chunks_ref, zh, block, layout):
    tile, last_tile, last_lane = layout
    start = last_tile * LANES + last_lane
    if block < 9:
        start = (tile + block % 3) * LANES + block // 3 * COLUMNS
    return jnp.concatenate(
        [
            chunks_ref[spot(span, zh)].astype(jnp.float32)[:, start : start + COLUMNS]
            for span in range(SPAN)
        ],
        axis=1,
    )


def assemble_into(chunks_ref, layout, put):
    for zh in range(ZH):
        for block in range(0, ROWS // SUB, 2):
            rows = [gather_rows(chunks_ref, zh, block + n, layout) for n in range(2)]
            put(zh * ROWS + block * SUB, jnp.concatenate(rows, axis=0))


def assemble_kernel(layout, chunks_ref, out_ref):
    def put(start, values):
        out_ref[pl.ds(start, 2 * SUB), :] = values.astype(jnp.bfloat16)

    assemble_into(chunks_ref, layout, put)


def assemble(chunks, layout):
    out = jax.ShapeDtypeStruct((ZH * ROWS, SPAN * COLUMNS), jnp.bfloat16)
    return call(functools.partial(assemble_kernel, layout), out, [VMEM])(chunks)


def assemble_turned_kernel(layout, chunks_ref, _, out_ref, whole):
    def put(start, values):
        whole[pl.ds(start, 2 * SUB), :] = values

    assemble_into(chunks_ref, layout, put)
    whole[pl.ds(ZH * ROWS, 64), :] = jnp.zeros((64, SPAN * COLUMNS), jnp.float32)
    for part in range(SPAN * COLUMNS // 128):
        turned = whole[:, part * 128 : (part + 1) * 128].T
        out_ref[pl.ds(part * 128, 128), :] = turned[:, : ZH * ROWS].astype(jnp.bfloat16)


def assemble_turned(chunks, layout, after):
    out = jax.ShapeDtypeStruct((SPAN * COLUMNS, ZH * ROWS), jnp.bfloat16)
    scratch = [pltpu.VMEM((ZH * ROWS + 64, SPAN * COLUMNS), jnp.float32)]
    kernel = functools.partial(assemble_turned_kernel, layout)
    return call(kernel, out, [VMEM, ANY], scratch)(chunks, after)


def chunk_of(total, zh, start):
    pieces = [
        total[pl.ds(zh * ROWS + block * SUB, SUB), :][:, start : start + COLUMNS]
        for block in range(ROWS // SUB)
    ]
    lanes = []
    for tile in range(WHOLE):
        lanes += pieces[tile:9:3] + [jnp.zeros((SUB, LANES - 3 * COLUMNS), jnp.float32)]
    lanes += [pieces[9], jnp.zeros((SUB, LANES - COLUMNS), jnp.float32)]
    return jnp.concatenate(lanes, axis=1).astype(jnp.bfloat16)


def blocks_of(refs):
    whole = [ref[...] for ref in refs]
    return [whole[0], whole[1], jnp.concatenate(whole[2:4], axis=0), whole[4]]


def outgoing_kernel(core_ref, left_ref, *rest):
    rights, (out_ref, left_s, total) = rest[: X + 1], rest[X + 1 :]
    assemble_kernel(ALONE, left_ref, left_s)
    for n, right in enumerate(blocks_of(rights)):
        total[:, n * ZH * ROWS : (n + 1) * ZH * ROWS] = lax.dot_general(
            left_s[...],
            right,
            (((1,), (1,)), ((), ())),
            preferred_element_type=jnp.float32,
        )
    for half in range(2):
        slot = lax.rem(core_ref[0] + half, 2)
        for n in range(X):
            x = lax.rem(core_ref[1] + n, X)
            for low in range(ZH):
                span = ((lax.rem(x, 2) * ZH + low) * ZH) * 2 + x // 2
                for zh in range(ZH):
                    start = ((n * ZH + low) * 2 + half) * COLUMNS
                    out_ref[slot, span + zh * 2] = chunk_of(total, zh, start)


def outgoing(core, left, rights):
    out = jax.ShapeDtypeStruct((2,) + CHUNKS.shape, jnp.bfloat16)
    scratch = [
        pltpu.VMEM((ZH * ROWS, SPAN * COLUMNS), jnp.bfloat16),
        pltpu.VMEM((ZH * ROWS, X * ZH * ROWS), jnp.float32),
    ]
    return call(outgoing_kernel, out, [SMEM] + [VMEM] * (2 + X), scratch, 6 * 10**8)(
        core, left, *rights
    )


def incoming_kernel(core_ref, own_ref, other_ref, *rest):
    rights, (_, out_ref, total) = rest[: X + 1], rest[X + 1 :]
    for n, left_ref in enumerate((own_ref, other_ref)):
        side = lax.rem(core_ref[0] + n, 2)
        product = jnp.zeros((ZH * COLUMNS, SPAN * COLUMNS), jnp.float32)
        for m, right in enumerate(blocks_of(rights)):
            product = product + jnp.dot(
                left_ref[lax.rem(core_ref[1] + m, X)],
                right,
                preferred_element_type=jnp.float32,
            )
        for zh in range(ZH):
            start = pl.multiple_of(zh * ROWS + side * COLUMNS, 8)
            total[pl.ds(start, COLUMNS), :] = product[zh * COLUMNS : (zh + 1) * COLUMNS]
    for span in range(SPAN):
        for zh in range(ZH):
            out_ref[spot(span, zh)] = chunk_of(total, zh, span * COLUMNS)


def incoming(core, own, other, rights, gate):
    scratch = [pltpu.VMEM((ZH * ROWS, SPAN * COLUMNS), jnp.float32)]
    return call(
        incoming_kernel, CHUNKS, [SMEM] + [VMEM] * (3 + X) + [ANY], scratch, 6 * 10**8
    )(core, own, other, *rights, gate)


def gather_x(block):
    def shift(values, by):
        return lax.ppermute(values, "x", [(x, (x - by) % X) for x in range(X)])

    half = block.shape[0] // 2
    before = shift(block, 3)
    after = shift(block, 1)
    straight = shift(block[:half], 2)
    return [block, after, straight, shift(after[half:], 1), before]


def exchange(values, axes):
    return lax.all_to_all(values, axes, split_axis=0, concat_axis=0, tiled=True)


def swap_cores(values):
    return lax.ppermute(values, "core", [(0, 1), (1, 0)])


def body(
    pair_acts,
    residue_valid,
    chain_index,
    norm_gain,
    norm_bias,
    projection,
    gate_weight,
    chain_bias,
    out_gain,
    out_weight,
):
    row_start = (lax.axis_index("x") * ZH + lax.axis_index("zh")) * ROWS
    core_index = lax.axis_index("core")
    column_block = (lax.axis_index("zl") * 8 + lax.axis_index("y")) * 2 + core_index
    place = jnp.stack([row_start, column_block * COLUMNS]).astype(jnp.int32)
    core = jnp.stack([core_index, lax.axis_index("x")]).astype(jnp.int32)

    vectors = jnp.concatenate([norm_gain, norm_bias, chain_bias], axis=0)
    normed, right = project_right(place, residue_valid, pair_acts, vectors, projection)
    rights = gather_x(assemble(exchange(right, PLANE), ALONE))
    left, gate = left_and_gates(
        place, residue_valid, chain_index, normed, projection, gate_weight, vectors, pair_acts
    )
    halves = outgoing(core, exchange(left, PLANE), rights)
    total = halves[0].astype(jnp.float32) + swap_cores(halves[1]).astype(jnp.float32)
    product = exchange(total.astype(jnp.bfloat16), PLANE)
    middle, normed, both = finish(
        0, place, residue_valid, out_gain, gate, product, out_weight, vectors, projection
    )
    both = exchange(both, PLANE)
    rights = gather_x(assemble(both, RIGHT))
    gate = gates(1, place, chain_index, normed, gate_weight, vectors, middle)
    left = assemble_turned(both, LEFT, rights[0]).reshape(X, ZH * COLUMNS, ZH * ROWS)
    left = exchange(left, "x")
    product = exchange(incoming(core, left, swap_cores(left), rights, gate), PLANE)
    return finish(1, place, residue_valid, out_gain, gate, product, out_weight)[0]


def solution(mesh):
    fine = Mesh(mesh.devices.reshape(SIZES), AXES)
    pairs = P(("x", "zh"), ("zl", "y", "core"), None)
    placed = (pairs, P(), P(), P(), P(), P(), P(), P(), P(), P())
    return jax.shard_map(body, mesh=fine, in_specs=placed, out_specs=pairs, check_vma=False)
```

```python
import functools

import jax
import jax.numpy as jnp
from jax import lax
from jax.experimental import pallas as pl
from jax.experimental.pallas import tpu as pltpu
from jax.sharding import Mesh
from jax.sharding import PartitionSpec as P

AXES = ("zl", "y", "core", "x", "zh")
SIZES = (2, 8, 2, 4, 4)
PLANE = ("y", "zh", "zl")
ROWS = 80
COLUMNS = 40
WIDTH = 128
HIDDEN = 64
X = 4
ZH = 4
SPAN = 16
EPS = 1e-05
DEPTH = 32
LANES = 128
SUB = 8
WHOLE = 3
TAIL = 8 * 9
STRIDE = 40
BATCH = 8
CHUNKS = jax.ShapeDtypeStruct((HIDDEN, SUB, DEPTH // SUB * LANES), jnp.bfloat16)
NORMED = jax.ShapeDtypeStruct((DEPTH, LANES, WIDTH), jnp.bfloat16)
GATES = jax.ShapeDtypeStruct((2, DEPTH, LANES, WIDTH), jnp.float32)
VMEM = pl.BlockSpec(memory_space=pltpu.VMEM)
ANY = pl.BlockSpec(memory_space=pl.ANY)
SMEM = pl.BlockSpec(memory_space=pltpu.SMEM)


def spot(span, zh):
    zl, y = divmod(span, 8)
    return (y * ZH + zh) * 2 + zl


def call(kernel, out_shape, in_specs, scratch_shapes=(), flops=10**8, outs=None, grant=40):
    outs = outs or jax.tree.map(lambda _: VMEM, out_shape)
    moved = 4 * 10**6
    return pl.pallas_call(
        kernel,
        out_shape=out_shape,
        in_specs=in_specs,
        out_specs=outs,
        scratch_shapes=scratch_shapes,
        compiler_params=pltpu.CompilerParams(vmem_limit_bytes=grant * 2**20),
        cost_estimate=pl.CostEstimate(flops=flops, bytes_accessed=moved, transcendentals=0),
    )


def normalize(values, gain, bias):
    average = jnp.mean(values, axis=-1, keepdims=True)
    centred = values - average
    spread = jnp.mean(centred * centred, axis=-1, keepdims=True)
    return centred * lax.rsqrt(spread + EPS) * gain + bias


def batches(work):
    pl.loop(0, WHOLE)(lambda step: work(step * BATCH, 3))
    work(WHOLE * BATCH, 1)


def block_rows(first, count):
    if count == 1:
        return [[TAIL + n] for n in range(BATCH)]
    return [[first + n + WHOLE * SUB * group for group in range(count)] for n in range(BATCH)]


def load_pairs(pair_ref, first, count):
    rows = [row for rows in block_rows(first, count) for row in rows]
    return jnp.concatenate([pair_ref[row].astype(jnp.float32) for row in rows], axis=0)


def pad_rows(values, count):
    size = count * COLUMNS
    empty = jnp.zeros((LANES - size, WIDTH), jnp.float32)
    return [
        jnp.concatenate([values[n * size : (n + 1) * size], empty], axis=0).astype(jnp.bfloat16)
        for n in range(BATCH)
    ]


def spread_columns(place_ref, valid_ref):
    lane = lax.broadcasted_iota(jnp.int32, (1, LANES), 1)
    inside = lane % COLUMNS
    found = jnp.zeros((1, LANES), jnp.float32)
    for column in range(COLUMNS):
        value = valid_ref[place_ref[1] + column].astype(jnp.float32)
        found = jnp.where(inside == column, value, found)
    return jnp.where(lane < 3 * COLUMNS, found, 0.0)


def mask_of(first, count, place_ref, valid_ref, columns):
    lane = lax.broadcasted_iota(jnp.int32, (1, LANES), 1)
    masks = []
    for rows in block_rows(first, count):
        mask = jnp.zeros((1, LANES), jnp.float32)
        for group, row in enumerate(rows):
            value = valid_ref[place_ref[0] + row].astype(jnp.float32)
            start = group * COLUMNS
            inside = (lane >= start) & (lane < start + COLUMNS)
            mask = jnp.where(inside, value, mask)
        masks.append(mask * columns)
    return jnp.concatenate(masks, axis=1)


def weight_of(weight_ref, which, start):
    columns = weight_ref[which][:, start : start + 2 * HIDDEN]
    return columns.astype(jnp.float32).T.astype(jnp.bfloat16)


def factor_of(normed, weight, mask):
    proj = lax.dot_general(
        weight, normed, (((1,), (1,)), ((), ())), preferred_element_type=jnp.float32
    )
    return jax.nn.sigmoid(proj[HIDDEN:]) * proj[:HIDDEN] * mask


def keep_rows(factor, scratch, first):
    for n in range(BATCH):
        place = pl.ds(first + n, HIDDEN, stride=STRIDE)
        scratch[place, :] = factor[:, n * LANES : (n + 1) * LANES]


def put_chunks(scratch, out_ref):
    for channel in range(HIDDEN):
        rows = scratch[pl.ds(channel * STRIDE, DEPTH), :]
        tiles = [rows[n : n + SUB] for n in range(0, DEPTH, SUB)]
        out_ref[channel] = jnp.concatenate(tiles, axis=1).astype(jnp.bfloat16)


SCRATCH = pltpu.VMEM(((HIDDEN + 1) * STRIDE, LANES), jnp.float32)


def right_kernel(
    place_ref,
    valid_ref,
    pair_any,
    gain_any,
    bias_any,
    weight_any,
    normed_ref,
    right_ref,
    right_s,
    pair_ref,
    gain_ref,
    bias_ref,
    weight_ref,
    sems,
):
    moves = ((gain_any, gain_ref), (bias_any, bias_ref), (weight_any, weight_ref), (pair_any, pair_ref))
    copies = [pltpu.make_async_copy(a, b, sems.at[n]) for n, (a, b) in enumerate(moves)]
    for copy in copies:
        copy.start()
    columns = spread_columns(place_ref, valid_ref)
    for copy in copies:
        copy.wait()
    weight = weight_of(weight_ref, 0, 2 * HIDDEN)

    def work(first, count):
        values = load_pairs(pair_ref, first, count)
        pieces = pad_rows(normalize(values, gain_ref[0:1], bias_ref[0:1]), count)
        for n in range(BATCH):
            normed_ref[first + n] = pieces[n]
        mask = mask_of(first, count, place_ref, valid_ref, columns)
        factor = factor_of(jnp.concatenate(pieces, axis=0), weight, mask)
        keep_rows(factor, right_s, first)

    batches(work)
    put_chunks(right_s, right_ref)


def project_right(place, valid, *operands):
    scratch = [pltpu.VMEM(each.shape, each.dtype) for each in operands]
    return call(
        right_kernel,
        [NORMED, CHUNKS],
        [SMEM, SMEM] + [ANY] * 4,
        [SCRATCH] + scratch + [pltpu.SemaphoreType.DMA((4,))],
        grant=60,
    )(place, valid, *operands)


def load_normed(normed_ref, first):
    return normed_ref[pl.ds(first, BATCH)].reshape(BATCH * LANES, WIDTH)


def gate_work(
    which, place_ref, chain_ref, normed_ref, gate_ref, chain_bias_ref, pair_ref, out_ref
):
    row = lax.broadcasted_iota(jnp.int32, (COLUMNS, WIDTH), 0)
    chain_columns = jnp.full((COLUMNS, WIDTH), -1, jnp.int32)
    for column in range(COLUMNS):
        chain_columns = jnp.where(row == column, chain_ref[place_ref[1] + column], chain_columns)
    offset = chain_bias_ref[which : which + 1]

    def work(first, count):
        logit = jnp.dot(
            load_normed(normed_ref, first), gate_ref[which], preferred_element_type=jnp.float32
        )
        for n, rows in enumerate(block_rows(first, count)):
            for group, row in enumerate(rows):
                same = chain_columns == chain_ref[place_ref[0] + row]
                start = n * LANES + group * COLUMNS
                place = pl.ds(group * COLUMNS, COLUMNS)
                out_ref[0, first + n, place] = jax.nn.sigmoid(
                    logit[start : start + COLUMNS] + jnp.where(same, offset, 0.0)
                )
                out_ref[1, first + n, place] = pair_ref[row].astype(jnp.float32)

    return work


def left_and_gate_kernel(
    which,
    place_ref,
    valid_ref,
    chain_ref,
    normed_ref,
    weight_ref,
    gate_ref,
    chain_bias_ref,
    pair_ref,
    left_ref,
    out_ref,
    left_s,
):
    columns = spread_columns(place_ref, valid_ref)
    weight = weight_of(weight_ref, which, 0)
    gate = gate_work(
        which, place_ref, chain_ref, normed_ref, gate_ref, chain_bias_ref, pair_ref, out_ref
    )

    def work(first, count):
        mask = mask_of(first, count, place_ref, valid_ref, columns)
        keep_rows(factor_of(load_normed(normed_ref, first), weight, mask), left_s, first)
        gate(first, count)

    batches(work)
    put_chunks(left_s, left_ref)


def left_and_gates(which, place, valid, chain, normed, weight, gate, chain_bias, pair):
    kernel = functools.partial(left_and_gate_kernel, which)
    return call(kernel, [CHUNKS, GATES], [SMEM] * 3 + [VMEM] * 5, [SCRATCH])(
        place, valid, chain, normed, weight, gate, chain_bias, pair
    )


def finish_kernel(which, place_ref, valid_ref, out_gain_ref, gates_ref, product_ref, out_weight_ref, *rest):
    then = which == 0
    if then:
        gain_ref, bias_ref, weight_ref, out_ref, normed_ref, right_ref, hidden_s, right_s = rest
        new_s = out_ref
        columns = spread_columns(place_ref, valid_ref)
        weight = weight_of(weight_ref, 1, 2 * HIDDEN)
    else:
        out_ref, hidden_s, new_s, out_sem = rest

    def channel(n):
        return product_ref[n].astype(jnp.float32)

    average = channel(0)
    for n in range(1, HIDDEN):
        average = average + channel(n)
    average = average / HIDDEN
    spread = jnp.zeros_like(average)
    for n in range(HIDDEN):
        centred = channel(n) - average
        spread = spread + centred * centred
    scale = lax.rsqrt(spread / HIDDEN + EPS)
    for n in range(HIDDEN):
        hidden = (channel(n) - average) * scale * out_gain_ref[which, n]
        for part in range(DEPTH // SUB):
            place = pl.ds(n * STRIDE + part * SUB, SUB)
            hidden_s[place, :] = hidden[:, part * LANES : (part + 1) * LANES]

    def work(first, count):
        size = count * COLUMNS
        hidden = jnp.concatenate(
            [hidden_s[pl.ds(first + n, HIDDEN, stride=STRIDE), :] for n in range(BATCH)], axis=1
        ).astype(jnp.bfloat16)
        branch = lax.dot_general(
            hidden,
            out_weight_ref[which],
            (((0,), (0,)), ((), ())),
            preferred_element_type=jnp.float32,
        )
        new = jnp.concatenate(
            [
                gates_ref[1, first + n, pl.ds(0, size)]
                + gates_ref[0, first + n, pl.ds(0, size)] * branch[n * LANES : n * LANES + size]
                for n in range(BATCH)
            ],
            axis=0,
        )
        places = [row for rows in block_rows(first, count) for row in rows]
        for n, row in enumerate(places):
            new_s[row] = new[n * COLUMNS : (n + 1) * COLUMNS].astype(jnp.bfloat16)
        if not then:
            for group in range(count):
                span = pl.ds(block_rows(first, count)[0][group], BATCH)
                pltpu.make_async_copy(new_s.at[span], out_ref.at[span], out_sem).start()
            return
        new = new.astype(jnp.bfloat16).astype(jnp.float32)
        pieces = pad_rows(normalize(new, gain_ref[1:2], bias_ref[1:2]), count)
        for n in range(BATCH):
            normed_ref[first + n] = pieces[n]
        mask = mask_of(first, count, place_ref, valid_ref, columns)
        factor = factor_of(jnp.concatenate(pieces, axis=0), weight, mask)
        keep_rows(factor, right_s, first)

    batches(work)
    if then:
        put_chunks(right_s, right_ref)
    else:
        pltpu.make_async_copy(new_s, out_ref, out_sem).wait()


def finish(which, place, valid, out_gain, gate, product, out_weight, *then):
    shape = (ROWS, COLUMNS, WIDTH)
    out = jax.ShapeDtypeStruct(shape, jnp.bfloat16)
    last = [pltpu.VMEM(shape, jnp.bfloat16), pltpu.SemaphoreType.DMA]
    return call(
        functools.partial(finish_kernel, which),
        [out, NORMED, CHUNKS] if then else [out],
        [SMEM] * 3 + [VMEM] * (3 + len(then)),
        [SCRATCH] + ([SCRATCH] if then else last),
        outs=None if then else [ANY],
    )(place, valid, out_gain, gate, product, out_weight, *then)


def gather_rows(chunks_ref, zh, block):
    start = WHOLE * LANES
    if block < 9:
        start = block % 3 * LANES + block // 3 * COLUMNS
    return jnp.concatenate(
        [
            chunks_ref[spot(span, zh)].astype(jnp.float32)[:, start : start + COLUMNS]
            for span in range(SPAN)
        ],
        axis=1,
    )


def assemble_into(chunks_ref, put):
    for zh in range(ZH):
        for block in range(0, ROWS // SUB, 2):
            rows = [gather_rows(chunks_ref, zh, block + n) for n in range(2)]
            put(zh * ROWS + block * SUB, jnp.concatenate(rows, axis=0))


def assemble_kernel(chunks_ref, out_ref):
    def put(start, values):
        rows = values.astype(jnp.bfloat16)
        for x in range(X):
            out_ref[x, pl.ds(start, 2 * SUB)] = rows

    assemble_into(chunks_ref, put)


def assemble(chunks):
    out = jax.ShapeDtypeStruct((X, ZH * ROWS, SPAN * COLUMNS), jnp.bfloat16)
    return call(assemble_kernel, out, [VMEM])(chunks)


def assemble_turned_kernel(chunks_ref, out_ref, whole):
    def put(start, values):
        whole[pl.ds(start, 2 * SUB), :] = values

    assemble_into(chunks_ref, put)
    whole[pl.ds(ZH * ROWS, 64), :] = jnp.zeros((64, SPAN * COLUMNS), jnp.float32)
    for part in range(SPAN * COLUMNS // 128):
        turned = whole[:, part * 128 : (part + 1) * 128].T
        out_ref[pl.ds(part * 128, 128), :] = turned[:, : ZH * ROWS].astype(jnp.bfloat16)


def assemble_turned(chunks):
    out = jax.ShapeDtypeStruct((SPAN * COLUMNS, ZH * ROWS), jnp.bfloat16)
    scratch = [pltpu.VMEM((ZH * ROWS + 64, SPAN * COLUMNS), jnp.float32)]
    return call(assemble_turned_kernel, out, [VMEM], scratch)(chunks)


def chunk_of(total, zh, start):
    pieces = [
        total[pl.ds(zh * ROWS + block * SUB, SUB), :][:, start : start + COLUMNS]
        for block in range(ROWS // SUB)
    ]
    lanes = []
    for tile in range(WHOLE):
        lanes += pieces[tile:9:3] + [jnp.zeros((SUB, LANES - 3 * COLUMNS), jnp.float32)]
    lanes += [pieces[9], jnp.zeros((SUB, LANES - COLUMNS), jnp.float32)]
    return jnp.concatenate(lanes, axis=1).astype(jnp.bfloat16)


def outgoing_kernel(core_ref, left_ref, right_ref, out_ref, left_s, total):
    def put(start, values):
        left_s[pl.ds(start, 2 * SUB), :] = values.astype(jnp.bfloat16)

    assemble_into(left_ref, put)
    for x in range(X):
        total[:, x * ZH * ROWS : (x + 1) * ZH * ROWS] = lax.dot_general(
            left_s[...],
            right_ref[x],
            (((1,), (1,)), ((), ())),
            preferred_element_type=jnp.float32,
        )
    for half in range(2):
        slot = lax.rem(core_ref[0] + half, 2)
        for span in range(SPAN):
            for zh in range(ZH):
                out_ref[slot, spot(span, zh)] = chunk_of(total, zh, (2 * span + half) * COLUMNS)


def outgoing(core, left, right):
    out = jax.ShapeDtypeStruct((2,) + CHUNKS.shape, jnp.bfloat16)
    scratch = [
        pltpu.VMEM((ZH * ROWS, SPAN * COLUMNS), jnp.bfloat16),
        pltpu.VMEM((ZH * ROWS, X * ZH * ROWS), jnp.float32),
    ]
    return call(outgoing_kernel, out, [SMEM, VMEM, VMEM], scratch, 6 * 10**8)(core, left, right)


def incoming_kernel(core_ref, own_ref, other_ref, right_ref, out_ref, total):
    for n, left_ref in enumerate((own_ref, other_ref)):
        side = lax.rem(core_ref[0] + n, 2)
        product = jnp.zeros((ZH * COLUMNS, SPAN * COLUMNS), jnp.float32)
        for x in range(X):
            product = product + jnp.dot(
                left_ref[x],
                right_ref[x],
                preferred_element_type=jnp.float32,
            )
        for zh in range(ZH):
            start = pl.multiple_of(zh * ROWS + side * COLUMNS, 8)
            total[pl.ds(start, COLUMNS), :] = product[zh * COLUMNS : (zh + 1) * COLUMNS]
    for span in range(SPAN):
        for zh in range(ZH):
            out_ref[spot(span, zh)] = chunk_of(total, zh, span * COLUMNS)


def incoming(core, own, other, right):
    scratch = [pltpu.VMEM((ZH * ROWS, SPAN * COLUMNS), jnp.float32)]
    return call(incoming_kernel, CHUNKS, [SMEM, VMEM, VMEM, VMEM], scratch, 6 * 10**8)(
        core, own, other, right
    )


def exchange(values, axes):
    return lax.all_to_all(values, axes, split_axis=0, concat_axis=0, tiled=True)


def swap_cores(values):
    return lax.ppermute(values, "core", [(0, 1), (1, 0)])


def body(
    pair_acts,
    residue_valid,
    chain_index,
    norm_gain,
    norm_bias,
    projection,
    gate_weight,
    chain_bias,
    out_gain,
    out_weight,
):
    row_start = (lax.axis_index("x") * ZH + lax.axis_index("zh")) * ROWS
    core_index = lax.axis_index("core")
    column_block = (lax.axis_index("zl") * 8 + lax.axis_index("y")) * 2 + core_index
    place = jnp.stack([row_start, column_block * COLUMNS]).astype(jnp.int32)
    core = core_index.reshape(1).astype(jnp.int32)

    def factors(which, normed, right, pair):
        right = exchange(assemble(exchange(right, PLANE)), "x")
        left, gate = left_and_gates(
            which,
            place,
            residue_valid,
            chain_index,
            normed,
            projection,
            gate_weight,
            chain_bias,
            pair,
        )
        return exchange(left, PLANE), right, gate

    normed, right = project_right(
        place, residue_valid, pair_acts, norm_gain, norm_bias, projection
    )
    left, right, gate = factors(0, normed, right, pair_acts)
    halves = outgoing(core, left, right)
    total = halves[0].astype(jnp.float32) + swap_cores(halves[1]).astype(jnp.float32)
    product = exchange(total.astype(jnp.bfloat16), PLANE)
    middle, normed, right = finish(
        0,
        place,
        residue_valid,
        out_gain,
        gate,
        product,
        out_weight,
        norm_gain,
        norm_bias,
        projection,
    )
    left, right, gate = factors(1, normed, right, middle)
    left = assemble_turned(left).reshape(X, ZH * COLUMNS, ZH * ROWS)
    left = exchange(left, "x")
    product = exchange(incoming(core, left, swap_cores(left), right), PLANE)
    return finish(1, place, residue_valid, out_gain, gate, product, out_weight)[0]


def solution(mesh):
    fine = Mesh(mesh.devices.reshape(SIZES), AXES)
    pairs = P(("x", "zh"), ("zl", "y", "core"), None)
    placed = (pairs, P(), P(), P(), P(), P(), P(), P(), P(), P())
    return jax.shard_map(body, mesh=fine, in_specs=placed, out_specs=pairs, check_vma=False)
```

```python
import functools

import jax
import jax.numpy as jnp
from jax import lax
from jax.experimental import pallas as pl
from jax.experimental.pallas import tpu as pltpu
from jax.sharding import Mesh
from jax.sharding import PartitionSpec as P

AXES = ("zl", "y", "core", "x", "zh")
SIZES = (2, 8, 2, 4, 4)
PLANE = ("y", "zh", "zl")
ROWS = 80
COLUMNS = 40
WIDTH = 128
HIDDEN = 64
X = 4
ZH = 4
SPAN = 16
EPS = 1e-05
DEPTH = 32
LANES = 128
SUB = 8
WHOLE = 3
TAIL = 8 * 9
STRIDE = 40
BOTH = 56
BATCH = 8
CHUNKS = jax.ShapeDtypeStruct((HIDDEN, SUB, DEPTH // SUB * LANES), jnp.bfloat16)
BOTH_CHUNKS = jax.ShapeDtypeStruct((HIDDEN, SUB, BOTH // SUB * LANES), jnp.bfloat16)
NORMED = jax.ShapeDtypeStruct((DEPTH, LANES, WIDTH), jnp.bfloat16)
GATES = jax.ShapeDtypeStruct((2, DEPTH, LANES, WIDTH), jnp.float32)
VMEM = pl.BlockSpec(memory_space=pltpu.VMEM)
ANY = pl.BlockSpec(memory_space=pl.ANY)
SMEM = pl.BlockSpec(memory_space=pltpu.SMEM)


def spot(span, zh):
    zl, y = divmod(span, 8)
    return (y * ZH + zh) * 2 + zl


def call(kernel, out_shape, in_specs, scratch_shapes=(), flops=10**8, outs=None, grant=40):
    outs = outs or jax.tree.map(lambda _: VMEM, out_shape)
    moved = 4 * 10**6
    return pl.pallas_call(
        kernel,
        out_shape=out_shape,
        in_specs=in_specs,
        out_specs=outs,
        scratch_shapes=scratch_shapes,
        compiler_params=pltpu.CompilerParams(vmem_limit_bytes=grant * 2**20),
        cost_estimate=pl.CostEstimate(flops=flops, bytes_accessed=moved, transcendentals=0),
    )


def normalize(values, gain, bias):
    average = jnp.mean(values, axis=-1, keepdims=True)
    centred = values - average
    spread = jnp.mean(centred * centred, axis=-1, keepdims=True)
    return centred * lax.rsqrt(spread + EPS) * gain + bias


def batches(work):
    for step in range(WHOLE):
        work(step * BATCH, 3)
    work(WHOLE * BATCH, 1)


def block_rows(first, count):
    if count == 1:
        return [[TAIL + n] for n in range(BATCH)]
    return [[first + n + WHOLE * SUB * group for group in range(count)] for n in range(BATCH)]


def load_pairs(pair_ref, first, count):
    rows = [row for rows in block_rows(first, count) for row in rows]
    return jnp.concatenate([pair_ref[row].astype(jnp.float32) for row in rows], axis=0)


def pad_rows(values, count):
    size = count * COLUMNS
    empty = jnp.zeros((LANES - size, WIDTH), jnp.float32)
    return [
        jnp.concatenate([values[n * size : (n + 1) * size], empty], axis=0).astype(jnp.bfloat16)
        for n in range(BATCH)
    ]


def spread_columns(place_ref, valid_ref):
    lane = lax.broadcasted_iota(jnp.int32, (1, LANES), 1)
    inside = lane % COLUMNS
    found = jnp.zeros((1, LANES), jnp.float32)
    for column in range(COLUMNS):
        value = valid_ref[place_ref[1] + column].astype(jnp.float32)
        found = jnp.where(inside == column, value, found)
    return jnp.where(lane < 3 * COLUMNS, found, 0.0)


def mask_of(first, count, place_ref, valid_ref, columns, shift=0):
    lane = lax.broadcasted_iota(jnp.int32, (1, LANES), 1)
    masks = []
    for rows in block_rows(first, count):
        mask = jnp.zeros((1, LANES), jnp.float32)
        for group, row in enumerate(rows):
            value = valid_ref[place_ref[0] + row].astype(jnp.float32)
            start = (group + shift) * COLUMNS
            inside = (lane >= start) & (lane < start + COLUMNS)
            mask = jnp.where(inside, value, mask)
        masks.append(mask * columns)
    return jnp.concatenate(masks, axis=1)


def weight_of(weight_ref, which, start):
    columns = weight_ref[which][:, start : start + 2 * HIDDEN]
    return columns.astype(jnp.float32).T.astype(jnp.bfloat16)


def factor_of(normed, weight, mask):
    proj = lax.dot_general(
        weight, normed, (((1,), (1,)), ((), ())), preferred_element_type=jnp.float32
    )
    return jax.nn.sigmoid(proj[HIDDEN:]) * proj[:HIDDEN] * mask


def keep_rows(factor, scratch, first, stride):
    for n in range(BATCH):
        place = pl.ds(first + n, HIDDEN, stride=stride)
        scratch[place, :] = factor[:, n * LANES : (n + 1) * LANES]


def put_chunks(scratch, out_ref, stride, depth):
    for channel in range(HIDDEN):
        rows = scratch[pl.ds(channel * stride, depth), :]
        tiles = [rows[n : n + SUB] for n in range(0, depth, SUB)]
        out_ref[channel] = jnp.concatenate(tiles, axis=1).astype(jnp.bfloat16)


SCRATCH = pltpu.VMEM(((HIDDEN + 1) * STRIDE, LANES), jnp.float32)


def right_kernel(
    place_ref,
    valid_ref,
    pair_any,
    gain_any,
    bias_any,
    weight_any,
    right_ref,
    right_s,
    pair_ref,
    gain_ref,
    bias_ref,
    weight_ref,
    sems,
):
    moves = [(gain_any, gain_ref), (bias_any, bias_ref), (weight_any, weight_ref)]
    parts = []
    for first in range(0, DEPTH, BATCH):
        for row in block_rows(first, 3 if first < WHOLE * BATCH else 1)[0]:
            parts.append(len(moves))
            rows = pl.ds(row, BATCH)
            moves.append((pair_any.at[rows], pair_ref.at[rows]))
    copies = [pltpu.make_async_copy(a, b, sems.at[n]) for n, (a, b) in enumerate(moves)]
    for copy in copies:
        copy.start()
    columns = spread_columns(place_ref, valid_ref)
    for copy in copies[: parts[0]]:
        copy.wait()
    weight = weight_of(weight_ref, 0, 2 * HIDDEN)

    def work(first, count):
        for part in parts[first // BATCH * 3 :][:count]:
            copies[part].wait()
        values = load_pairs(pair_ref, first, count)
        pieces = pad_rows(normalize(values, gain_ref[0:1], bias_ref[0:1]), count)
        mask = mask_of(first, count, place_ref, valid_ref, columns)
        factor = factor_of(jnp.concatenate(pieces, axis=0), weight, mask)
        keep_rows(factor, right_s, first, STRIDE)

    batches(work)
    put_chunks(right_s, right_ref, STRIDE, DEPTH)


def project_right(place, valid, *operands):
    scratch = [pltpu.VMEM(each.shape, each.dtype) for each in operands]
    return call(
        right_kernel,
        CHUNKS,
        [SMEM, SMEM] + [ANY] * 4,
        [SCRATCH] + scratch + [pltpu.SemaphoreType.DMA((13,))],
        grant=60,
    )(place, valid, *operands)


def load_normed(normed_ref, first):
    return normed_ref[pl.ds(first, BATCH)].reshape(BATCH * LANES, WIDTH)


def gate_work(which, place_ref, chain_ref, normed_of, gate_ref, vectors_ref, pair_ref, out_ref):
    row = lax.broadcasted_iota(jnp.int32, (COLUMNS, WIDTH), 0)
    chain_columns = jnp.full((COLUMNS, WIDTH), -1, jnp.int32)
    for column in range(COLUMNS):
        chain_columns = jnp.where(row == column, chain_ref[place_ref[1] + column], chain_columns)
    offset = vectors_ref[4 + which : 5 + which]

    def work(first, count):
        logit = jnp.dot(
            normed_of(first, count), gate_ref[which], preferred_element_type=jnp.float32
        )
        for n, rows in enumerate(block_rows(first, count)):
            for group, row in enumerate(rows):
                same = chain_columns == chain_ref[place_ref[0] + row]
                start = n * LANES + group * COLUMNS
                place = pl.ds(group * COLUMNS, COLUMNS)
                out_ref[0, first + n, place] = jax.nn.sigmoid(
                    logit[start : start + COLUMNS] + jnp.where(same, offset, 0.0)
                )
                out_ref[1, first + n, place] = pair_ref[row].astype(jnp.float32)

    return work


def gate_kernel(
    which, place_ref, chain_ref, normed_ref, gate_ref, vectors_ref, pair_ref, out_ref
):
    def normed_of(first, count):
        return load_normed(normed_ref, first)

    batches(
        gate_work(which, place_ref, chain_ref, normed_of, gate_ref, vectors_ref, pair_ref, out_ref)
    )


def gates(which, place, chain, normed, gate, vectors, pair):
    kernel = functools.partial(gate_kernel, which)
    return call(kernel, GATES, [SMEM, SMEM, VMEM, VMEM, VMEM, VMEM])(
        place, chain, normed, gate, vectors, pair
    )


def left_and_gate_kernel(
    place_ref,
    valid_ref,
    chain_ref,
    weight_ref,
    gate_ref,
    vectors_ref,
    pair_ref,
    left_ref,
    out_ref,
    left_s,
):
    columns = spread_columns(place_ref, valid_ref)
    weight = weight_of(weight_ref, 0, 0)

    def work(first, count):
        values = load_pairs(pair_ref, first, count)
        pieces = pad_rows(normalize(values, vectors_ref[0:1], vectors_ref[2:3]), count)
        normed = jnp.concatenate(pieces, axis=0)
        mask = mask_of(first, count, place_ref, valid_ref, columns)
        keep_rows(factor_of(normed, weight, mask), left_s, first, STRIDE)
        gate(lambda *_: normed, first, count)

    def gate(normed_of, first, count):
        gate_work(
            0, place_ref, chain_ref, normed_of, gate_ref, vectors_ref, pair_ref, out_ref
        )(first, count)

    batches(work)
    put_chunks(left_s, left_ref, STRIDE, DEPTH)


def left_and_gates(place, valid, chain, weight, gate, vectors, pair):
    return call(left_and_gate_kernel, [CHUNKS, GATES], [SMEM] * 3 + [VMEM] * 4, [SCRATCH])(
        place, valid, chain, weight, gate, vectors, pair
    )


def finish_kernel(which, place_ref, valid_ref, out_gain_ref, gates_ref, product_ref, out_weight_ref, *rest):
    then = which == 0
    if then:
        vectors_ref, weight_ref, out_ref, normed_ref, both_ref, hidden_s, both_s = rest
        new_s = out_ref
        columns = spread_columns(place_ref, valid_ref)
        left_weight = weight_of(weight_ref, 1, 0)
        right_weight = weight_of(weight_ref, 1, 2 * HIDDEN)
    else:
        out_ref, hidden_s, new_s, out_sem = rest

    def channel(n):
        return product_ref[n].astype(jnp.float32)

    average = channel(0)
    for n in range(1, HIDDEN):
        average = average + channel(n)
    average = average / HIDDEN
    spread = jnp.zeros_like(average)
    for n in range(HIDDEN):
        centred = channel(n) - average
        spread = spread + centred * centred
    scale = lax.rsqrt(spread / HIDDEN + EPS)
    for n in range(HIDDEN):
        hidden = (channel(n) - average) * scale * out_gain_ref[which, n]
        for part in range(DEPTH // SUB):
            place = pl.ds(n * STRIDE + part * SUB, SUB)
            hidden_s[place, :] = hidden[:, part * LANES : (part + 1) * LANES]

    def work(first, count):
        size = count * COLUMNS
        hidden = jnp.concatenate(
            [hidden_s[pl.ds(first + n, HIDDEN, stride=STRIDE), :] for n in range(BATCH)], axis=1
        ).astype(jnp.bfloat16)
        branch = lax.dot_general(
            hidden,
            out_weight_ref[which],
            (((0,), (0,)), ((), ())),
            preferred_element_type=jnp.float32,
        )
        new = jnp.concatenate(
            [
                gates_ref[1, first + n, pl.ds(0, size)]
                + gates_ref[0, first + n, pl.ds(0, size)] * branch[n * LANES : n * LANES + size]
                for n in range(BATCH)
            ],
            axis=0,
        )
        places = [row for rows in block_rows(first, count) for row in rows]
        for n, row in enumerate(places):
            new_s[row] = new[n * COLUMNS : (n + 1) * COLUMNS].astype(jnp.bfloat16)
        if not then:
            for group in range(count):
                span = pl.ds(block_rows(first, count)[0][group], BATCH)
                pltpu.make_async_copy(new_s.at[span], out_ref.at[span], out_sem).start()
            return
        new = new.astype(jnp.bfloat16).astype(jnp.float32)
        values = normalize(new, vectors_ref[1:2], vectors_ref[3:4])
        pieces = pad_rows(values, count)
        for n in range(BATCH):
            normed_ref[first + n] = pieces[n]
        mask = mask_of(first, count, place_ref, valid_ref, columns)
        if count == 3:
            normed = jnp.concatenate(pieces, axis=0)
            keep_rows(factor_of(normed, left_weight, mask), both_s, first, BOTH)
            right_first = first + WHOLE * SUB
            keep_rows(factor_of(normed, right_weight, mask), both_s, right_first, BOTH)
        else:
            twice = [values[n * size : (n + 1) * size] for n in range(BATCH) for _ in range(2)]
            normed = jnp.concatenate(
                [
                    each
                    for n in range(BATCH)
                    for each in twice[2 * n : 2 * n + 2]
                    + [jnp.zeros((LANES - 2 * size, WIDTH), jnp.float32)]
                ],
                axis=0,
            ).astype(jnp.bfloat16)
            other = mask_of(first, count, place_ref, valid_ref, columns, 1)
            factor = factor_of(normed, left_weight, mask) + factor_of(normed, right_weight, other)
            keep_rows(factor, both_s, 2 * WHOLE * SUB, BOTH)

    batches(work)
    if then:
        put_chunks(both_s, both_ref, BOTH, BOTH)
    else:
        pltpu.make_async_copy(new_s, out_ref, out_sem).wait()


def finish(which, place, valid, out_gain, gate, product, out_weight, *then):
    shape = (ROWS, COLUMNS, WIDTH)
    out = jax.ShapeDtypeStruct(shape, jnp.bfloat16)
    both = [pltpu.VMEM(((HIDDEN + 1) * BOTH, LANES), jnp.float32)]
    last = [pltpu.VMEM(shape, jnp.bfloat16), pltpu.SemaphoreType.DMA]
    return call(
        functools.partial(finish_kernel, which),
        [out, NORMED, BOTH_CHUNKS] if then else [out],
        [SMEM] * 3 + [VMEM] * (3 + len(then)),
        [SCRATCH] + (both if then else last),
        outs=None if then else [ANY],
    )(place, valid, out_gain, gate, product, out_weight, *then)


ALONE = (0, 3, 0)
LEFT = (0, 6, 0)
RIGHT = (3, 6, COLUMNS)


def gather_rows(chunks_ref, zh, block, layout):
    tile, last_tile, last_lane = layout
    start = last_tile * LANES + last_lane
    if block < 9:
        start = (tile + block % 3) * LANES + block // 3 * COLUMNS
    return jnp.concatenate(
        [
            chunks_ref[spot(span, zh)].astype(jnp.float32)[:, start : start + COLUMNS]
            for span in range(SPAN)
        ],
        axis=1,
    )


def assemble_into(chunks_ref, layout, put):
    for zh in range(ZH):
        for block in range(0, ROWS // SUB, 2):
            rows = [gather_rows(chunks_ref, zh, block + n, layout) for n in range(2)]
            put(zh * ROWS + block * SUB, jnp.concatenate(rows, axis=0))


def assemble_kernel(layout, chunks_ref, out_ref):
    def put(start, values):
        out_ref[pl.ds(start, 2 * SUB), :] = values.astype(jnp.bfloat16)

    assemble_into(chunks_ref, layout, put)


def assemble(chunks, layout):
    out = jax.ShapeDtypeStruct((ZH * ROWS, SPAN * COLUMNS), jnp.bfloat16)
    return call(functools.partial(assemble_kernel, layout), out, [VMEM])(chunks)


def assemble_turned_kernel(layout, chunks_ref, out_ref, whole):
    def put(start, values):
        whole[pl.ds(start, 2 * SUB), :] = values

    assemble_into(chunks_ref, layout, put)
    whole[pl.ds(ZH * ROWS, 64), :] = jnp.zeros((64, SPAN * COLUMNS), jnp.float32)
    for part in range(SPAN * COLUMNS // 128):
        turned = whole[:, part * 128 : (part + 1) * 128].T
        out_ref[pl.ds(part * 128, 128), :] = turned[:, : ZH * ROWS].astype(jnp.bfloat16)


def assemble_turned(chunks, layout):
    out = jax.ShapeDtypeStruct((SPAN * COLUMNS, ZH * ROWS), jnp.bfloat16)
    scratch = [pltpu.VMEM((ZH * ROWS + 64, SPAN * COLUMNS), jnp.float32)]
    kernel = functools.partial(assemble_turned_kernel, layout)
    return call(kernel, out, [VMEM], scratch)(chunks)


def chunk_of(total, zh, start):
    pieces = [
        total[pl.ds(zh * ROWS + block * SUB, SUB), :][:, start : start + COLUMNS]
        for block in range(ROWS // SUB)
    ]
    lanes = []
    for tile in range(WHOLE):
        lanes += pieces[tile:9:3] + [jnp.zeros((SUB, LANES - 3 * COLUMNS), jnp.float32)]
    lanes += [pieces[9], jnp.zeros((SUB, LANES - COLUMNS), jnp.float32)]
    return jnp.concatenate(lanes, axis=1).astype(jnp.bfloat16)


def outgoing_kernel(core_ref, left_ref, *rest):
    rights, (out_ref, left_s, total) = rest[:X], rest[X:]
    assemble_kernel(ALONE, left_ref, left_s)
    for n, right_ref in enumerate(rights):
        total[:, n * ZH * ROWS : (n + 1) * ZH * ROWS] = lax.dot_general(
            left_s[...],
            right_ref[...],
            (((1,), (1,)), ((), ())),
            preferred_element_type=jnp.float32,
        )
    for half in range(2):
        slot = lax.rem(core_ref[0] + half, 2)
        for n in range(X):
            x = lax.rem(core_ref[1] + n, X)
            for low in range(ZH):
                span = ((lax.rem(x, 2) * ZH + low) * ZH) * 2 + x // 2
                for zh in range(ZH):
                    start = ((n * ZH + low) * 2 + half) * COLUMNS
                    out_ref[slot, span + zh * 2] = chunk_of(total, zh, start)


def outgoing(core, left, rights):
    out = jax.ShapeDtypeStruct((2,) + CHUNKS.shape, jnp.bfloat16)
    scratch = [
        pltpu.VMEM((ZH * ROWS, SPAN * COLUMNS), jnp.bfloat16),
        pltpu.VMEM((ZH * ROWS, X * ZH * ROWS), jnp.float32),
    ]
    return call(outgoing_kernel, out, [SMEM] + [VMEM] * (1 + X), scratch, 6 * 10**8)(
        core, left, *rights
    )


def incoming_kernel(core_ref, own_ref, other_ref, *rest):
    rights, (_, out_ref, total) = rest[:X], rest[X:]
    for n, left_ref in enumerate((own_ref, other_ref)):
        side = lax.rem(core_ref[0] + n, 2)
        product = jnp.zeros((ZH * COLUMNS, SPAN * COLUMNS), jnp.float32)
        for m, right_ref in enumerate(rights):
            product = product + jnp.dot(
                left_ref[lax.rem(core_ref[1] + m, X)],
                right_ref[...],
                preferred_element_type=jnp.float32,
            )
        for zh in range(ZH):
            start = pl.multiple_of(zh * ROWS + side * COLUMNS, 8)
            total[pl.ds(start, COLUMNS), :] = product[zh * COLUMNS : (zh + 1) * COLUMNS]
    for span in range(SPAN):
        for zh in range(ZH):
            out_ref[spot(span, zh)] = chunk_of(total, zh, span * COLUMNS)


def incoming(core, own, other, rights, gate):
    scratch = [pltpu.VMEM((ZH * ROWS, SPAN * COLUMNS), jnp.float32)]
    return call(
        incoming_kernel, CHUNKS, [SMEM] + [VMEM] * (2 + X) + [ANY], scratch, 6 * 10**8
    )(core, own, other, *rights, gate)


def gather_x(block):
    def shift(by):
        return lax.ppermute(block, "x", [(x, (x + by) % X) for x in range(X)])

    return [block] + [shift(-n) for n in range(1, X)]


def exchange(values, axes):
    return lax.all_to_all(values, axes, split_axis=0, concat_axis=0, tiled=True)


def swap_cores(values):
    return lax.ppermute(values, "core", [(0, 1), (1, 0)])


def body(
    pair_acts,
    residue_valid,
    chain_index,
    norm_gain,
    norm_bias,
    projection,
    gate_weight,
    chain_bias,
    out_gain,
    out_weight,
):
    row_start = (lax.axis_index("x") * ZH + lax.axis_index("zh")) * ROWS
    core_index = lax.axis_index("core")
    column_block = (lax.axis_index("zl") * 8 + lax.axis_index("y")) * 2 + core_index
    place = jnp.stack([row_start, column_block * COLUMNS]).astype(jnp.int32)
    core = jnp.stack([core_index, lax.axis_index("x")]).astype(jnp.int32)

    vectors = jnp.concatenate([norm_gain, norm_bias, chain_bias], axis=0)
    right = project_right(place, residue_valid, pair_acts, norm_gain, norm_bias, projection)
    rights = gather_x(assemble(exchange(right, PLANE), ALONE))
    left, gate = left_and_gates(
        place, residue_valid, chain_index, projection, gate_weight, vectors, pair_acts
    )
    halves = outgoing(core, exchange(left, PLANE), rights)
    total = halves[0].astype(jnp.float32) + swap_cores(halves[1]).astype(jnp.float32)
    product = exchange(total.astype(jnp.bfloat16), PLANE)
    middle, normed, both = finish(
        0, place, residue_valid, out_gain, gate, product, out_weight, vectors, projection
    )
    both = exchange(both, PLANE)
    rights = gather_x(assemble(both, RIGHT))
    gate = gates(1, place, chain_index, normed, gate_weight, vectors, middle)
    left = assemble_turned(both, LEFT).reshape(X, ZH * COLUMNS, ZH * ROWS)
    left = exchange(left, "x")
    product = exchange(incoming(core, left, swap_cores(left), rights, gate), PLANE)
    return finish(1, place, residue_valid, out_gain, gate, product, out_weight)[0]


def solution(mesh):
    fine = Mesh(mesh.devices.reshape(SIZES), AXES)
    pairs = P(("x", "zh"), ("zl", "y", "core"), None)
    placed = (pairs, P(), P(), P(), P(), P(), P(), P(), P(), P())
    return jax.shard_map(body, mesh=fine, in_specs=placed, out_specs=pairs, check_vma=False)
```

```python
import functools

import jax
import jax.numpy as jnp
from jax import lax
from jax.experimental import pallas as pl
from jax.experimental.pallas import tpu as pltpu
from jax.sharding import Mesh
from jax.sharding import PartitionSpec as P

AXES = ("zl", "y", "core", "x", "zh")
SIZES = (2, 8, 2, 4, 4)
PLANE = ("y", "zh", "zl")
ROWS = 80
COLUMNS = 40
WIDTH = 128
HIDDEN = 64
X = 4
ZH = 4
SPAN = 16
EPS = 1e-05
DEPTH = 32
LANES = 128
SUB = 8
WHOLE = 3
TAIL = 8 * 9
ORDER = (0, 2, 1, 3)
STRIDE = 40
BOTH = 56
BATCH = 8
CHUNKS = jax.ShapeDtypeStruct((HIDDEN, SUB, DEPTH // SUB * LANES), jnp.bfloat16)
BOTH_CHUNKS = jax.ShapeDtypeStruct((HIDDEN, SUB, BOTH // SUB * LANES), jnp.bfloat16)
NORMED = jax.ShapeDtypeStruct((DEPTH, LANES, WIDTH), jnp.bfloat16)
GATES = jax.ShapeDtypeStruct((2, DEPTH, LANES, WIDTH), jnp.float32)
VMEM = pl.BlockSpec(memory_space=pltpu.VMEM)
ANY = pl.BlockSpec(memory_space=pl.ANY)
SMEM = pl.BlockSpec(memory_space=pltpu.SMEM)


def spot(span, zh):
    zl, y = divmod(span, 8)
    return (y * ZH + zh) * 2 + zl


def call(kernel, out_shape, in_specs, scratch_shapes=(), flops=10**8, outs=None, grant=40):
    outs = outs or jax.tree.map(lambda _: VMEM, out_shape)
    moved = 4 * 10**6
    return pl.pallas_call(
        kernel,
        out_shape=out_shape,
        in_specs=in_specs,
        out_specs=outs,
        scratch_shapes=scratch_shapes,
        compiler_params=pltpu.CompilerParams(vmem_limit_bytes=grant * 2**20),
        cost_estimate=pl.CostEstimate(flops=flops, bytes_accessed=moved, transcendentals=0),
    )


def normalize(values, gain, bias):
    average = jnp.mean(values, axis=-1, keepdims=True)
    centred = values - average
    spread = jnp.mean(centred * centred, axis=-1, keepdims=True)
    return centred * lax.rsqrt(spread + EPS) * gain + bias


def batches(work):
    for step in range(WHOLE):
        work(step * BATCH, 3)
    work(WHOLE * BATCH, 1)


def block_rows(first, count):
    if count == 1:
        return [[TAIL + n] for n in range(BATCH)]
    return [[first + n + WHOLE * SUB * group for group in range(count)] for n in range(BATCH)]


def load_pairs(pair_ref, first, count):
    rows = [row for rows in block_rows(first, count) for row in rows]
    return jnp.concatenate([pair_ref[row].astype(jnp.float32) for row in rows], axis=0)


def pad_rows(values, count):
    size = count * COLUMNS
    empty = jnp.zeros((LANES - size, WIDTH), jnp.float32)
    return [
        jnp.concatenate([values[n * size : (n + 1) * size], empty], axis=0).astype(jnp.bfloat16)
        for n in range(BATCH)
    ]


def spread_columns(place_ref, valid_ref):
    lane = lax.broadcasted_iota(jnp.int32, (1, LANES), 1)
    inside = lane % COLUMNS
    found = jnp.zeros((1, LANES), jnp.float32)
    for column in range(COLUMNS):
        value = valid_ref[place_ref[1] + column].astype(jnp.float32)
        found = jnp.where(inside == column, value, found)
    return jnp.where(lane < 3 * COLUMNS, found, 0.0)


def mask_of(first, count, place_ref, valid_ref, columns, shift=0):
    lane = lax.broadcasted_iota(jnp.int32, (1, LANES), 1)
    masks = []
    for rows in block_rows(first, count):
        mask = jnp.zeros((1, LANES), jnp.float32)
        for group, row in enumerate(rows):
            value = valid_ref[place_ref[0] + row].astype(jnp.float32)
            start = (group + shift) * COLUMNS
            inside = (lane >= start) & (lane < start + COLUMNS)
            mask = jnp.where(inside, value, mask)
        masks.append(mask * columns)
    return jnp.concatenate(masks, axis=1)


def weight_of(weight_ref, which, start):
    columns = weight_ref[which][:, start : start + 2 * HIDDEN]
    return columns.astype(jnp.float32).T.astype(jnp.bfloat16)


def factor_of(normed, weight, mask):
    proj = lax.dot_general(
        weight, normed, (((1,), (1,)), ((), ())), preferred_element_type=jnp.float32
    )
    return jax.nn.sigmoid(proj[HIDDEN:]) * proj[:HIDDEN] * mask


def keep_rows(factor, scratch, first, stride):
    for n in range(BATCH):
        place = pl.ds(first + n, HIDDEN, stride=stride)
        scratch[place, :] = factor[:, n * LANES : (n + 1) * LANES]


def put_chunks(scratch, out_ref, stride, depth, channels=range(HIDDEN)):
    for channel in channels:
        rows = scratch[pl.ds(channel * stride, depth), :]
        tiles = [rows[n : n + SUB] for n in range(0, depth, SUB)]
        out_ref[channel] = jnp.concatenate(tiles, axis=1).astype(jnp.bfloat16)


SCRATCH = pltpu.VMEM(((HIDDEN + 1) * STRIDE, LANES), jnp.float32)


def right_kernel(
    place_ref,
    valid_ref,
    pair_any,
    gain_any,
    bias_any,
    weight_any,
    right_any,
    right_s,
    right_ref,
    pair_ref,
    gain_ref,
    bias_ref,
    weight_ref,
    sems,
    out_sem,
):
    moves = [(gain_any, gain_ref), (bias_any, bias_ref), (weight_any, weight_ref)]
    parts = []
    for first in range(0, DEPTH, BATCH):
        for row in block_rows(first, 3 if first < WHOLE * BATCH else 1)[0]:
            parts.append(len(moves))
            rows = pl.ds(row, BATCH)
            moves.append((pair_any.at[rows], pair_ref.at[rows]))
    copies = [pltpu.make_async_copy(a, b, sems.at[n]) for n, (a, b) in enumerate(moves)]
    for copy in copies:
        copy.start()
    columns = spread_columns(place_ref, valid_ref)
    for copy in copies[: parts[0]]:
        copy.wait()
    weight = weight_of(weight_ref, 0, 2 * HIDDEN)

    def work(first, count):
        for part in parts[first // BATCH * 3 :][:count]:
            copies[part].wait()
        values = load_pairs(pair_ref, first, count)
        pieces = pad_rows(normalize(values, gain_ref[0:1], bias_ref[0:1]), count)
        mask = mask_of(first, count, place_ref, valid_ref, columns)
        factor = factor_of(jnp.concatenate(pieces, axis=0), weight, mask)
        keep_rows(factor, right_s, first, STRIDE)

    batches(work)
    for part in range(0, HIDDEN, 16):
        put_chunks(right_s, right_ref, STRIDE, DEPTH, range(part, part + 16))
        span = pl.ds(part, 16)
        pltpu.make_async_copy(right_ref.at[span], right_any.at[span], out_sem).start()
    pltpu.make_async_copy(right_ref, right_any, out_sem).wait()


def project_right(place, valid, *operands):
    scratch = [pltpu.VMEM(each.shape, each.dtype) for each in (CHUNKS,) + operands]
    sems = [pltpu.SemaphoreType.DMA((13,)), pltpu.SemaphoreType.DMA]
    return call(
        right_kernel,
        CHUNKS,
        [SMEM, SMEM] + [ANY] * 4,
        [SCRATCH] + scratch + sems,
        outs=ANY,
        grant=60,
    )(place, valid, *operands)


def load_normed(normed_ref, first):
    return normed_ref[pl.ds(first, BATCH)].reshape(BATCH * LANES, WIDTH)


def gate_work(which, place_ref, chain_ref, normed_of, gate_ref, vectors_ref, pair_ref, out_ref):
    row = lax.broadcasted_iota(jnp.int32, (COLUMNS, WIDTH), 0)
    chain_columns = jnp.full((COLUMNS, WIDTH), -1, jnp.int32)
    for column in range(COLUMNS):
        chain_columns = jnp.where(row == column, chain_ref[place_ref[1] + column], chain_columns)
    offset = vectors_ref[4 + which : 5 + which]

    def work(first, count):
        logit = jnp.dot(
            normed_of(first, count), gate_ref[which], preferred_element_type=jnp.float32
        )
        for n, rows in enumerate(block_rows(first, count)):
            for group, row in enumerate(rows):
                same = chain_columns == chain_ref[place_ref[0] + row]
                start = n * LANES + group * COLUMNS
                place = pl.ds(group * COLUMNS, COLUMNS)
                out_ref[0, first + n, place] = jax.nn.sigmoid(
                    logit[start : start + COLUMNS] + jnp.where(same, offset, 0.0)
                )
                out_ref[1, first + n, place] = pair_ref[row].astype(jnp.float32)

    return work


def gate_kernel(
    which, place_ref, chain_ref, normed_ref, gate_ref, vectors_ref, pair_ref, out_ref
):
    def normed_of(first, count):
        return load_normed(normed_ref, first)

    batches(
        gate_work(which, place_ref, chain_ref, normed_of, gate_ref, vectors_ref, pair_ref, out_ref)
    )


def gates(which, place, chain, normed, gate, vectors, pair):
    kernel = functools.partial(gate_kernel, which)
    return call(kernel, GATES, [SMEM, SMEM, VMEM, VMEM, VMEM, VMEM])(
        place, chain, normed, gate, vectors, pair
    )


def left_and_gate_kernel(
    place_ref,
    valid_ref,
    chain_ref,
    weight_ref,
    gate_ref,
    vectors_ref,
    pair_ref,
    left_ref,
    out_ref,
    left_s,
):
    columns = spread_columns(place_ref, valid_ref)
    weight = weight_of(weight_ref, 0, 0)

    def work(first, count):
        values = load_pairs(pair_ref, first, count)
        pieces = pad_rows(normalize(values, vectors_ref[0:1], vectors_ref[2:3]), count)
        normed = jnp.concatenate(pieces, axis=0)
        mask = mask_of(first, count, place_ref, valid_ref, columns)
        keep_rows(factor_of(normed, weight, mask), left_s, first, STRIDE)
        gate(lambda *_: normed, first, count)

    def gate(normed_of, first, count):
        gate_work(
            0, place_ref, chain_ref, normed_of, gate_ref, vectors_ref, pair_ref, out_ref
        )(first, count)

    batches(work)
    put_chunks(left_s, left_ref, STRIDE, DEPTH)


def left_and_gates(place, valid, chain, weight, gate, vectors, pair):
    return call(left_and_gate_kernel, [CHUNKS, GATES], [SMEM] * 3 + [VMEM] * 4, [SCRATCH])(
        place, valid, chain, weight, gate, vectors, pair
    )


def finish_kernel(which, place_ref, valid_ref, out_gain_ref, gates_ref, product_ref, out_weight_ref, *rest):
    then = which == 0
    if then:
        vectors_ref, weight_ref, out_ref, normed_ref, both_ref, hidden_s, both_s = rest
        new_s = out_ref
        columns = spread_columns(place_ref, valid_ref)
        left_weight = weight_of(weight_ref, 1, 0)
        right_weight = weight_of(weight_ref, 1, 2 * HIDDEN)
    else:
        out_ref, hidden_s, new_s, out_sem = rest

    def channel(n):
        return product_ref[n].astype(jnp.float32)

    average = channel(0)
    for n in range(1, HIDDEN):
        average = average + channel(n)
    average = average / HIDDEN
    spread = jnp.zeros_like(average)
    for n in range(HIDDEN):
        centred = channel(n) - average
        spread = spread + centred * centred
    scale = lax.rsqrt(spread / HIDDEN + EPS)
    for n in range(HIDDEN):
        hidden = (channel(n) - average) * scale * out_gain_ref[which, n]
        for part in range(DEPTH // SUB):
            place = pl.ds(n * STRIDE + part * SUB, SUB)
            hidden_s[place, :] = hidden[:, part * LANES : (part + 1) * LANES]

    def work(first, count):
        size = count * COLUMNS
        hidden = jnp.concatenate(
            [hidden_s[pl.ds(first + n, HIDDEN, stride=STRIDE), :] for n in range(BATCH)], axis=1
        ).astype(jnp.bfloat16)
        branch = lax.dot_general(
            hidden,
            out_weight_ref[which],
            (((0,), (0,)), ((), ())),
            preferred_element_type=jnp.float32,
        )
        new = jnp.concatenate(
            [
                gates_ref[1, first + n, pl.ds(0, size)]
                + gates_ref[0, first + n, pl.ds(0, size)] * branch[n * LANES : n * LANES + size]
                for n in range(BATCH)
            ],
            axis=0,
        )
        places = [row for rows in block_rows(first, count) for row in rows]
        for n, row in enumerate(places):
            new_s[row] = new[n * COLUMNS : (n + 1) * COLUMNS].astype(jnp.bfloat16)
        if not then:
            for group in range(count):
                span = pl.ds(block_rows(first, count)[0][group], BATCH)
                pltpu.make_async_copy(new_s.at[span], out_ref.at[span], out_sem).start()
            return
        new = new.astype(jnp.bfloat16).astype(jnp.float32)
        values = normalize(new, vectors_ref[1:2], vectors_ref[3:4])
        pieces = pad_rows(values, count)
        for n in range(BATCH):
            normed_ref[first + n] = pieces[n]
        mask = mask_of(first, count, place_ref, valid_ref, columns)
        if count == 3:
            normed = jnp.concatenate(pieces, axis=0)
            keep_rows(factor_of(normed, left_weight, mask), both_s, first, BOTH)
            right_first = first + WHOLE * SUB
            keep_rows(factor_of(normed, right_weight, mask), both_s, right_first, BOTH)
        else:
            twice = [values[n * size : (n + 1) * size] for n in range(BATCH) for _ in range(2)]
            normed = jnp.concatenate(
                [
                    each
                    for n in range(BATCH)
                    for each in twice[2 * n : 2 * n + 2]
                    + [jnp.zeros((LANES - 2 * size, WIDTH), jnp.float32)]
                ],
                axis=0,
            ).astype(jnp.bfloat16)
            other = mask_of(first, count, place_ref, valid_ref, columns, 1)
            factor = factor_of(normed, left_weight, mask) + factor_of(normed, right_weight, other)
            keep_rows(factor, both_s, 2 * WHOLE * SUB, BOTH)

    batches(work)
    if then:
        put_chunks(both_s, both_ref, BOTH, BOTH)
    else:
        pltpu.make_async_copy(new_s, out_ref, out_sem).wait()


def finish(which, place, valid, out_gain, gate, product, out_weight, *then):
    shape = (ROWS, COLUMNS, WIDTH)
    out = jax.ShapeDtypeStruct(shape, jnp.bfloat16)
    both = [pltpu.VMEM(((HIDDEN + 1) * BOTH, LANES), jnp.float32)]
    last = [pltpu.VMEM(shape, jnp.bfloat16), pltpu.SemaphoreType.DMA]
    return call(
        functools.partial(finish_kernel, which),
        [out, NORMED, BOTH_CHUNKS] if then else [out],
        [SMEM] * 3 + [VMEM] * (3 + len(then)),
        [SCRATCH] + (both if then else last),
        outs=None if then else [ANY],
    )(place, valid, out_gain, gate, product, out_weight, *then)


ALONE = (0, 3, 0)
LEFT = (0, 6, 0)
RIGHT = (3, 6, COLUMNS)


def gather_rows(chunks_ref, zh, block, layout):
    tile, last_tile, last_lane = layout
    start = last_tile * LANES + last_lane
    if block < 9:
        start = (tile + block % 3) * LANES + block // 3 * COLUMNS
    return jnp.concatenate(
        [
            chunks_ref[spot(span, zh)].astype(jnp.float32)[:, start : start + COLUMNS]
            for span in range(SPAN)
        ],
        axis=1,
    )


def assemble_into(chunks_ref, layout, put):
    for zh in range(ZH):
        for block in range(0, ROWS // SUB, 2):
            rows = [gather_rows(chunks_ref, zh, block + n, layout) for n in range(2)]
            put(zh * ROWS + block * SUB, jnp.concatenate(rows, axis=0))


def assemble_kernel(layout, chunks_ref, out_ref):
    def put(start, values):
        out_ref[pl.ds(start, 2 * SUB), :] = values.astype(jnp.bfloat16)

    assemble_into(chunks_ref, layout, put)


def assemble(chunks, layout):
    out = jax.ShapeDtypeStruct((ZH * ROWS, SPAN * COLUMNS), jnp.bfloat16)
    return call(functools.partial(assemble_kernel, layout), out, [VMEM])(chunks)


def assemble_turned_kernel(layout, chunks_ref, out_ref, whole):
    def put(start, values):
        whole[pl.ds(start, 2 * SUB), :] = values

    assemble_into(chunks_ref, layout, put)
    whole[pl.ds(ZH * ROWS, 64), :] = jnp.zeros((64, SPAN * COLUMNS), jnp.float32)
    for part in range(SPAN * COLUMNS // 128):
        turned = whole[:, part * 128 : (part + 1) * 128].T
        out_ref[pl.ds(part * 128, 128), :] = turned[:, : ZH * ROWS].astype(jnp.bfloat16)


def assemble_turned(chunks, layout):
    out = jax.ShapeDtypeStruct((SPAN * COLUMNS, ZH * ROWS), jnp.bfloat16)
    scratch = [pltpu.VMEM((ZH * ROWS + 64, SPAN * COLUMNS), jnp.float32)]
    kernel = functools.partial(assemble_turned_kernel, layout)
    return call(kernel, out, [VMEM], scratch)(chunks)


def chunk_of(total, zh, start):
    pieces = [
        total[pl.ds(zh * ROWS + block * SUB, SUB), :][:, start : start + COLUMNS]
        for block in range(ROWS // SUB)
    ]
    lanes = []
    for tile in range(WHOLE):
        lanes += pieces[tile:9:3] + [jnp.zeros((SUB, LANES - 3 * COLUMNS), jnp.float32)]
    lanes += [pieces[9], jnp.zeros((SUB, LANES - COLUMNS), jnp.float32)]
    return jnp.concatenate(lanes, axis=1).astype(jnp.bfloat16)


def outgoing_kernel(core_ref, left_ref, *rest):
    rights, (out_ref, left_s, total) = rest[:X], rest[X:]
    assemble_kernel(ALONE, left_ref, left_s)
    for n, right_ref in enumerate(rights):
        total[:, n * ZH * ROWS : (n + 1) * ZH * ROWS] = lax.dot_general(
            left_s[...],
            right_ref[...],
            (((1,), (1,)), ((), ())),
            preferred_element_type=jnp.float32,
        )
    for half in range(2):
        slot = lax.rem(core_ref[0] + half, 2)
        for n, ahead in enumerate(ORDER):
            x = lax.rem(core_ref[1] + ahead, X)
            for low in range(ZH):
                span = ((lax.rem(x, 2) * ZH + low) * ZH) * 2 + x // 2
                for zh in range(ZH):
                    start = ((n * ZH + low) * 2 + half) * COLUMNS
                    out_ref[slot, span + zh * 2] = chunk_of(total, zh, start)


def outgoing(core, left, rights):
    out = jax.ShapeDtypeStruct((2,) + CHUNKS.shape, jnp.bfloat16)
    scratch = [
        pltpu.VMEM((ZH * ROWS, SPAN * COLUMNS), jnp.bfloat16),
        pltpu.VMEM((ZH * ROWS, X * ZH * ROWS), jnp.float32),
    ]
    return call(outgoing_kernel, out, [SMEM] + [VMEM] * (1 + X), scratch, 6 * 10**8)(
        core, left, *rights
    )


def incoming_kernel(core_ref, own_ref, other_ref, *rest):
    rights, (_, out_ref, total) = rest[:X], rest[X:]
    for n, left_ref in enumerate((own_ref, other_ref)):
        side = lax.rem(core_ref[0] + n, 2)
        product = jnp.zeros((ZH * COLUMNS, SPAN * COLUMNS), jnp.float32)
        for ahead, right_ref in zip(ORDER, rights):
            product = product + jnp.dot(
                left_ref[lax.rem(core_ref[1] + ahead, X)],
                right_ref[...],
                preferred_element_type=jnp.float32,
            )
        for zh in range(ZH):
            start = pl.multiple_of(zh * ROWS + side * COLUMNS, 8)
            total[pl.ds(start, COLUMNS), :] = product[zh * COLUMNS : (zh + 1) * COLUMNS]
    for span in range(SPAN):
        for zh in range(ZH):
            out_ref[spot(span, zh)] = chunk_of(total, zh, span * COLUMNS)


def incoming(core, own, other, rights, gate):
    scratch = [pltpu.VMEM((ZH * ROWS, SPAN * COLUMNS), jnp.float32)]
    return call(
        incoming_kernel, CHUNKS, [SMEM] + [VMEM] * (2 + X) + [ANY], scratch, 6 * 10**8
    )(core, own, other, *rights, gate)


def gather_x(block):
    def shift(ahead):
        return lax.ppermute(block, "x", [(x, (x - ahead) % X) for x in range(X)])

    return [block] + [shift(ahead) for ahead in ORDER[1:]]


def exchange(values, axes):
    return lax.all_to_all(values, axes, split_axis=0, concat_axis=0, tiled=True)


def swap_cores(values):
    return lax.ppermute(values, "core", [(0, 1), (1, 0)])


def body(
    pair_acts,
    residue_valid,
    chain_index,
    norm_gain,
    norm_bias,
    projection,
    gate_weight,
    chain_bias,
    out_gain,
    out_weight,
):
    row_start = (lax.axis_index("x") * ZH + lax.axis_index("zh")) * ROWS
    core_index = lax.axis_index("core")
    column_block = (lax.axis_index("zl") * 8 + lax.axis_index("y")) * 2 + core_index
    place = jnp.stack([row_start, column_block * COLUMNS]).astype(jnp.int32)
    core = jnp.stack([core_index, lax.axis_index("x")]).astype(jnp.int32)

    vectors = jnp.concatenate([norm_gain, norm_bias, chain_bias], axis=0)
    right = project_right(place, residue_valid, pair_acts, norm_gain, norm_bias, projection)
    rights = gather_x(assemble(exchange(right, PLANE), ALONE))
    left, gate = left_and_gates(
        place, residue_valid, chain_index, projection, gate_weight, vectors, pair_acts
    )
    halves = outgoing(core, exchange(left, PLANE), rights)
    total = halves[0].astype(jnp.float32) + swap_cores(halves[1]).astype(jnp.float32)
    product = exchange(total.astype(jnp.bfloat16), PLANE)
    middle, normed, both = finish(
        0, place, residue_valid, out_gain, gate, product, out_weight, vectors, projection
    )
    both = exchange(both, PLANE)
    rights = gather_x(assemble(both, RIGHT))
    gate = gates(1, place, chain_index, normed, gate_weight, vectors, middle)
    left = assemble_turned(both, LEFT).reshape(X, ZH * COLUMNS, ZH * ROWS)
    left = exchange(left, "x")
    product = exchange(incoming(core, left, swap_cores(left), rights, gate), PLANE)
    return finish(1, place, residue_valid, out_gain, gate, product, out_weight)[0]


def solution(mesh):
    fine = Mesh(mesh.devices.reshape(SIZES), AXES)
    pairs = P(("x", "zh"), ("zl", "y", "core"), None)
    placed = (pairs, P(), P(), P(), P(), P(), P(), P(), P(), P())
    return jax.shard_map(body, mesh=fine, in_specs=placed, out_specs=pairs, check_vma=False)
```

```python
import functools

import jax
import jax.numpy as jnp
from jax import lax
from jax.experimental import pallas as pl
from jax.experimental.pallas import tpu as pltpu
from jax.sharding import Mesh
from jax.sharding import PartitionSpec as P

AXES = ("zl", "y", "core", "x", "zh")
SIZES = (2, 8, 2, 4, 4)
PLANE = ("y", "zh", "zl")
ROWS = 80
COLUMNS = 40
WIDTH = 128
HIDDEN = 64
X = 4
ZH = 4
SPAN = 16
EPS = 1e-05
DEPTH = 32
LANES = 128
SUB = 8
WHOLE = 3
TAIL = 8 * 9
ORDER = (0, 2, 1, 3)
STRIDE = 40
BOTH = 56
BATCH = 8
CHUNKS = jax.ShapeDtypeStruct((HIDDEN, SUB, DEPTH // SUB * LANES), jnp.bfloat16)
BOTH_CHUNKS = jax.ShapeDtypeStruct((HIDDEN, SUB, BOTH // SUB * LANES), jnp.bfloat16)
GATES = jax.ShapeDtypeStruct((2, DEPTH, LANES, WIDTH), jnp.float32)
VMEM = pl.BlockSpec(memory_space=pltpu.VMEM)
ANY = pl.BlockSpec(memory_space=pl.ANY)
SMEM = pl.BlockSpec(memory_space=pltpu.SMEM)


def spot(span, zh):
    zl, y = divmod(span, 8)
    return (y * ZH + zh) * 2 + zl


def call(kernel, out_shape, in_specs, scratch_shapes=(), flops=10**8, outs=None, grant=40):
    outs = outs or jax.tree.map(lambda _: VMEM, out_shape)
    moved = 4 * 10**6
    return pl.pallas_call(
        kernel,
        out_shape=out_shape,
        in_specs=in_specs,
        out_specs=outs,
        scratch_shapes=scratch_shapes,
        compiler_params=pltpu.CompilerParams(vmem_limit_bytes=grant * 2**20),
        cost_estimate=pl.CostEstimate(flops=flops, bytes_accessed=moved, transcendentals=0),
    )


def normalize(values, gain, bias):
    average = jnp.mean(values, axis=-1, keepdims=True)
    centred = values - average
    spread = jnp.mean(centred * centred, axis=-1, keepdims=True)
    return centred * lax.rsqrt(spread + EPS) * gain + bias


def batches(work):
    for step in range(WHOLE):
        work(step * BATCH, 3)
    work(WHOLE * BATCH, 1)


def block_rows(first, count):
    if count == 1:
        return [[TAIL + n] for n in range(BATCH)]
    return [[first + n + WHOLE * SUB * group for group in range(count)] for n in range(BATCH)]


def load_pairs(pair_ref, first, count):
    rows = [row for rows in block_rows(first, count) for row in rows]
    return jnp.concatenate([pair_ref[row].astype(jnp.float32) for row in rows], axis=0)


def pad_rows(values, count):
    size = count * COLUMNS
    empty = jnp.zeros((LANES - size, WIDTH), jnp.float32)
    return [
        jnp.concatenate([values[n * size : (n + 1) * size], empty], axis=0).astype(jnp.bfloat16)
        for n in range(BATCH)
    ]


def spread_columns(place_ref, valid_ref):
    lane = lax.broadcasted_iota(jnp.int32, (1, LANES), 1)
    inside = lane % COLUMNS
    found = jnp.zeros((1, LANES), jnp.float32)
    for column in range(COLUMNS):
        value = valid_ref[place_ref[1] + column].astype(jnp.float32)
        found = jnp.where(inside == column, value, found)
    return jnp.where(lane < 3 * COLUMNS, found, 0.0)


def mask_of(first, count, place_ref, valid_ref, columns, shift=0):
    lane = lax.broadcasted_iota(jnp.int32, (1, LANES), 1)
    masks = []
    for rows in block_rows(first, count):
        mask = jnp.zeros((1, LANES), jnp.float32)
        for group, row in enumerate(rows):
            value = valid_ref[place_ref[0] + row].astype(jnp.float32)
            start = (group + shift) * COLUMNS
            inside = (lane >= start) & (lane < start + COLUMNS)
            mask = jnp.where(inside, value, mask)
        masks.append(mask * columns)
    return jnp.concatenate(masks, axis=1)


def weight_of(weight_ref, which, start):
    columns = weight_ref[which][:, start : start + 2 * HIDDEN]
    return columns.astype(jnp.float32).T.astype(jnp.bfloat16)


def factor_of(normed, weight, mask):
    proj = lax.dot_general(
        weight, normed, (((1,), (1,)), ((), ())), preferred_element_type=jnp.float32
    )
    return jax.nn.sigmoid(proj[HIDDEN:]) * proj[:HIDDEN] * mask


def keep_rows(factor, scratch, first, stride):
    for n in range(BATCH):
        place = pl.ds(first + n, HIDDEN, stride=stride)
        scratch[place, :] = factor[:, n * LANES : (n + 1) * LANES]


def put_chunks(scratch, out_ref, channels):
    for channel in channels:
        rows = scratch[pl.ds(channel * BOTH, BOTH), :]
        tiles = [rows[n : n + SUB] for n in range(0, BOTH, SUB)]
        out_ref[channel] = jnp.concatenate(tiles, axis=1).astype(jnp.bfloat16)


def factor_rows(first, count, normed, weights, mask_at, both_s):
    left_weight, right_weight = weights
    if count == 3:
        rows = jnp.concatenate(pad_rows(normed, count), axis=0)
        mask = mask_at(first, count, 0)
        keep_rows(factor_of(rows, left_weight, mask), both_s, first, BOTH)
        keep_rows(factor_of(rows, right_weight, mask), both_s, first + WHOLE * SUB, BOTH)
        return
    pieces = []
    for n in range(BATCH):
        piece = normed[n * COLUMNS : (n + 1) * COLUMNS]
        pieces += [piece, piece, jnp.zeros((LANES - 2 * COLUMNS, WIDTH), jnp.float32)]
    rows = jnp.concatenate(pieces, axis=0).astype(jnp.bfloat16)
    factor = factor_of(rows, left_weight, mask_at(first, count, 0))
    factor = factor + factor_of(rows, right_weight, mask_at(first, count, 1))
    keep_rows(factor, both_s, 2 * WHOLE * SUB, BOTH)


SCRATCH = pltpu.VMEM(((HIDDEN + 1) * STRIDE, LANES), jnp.float32)
BOTH_SCRATCH = pltpu.VMEM(((HIDDEN + 1) * BOTH, LANES), jnp.float32)


def project_kernel(
    place_ref,
    valid_ref,
    pair_any,
    gain_any,
    bias_any,
    weight_any,
    both_any,
    both_s,
    both_ref,
    pair_ref,
    gain_ref,
    bias_ref,
    weight_ref,
    sems,
    out_sem,
):
    moves = [(gain_any, gain_ref), (bias_any, bias_ref), (weight_any, weight_ref)]
    parts = []
    for first in range(0, DEPTH, BATCH):
        for row in block_rows(first, 3 if first < WHOLE * BATCH else 1)[0]:
            parts.append(len(moves))
            rows = pl.ds(row, BATCH)
            moves.append((pair_any.at[rows], pair_ref.at[rows]))
    copies = [pltpu.make_async_copy(a, b, sems.at[n]) for n, (a, b) in enumerate(moves)]
    for copy in copies:
        copy.start()
    columns = spread_columns(place_ref, valid_ref)
    for copy in copies[: parts[0]]:
        copy.wait()
    weights = [weight_of(weight_ref, 0, start) for start in (0, 2 * HIDDEN)]

    def mask_at(first, count, shift):
        return mask_of(first, count, place_ref, valid_ref, columns, shift)

    def work(first, count):
        for part in parts[first // BATCH * 3 :][:count]:
            copies[part].wait()
        values = load_pairs(pair_ref, first, count)
        normed = normalize(values, gain_ref[0:1], bias_ref[0:1])
        factor_rows(first, count, normed, weights, mask_at, both_s)

    batches(work)
    for part in range(0, HIDDEN, 16):
        put_chunks(both_s, both_ref, range(part, part + 16))
        span = pl.ds(part, 16)
        pltpu.make_async_copy(both_ref.at[span], both_any.at[span], out_sem).start()
    pltpu.make_async_copy(both_ref, both_any, out_sem).wait()


def project(place, valid, *operands):
    scratch = [pltpu.VMEM(each.shape, each.dtype) for each in (BOTH_CHUNKS,) + operands]
    sems = [pltpu.SemaphoreType.DMA((13,)), pltpu.SemaphoreType.DMA]
    return call(
        project_kernel,
        BOTH_CHUNKS,
        [SMEM, SMEM] + [ANY] * 4,
        [BOTH_SCRATCH] + scratch + sems,
        outs=ANY,
        grant=60,
    )(place, valid, *operands)


def gate_kernel(which, place_ref, chain_ref, gate_ref, vectors_ref, pair_ref, _, out_ref):
    row = lax.broadcasted_iota(jnp.int32, (COLUMNS, WIDTH), 0)
    chain_columns = jnp.full((COLUMNS, WIDTH), -1, jnp.int32)
    for column in range(COLUMNS):
        chain_columns = jnp.where(row == column, chain_ref[place_ref[1] + column], chain_columns)
    gain, bias, offset = [vectors_ref[n + which : n + which + 1] for n in (0, 2, 4)]

    def work(first, count):
        values = load_pairs(pair_ref, first, count)
        pieces = pad_rows(normalize(values, gain, bias), count)
        logit = jnp.dot(
            jnp.concatenate(pieces, axis=0), gate_ref[which], preferred_element_type=jnp.float32
        )
        for n, rows in enumerate(block_rows(first, count)):
            for group, row in enumerate(rows):
                same = chain_columns == chain_ref[place_ref[0] + row]
                start = n * LANES + group * COLUMNS
                place = pl.ds(group * COLUMNS, COLUMNS)
                out_ref[0, first + n, place] = jax.nn.sigmoid(
                    logit[start : start + COLUMNS] + jnp.where(same, offset, 0.0)
                )
                old = (n * count + group) * COLUMNS
                out_ref[1, first + n, place] = values[old : old + COLUMNS]

    batches(work)


def gates(which, place, chain, gate, vectors, pair, after):
    kernel = functools.partial(gate_kernel, which)
    return call(kernel, GATES, [SMEM, SMEM, VMEM, VMEM, VMEM, ANY])(
        place, chain, gate, vectors, pair, after
    )


def finish_kernel(which, place_ref, valid_ref, out_gain_ref, gates_ref, product_ref, out_weight_ref, *rest):
    then = which == 0
    if then:
        vectors_ref, weight_ref, out_ref, both_ref, hidden_s, both_s = rest
        new_s = out_ref
        columns = spread_columns(place_ref, valid_ref)
        weights = [weight_of(weight_ref, 1, start) for start in (0, 2 * HIDDEN)]

        def mask_at(first, count, shift):
            return mask_of(first, count, place_ref, valid_ref, columns, shift)

    else:
        out_ref, hidden_s, new_s, out_sem = rest

    def channel(n):
        return product_ref[n].astype(jnp.float32)

    average = channel(0)
    for n in range(1, HIDDEN):
        average = average + channel(n)
    average = average / HIDDEN
    spread = jnp.zeros_like(average)
    for n in range(HIDDEN):
        centred = channel(n) - average
        spread = spread + centred * centred
    scale = lax.rsqrt(spread / HIDDEN + EPS)
    for n in range(HIDDEN):
        hidden = (channel(n) - average) * scale * out_gain_ref[which, n]
        for part in range(DEPTH // SUB):
            place = pl.ds(n * STRIDE + part * SUB, SUB)
            hidden_s[place, :] = hidden[:, part * LANES : (part + 1) * LANES]

    def work(first, count):
        size = count * COLUMNS
        hidden = jnp.concatenate(
            [hidden_s[pl.ds(first + n, HIDDEN, stride=STRIDE), :] for n in range(BATCH)], axis=1
        ).astype(jnp.bfloat16)
        branch = lax.dot_general(
            hidden,
            out_weight_ref[which],
            (((0,), (0,)), ((), ())),
            preferred_element_type=jnp.float32,
        )
        new = jnp.concatenate(
            [
                gates_ref[1, first + n, pl.ds(0, size)]
                + gates_ref[0, first + n, pl.ds(0, size)] * branch[n * LANES : n * LANES + size]
                for n in range(BATCH)
            ],
            axis=0,
        )
        places = [row for rows in block_rows(first, count) for row in rows]
        for n, row in enumerate(places):
            new_s[row] = new[n * COLUMNS : (n + 1) * COLUMNS].astype(jnp.bfloat16)
        if not then:
            for group in range(count):
                span = pl.ds(block_rows(first, count)[0][group], BATCH)
                pltpu.make_async_copy(new_s.at[span], out_ref.at[span], out_sem).start()
            return
        new = new.astype(jnp.bfloat16).astype(jnp.float32)
        normed = normalize(new, vectors_ref[1:2], vectors_ref[3:4])
        factor_rows(first, count, normed, weights, mask_at, both_s)

    batches(work)
    if then:
        put_chunks(both_s, both_ref, range(HIDDEN))
    else:
        pltpu.make_async_copy(new_s, out_ref, out_sem).wait()


def finish(which, place, valid, out_gain, gate, product, out_weight, *then):
    shape = (ROWS, COLUMNS, WIDTH)
    out = jax.ShapeDtypeStruct(shape, jnp.bfloat16)
    last = [pltpu.VMEM(shape, jnp.bfloat16), pltpu.SemaphoreType.DMA]
    return call(
        functools.partial(finish_kernel, which),
        [out, BOTH_CHUNKS] if then else [out],
        [SMEM] * 3 + [VMEM] * (3 + len(then)),
        [SCRATCH] + ([BOTH_SCRATCH] if then else last),
        outs=None if then else [ANY],
    )(place, valid, out_gain, gate, product, out_weight, *then)


LEFT = (0, 6, 0)
RIGHT = (3, 6, COLUMNS)


def gather_rows(chunks_ref, zh, block, layout):
    tile, last_tile, last_lane = layout
    start = last_tile * LANES + last_lane
    if block < 9:
        start = (tile + block % 3) * LANES + block // 3 * COLUMNS
    return jnp.concatenate(
        [
            chunks_ref[spot(span, zh)].astype(jnp.float32)[:, start : start + COLUMNS]
            for span in range(SPAN)
        ],
        axis=1,
    )


def assemble_into(chunks_ref, layout, put):
    for zh in range(ZH):
        for block in range(0, ROWS // SUB, 2):
            rows = [gather_rows(chunks_ref, zh, block + n, layout) for n in range(2)]
            put(zh * ROWS + block * SUB, jnp.concatenate(rows, axis=0))


def assemble_kernel(layout, chunks_ref, out_ref):
    def put(start, values):
        out_ref[pl.ds(start, 2 * SUB), :] = values.astype(jnp.bfloat16)

    assemble_into(chunks_ref, layout, put)


def assemble(chunks, layout):
    out = jax.ShapeDtypeStruct((ZH * ROWS, SPAN * COLUMNS), jnp.bfloat16)
    return call(functools.partial(assemble_kernel, layout), out, [VMEM])(chunks)


def assemble_turned_kernel(layout, chunks_ref, out_ref, whole):
    def put(start, values):
        whole[pl.ds(start, 2 * SUB), :] = values

    assemble_into(chunks_ref, layout, put)
    whole[pl.ds(ZH * ROWS, 64), :] = jnp.zeros((64, SPAN * COLUMNS), jnp.float32)
    for part in range(SPAN * COLUMNS // 128):
        turned = whole[:, part * 128 : (part + 1) * 128].T
        out_ref[pl.ds(part * 128, 128), :] = turned[:, : ZH * ROWS].astype(jnp.bfloat16)


def assemble_turned(chunks, layout):
    out = jax.ShapeDtypeStruct((SPAN * COLUMNS, ZH * ROWS), jnp.bfloat16)
    scratch = [pltpu.VMEM((ZH * ROWS + 64, SPAN * COLUMNS), jnp.float32)]
    kernel = functools.partial(assemble_turned_kernel, layout)
    return call(kernel, out, [VMEM], scratch)(chunks)


def chunk_of(total, zh, start):
    pieces = [
        total[pl.ds(zh * ROWS + block * SUB, SUB), :][:, start : start + COLUMNS]
        for block in range(ROWS // SUB)
    ]
    lanes = []
    for tile in range(WHOLE):
        lanes += pieces[tile:9:3] + [jnp.zeros((SUB, LANES - 3 * COLUMNS), jnp.float32)]
    lanes += [pieces[9], jnp.zeros((SUB, LANES - COLUMNS), jnp.float32)]
    return jnp.concatenate(lanes, axis=1).astype(jnp.bfloat16)


def outgoing_kernel(core_ref, left_ref, *rest):
    rights, (_, out_ref, total) = rest[:X], rest[X:]
    for n, right_ref in enumerate(rights):
        total[:, n * ZH * ROWS : (n + 1) * ZH * ROWS] = lax.dot_general(
            left_ref[...],
            right_ref[...],
            (((1,), (1,)), ((), ())),
            preferred_element_type=jnp.float32,
        )
    for half in range(2):
        slot = lax.rem(core_ref[0] + half, 2)
        for n, ahead in enumerate(ORDER):
            x = lax.rem(core_ref[1] + ahead, X)
            for low in range(ZH):
                span = ((lax.rem(x, 2) * ZH + low) * ZH) * 2 + x // 2
                for zh in range(ZH):
                    start = ((n * ZH + low) * 2 + half) * COLUMNS
                    out_ref[slot, span + zh * 2] = chunk_of(total, zh, start)


def outgoing(core, left, rights, gate):
    out = jax.ShapeDtypeStruct((2,) + CHUNKS.shape, jnp.bfloat16)
    scratch = [pltpu.VMEM((ZH * ROWS, X * ZH * ROWS), jnp.float32)]
    specs = [SMEM] + [VMEM] * (1 + X) + [ANY]
    return call(outgoing_kernel, out, specs, scratch, 6 * 10**8)(core, left, *rights, gate)


def incoming_kernel(core_ref, own_ref, other_ref, *rest):
    rights, (_, out_ref, total) = rest[:X], rest[X:]
    for n, left_ref in enumerate((own_ref, other_ref)):
        side = lax.rem(core_ref[0] + n, 2)
        product = jnp.zeros((ZH * COLUMNS, SPAN * COLUMNS), jnp.float32)
        for ahead, right_ref in zip(ORDER, rights):
            product = product + jnp.dot(
                left_ref[lax.rem(core_ref[1] + ahead, X)],
                right_ref[...],
                preferred_element_type=jnp.float32,
            )
        for zh in range(ZH):
            start = pl.multiple_of(zh * ROWS + side * COLUMNS, 8)
            total[pl.ds(start, COLUMNS), :] = product[zh * COLUMNS : (zh + 1) * COLUMNS]
    for span in range(SPAN):
        for zh in range(ZH):
            out_ref[spot(span, zh)] = chunk_of(total, zh, span * COLUMNS)


def incoming(core, own, other, rights, gate):
    scratch = [pltpu.VMEM((ZH * ROWS, SPAN * COLUMNS), jnp.float32)]
    return call(
        incoming_kernel, CHUNKS, [SMEM] + [VMEM] * (2 + X) + [ANY], scratch, 6 * 10**8
    )(core, own, other, *rights, gate)


def gather_x(block):
    def shift(ahead):
        return lax.ppermute(block, "x", [(x, (x - ahead) % X) for x in range(X)])

    return [block] + [shift(ahead) for ahead in ORDER[1:]]


def exchange(values, axes):
    return lax.all_to_all(values, axes, split_axis=0, concat_axis=0, tiled=True)


def swap_cores(values):
    return lax.ppermute(values, "core", [(0, 1), (1, 0)])


def body(
    pair_acts,
    residue_valid,
    chain_index,
    norm_gain,
    norm_bias,
    projection,
    gate_weight,
    chain_bias,
    out_gain,
    out_weight,
):
    row_start = (lax.axis_index("x") * ZH + lax.axis_index("zh")) * ROWS
    core_index = lax.axis_index("core")
    column_block = (lax.axis_index("zl") * 8 + lax.axis_index("y")) * 2 + core_index
    place = jnp.stack([row_start, column_block * COLUMNS]).astype(jnp.int32)
    core = jnp.stack([core_index, lax.axis_index("x")]).astype(jnp.int32)

    vectors = jnp.concatenate([norm_gain, norm_bias, chain_bias], axis=0)
    both = project(place, residue_valid, pair_acts, norm_gain, norm_bias, projection)
    both = exchange(both, PLANE)
    rights = gather_x(assemble(both, RIGHT))
    left = assemble(both, LEFT)
    gate = gates(0, place, chain_index, gate_weight, vectors, pair_acts, left)
    halves = outgoing(core, left, rights, gate)
    total = halves[0].astype(jnp.float32) + swap_cores(halves[1]).astype(jnp.float32)
    product = exchange(total.astype(jnp.bfloat16), PLANE)
    middle, both = finish(
        0, place, residue_valid, out_gain, gate, product, out_weight, vectors, projection
    )
    both = exchange(both, PLANE)
    rights = gather_x(assemble(both, RIGHT))
    left = assemble_turned(both, LEFT).reshape(X, ZH * COLUMNS, ZH * ROWS)
    gate = gates(1, place, chain_index, gate_weight, vectors, middle, left)
    left = exchange(left, "x")
    product = exchange(incoming(core, left, swap_cores(left), rights, gate), PLANE)
    return finish(1, place, residue_valid, out_gain, gate, product, out_weight)[0]


def solution(mesh):
    fine = Mesh(mesh.devices.reshape(SIZES), AXES)
    pairs = P(("x", "zh"), ("zl", "y", "core"), None)
    placed = (pairs, P(), P(), P(), P(), P(), P(), P(), P(), P())
    return jax.shard_map(body, mesh=fine, in_specs=placed, out_specs=pairs, check_vma=False)
```

```python
import functools

import jax
import jax.numpy as jnp
from jax import lax
from jax.experimental import pallas as pl
from jax.experimental.pallas import tpu as pltpu
from jax.sharding import Mesh
from jax.sharding import PartitionSpec as P

AXES = ("zl", "y", "core", "x", "zh")
SIZES = (2, 8, 2, 4, 4)
PLANE = ("y", "zh", "zl")
ROWS = 80
COLUMNS = 40
WIDTH = 128
HIDDEN = 64
X = 4
ZH = 4
SPAN = 16
EPS = 1e-05
DEPTH = 32
LANES = 128
SUB = 8
WHOLE = 3
TAIL = 8 * 9
ORDER = (0, 2, 1, 3)
STRIDE = 40
BOTH = 56
BATCH = 8
CHUNKS = jax.ShapeDtypeStruct((HIDDEN, SUB, DEPTH // SUB * LANES), jnp.bfloat16)
BOTH_CHUNKS = jax.ShapeDtypeStruct((HIDDEN, SUB, BOTH // SUB * LANES), jnp.bfloat16)
GATES = jax.ShapeDtypeStruct((2, DEPTH, LANES, WIDTH), jnp.float32)
VMEM = pl.BlockSpec(memory_space=pltpu.VMEM)
ANY = pl.BlockSpec(memory_space=pl.ANY)
SMEM = pl.BlockSpec(memory_space=pltpu.SMEM)


def spot(span, zh):
    zl, y = divmod(span, 8)
    return (y * ZH + zh) * 2 + zl


def call(kernel, out_shape, in_specs, scratch_shapes=(), flops=10**8, outs=None, grant=40):
    outs = outs or jax.tree.map(lambda _: VMEM, out_shape)
    moved = 4 * 10**6
    return pl.pallas_call(
        kernel,
        out_shape=out_shape,
        in_specs=in_specs,
        out_specs=outs,
        scratch_shapes=scratch_shapes,
        compiler_params=pltpu.CompilerParams(vmem_limit_bytes=grant * 2**20),
        cost_estimate=pl.CostEstimate(flops=flops, bytes_accessed=moved, transcendentals=0),
    )


def normalize(values, gain, bias):
    average = jnp.mean(values, axis=-1, keepdims=True)
    centred = values - average
    spread = jnp.mean(centred * centred, axis=-1, keepdims=True)
    return centred * lax.rsqrt(spread + EPS) * gain + bias


def batches(work):
    for step in range(WHOLE):
        work(step * BATCH, 3)
    work(WHOLE * BATCH, 1)


def block_rows(first, count):
    if count == 1:
        return [[TAIL + n] for n in range(BATCH)]
    return [[first + n + WHOLE * SUB * group for group in range(count)] for n in range(BATCH)]


def load_pairs(pair_ref, first, count):
    rows = [row for rows in block_rows(first, count) for row in rows]
    return jnp.concatenate([pair_ref[row].astype(jnp.float32) for row in rows], axis=0)


def pad_rows(values, count):
    size = count * COLUMNS
    empty = jnp.zeros((LANES - size, WIDTH), jnp.float32)
    return [
        jnp.concatenate([values[n * size : (n + 1) * size], empty], axis=0).astype(jnp.bfloat16)
        for n in range(BATCH)
    ]


def spread_columns(place_ref, valid_ref):
    lane = lax.broadcasted_iota(jnp.int32, (1, LANES), 1)
    inside = lane % COLUMNS
    found = jnp.zeros((1, LANES), jnp.float32)
    for column in range(COLUMNS):
        value = valid_ref[place_ref[1] + column].astype(jnp.float32)
        found = jnp.where(inside == column, value, found)
    return jnp.where(lane < 3 * COLUMNS, found, 0.0)


def mask_of(first, count, place_ref, valid_ref, columns, shift=0):
    lane = lax.broadcasted_iota(jnp.int32, (1, LANES), 1)
    masks = []
    for rows in block_rows(first, count):
        mask = jnp.zeros((1, LANES), jnp.float32)
        for group, row in enumerate(rows):
            value = valid_ref[place_ref[0] + row].astype(jnp.float32)
            start = (group + shift) * COLUMNS
            inside = (lane >= start) & (lane < start + COLUMNS)
            mask = jnp.where(inside, value, mask)
        masks.append(mask * columns)
    return jnp.concatenate(masks, axis=1)


def weight_of(weight_ref, which, start):
    columns = weight_ref[which][:, start : start + 2 * HIDDEN]
    return columns.astype(jnp.float32).T.astype(jnp.bfloat16)


def factor_of(normed, weight, mask):
    proj = lax.dot_general(
        weight, normed, (((1,), (1,)), ((), ())), preferred_element_type=jnp.float32
    )
    return jax.nn.sigmoid(proj[HIDDEN:]) * proj[:HIDDEN] * mask


def keep_rows(factor, scratch, first, stride):
    for n in range(BATCH):
        place = pl.ds(first + n, HIDDEN, stride=stride)
        scratch[place, :] = factor[:, n * LANES : (n + 1) * LANES]


def put_chunks(scratch, out_ref, channels):
    for channel in channels:
        rows = scratch[pl.ds(channel * BOTH, BOTH), :]
        tiles = [rows[n : n + SUB] for n in range(0, BOTH, SUB)]
        out_ref[channel] = jnp.concatenate(tiles, axis=1).astype(jnp.bfloat16)


def factor_rows(first, count, normed, weights, mask_at, both_s):
    left_weight, right_weight = weights
    if count == 3:
        rows = jnp.concatenate(pad_rows(normed, count), axis=0)
        mask = mask_at(first, count, 0)
        keep_rows(factor_of(rows, left_weight, mask), both_s, first, BOTH)
        keep_rows(factor_of(rows, right_weight, mask), both_s, first + WHOLE * SUB, BOTH)
        return
    pieces = []
    for n in range(BATCH):
        piece = normed[n * COLUMNS : (n + 1) * COLUMNS]
        pieces += [piece, piece, jnp.zeros((LANES - 2 * COLUMNS, WIDTH), jnp.float32)]
    rows = jnp.concatenate(pieces, axis=0).astype(jnp.bfloat16)
    factor = factor_of(rows, left_weight, mask_at(first, count, 0))
    factor = factor + factor_of(rows, right_weight, mask_at(first, count, 1))
    keep_rows(factor, both_s, 2 * WHOLE * SUB, BOTH)


SCRATCH = pltpu.VMEM(((HIDDEN + 1) * STRIDE, LANES), jnp.float32)
BOTH_SCRATCH = pltpu.VMEM(((HIDDEN + 1) * BOTH, LANES), jnp.float32)


def place_of():
    row = (lax.axis_index("x") * ZH + lax.axis_index("zh")) * ROWS
    block = (lax.axis_index("zl") * 8 + lax.axis_index("y")) * 2 + lax.axis_index("core")
    return row, block * COLUMNS


def project_kernel(
    valid_any,
    pair_any,
    gain_any,
    bias_any,
    weight_any,
    both_any,
    both_s,
    both_ref,
    valid_ref,
    pair_ref,
    gain_ref,
    bias_ref,
    weight_ref,
    sems,
    out_sem,
):
    place = place_of()
    moves = [(valid_any, valid_ref), (gain_any, gain_ref), (bias_any, bias_ref)]
    moves.append((weight_any, weight_ref))
    parts = []
    for first in range(0, DEPTH, BATCH):
        for row in block_rows(first, 3 if first < WHOLE * BATCH else 1)[0]:
            parts.append(len(moves))
            rows = pl.ds(row, BATCH)
            moves.append((pair_any.at[rows], pair_ref.at[rows]))
    copies = [pltpu.make_async_copy(a, b, sems.at[n]) for n, (a, b) in enumerate(moves)]
    for copy in copies:
        copy.start()
    for copy in copies[: parts[0]]:
        copy.wait()
    columns = spread_columns(place, valid_ref)
    weights = [weight_of(weight_ref, 0, start) for start in (0, 2 * HIDDEN)]

    def mask_at(first, count, shift):
        return mask_of(first, count, place, valid_ref, columns, shift)

    def work(first, count):
        for part in parts[first // BATCH * 3 :][:count]:
            copies[part].wait()
        values = load_pairs(pair_ref, first, count)
        normed = normalize(values, gain_ref[0:1], bias_ref[0:1])
        factor_rows(first, count, normed, weights, mask_at, both_s)

    batches(work)
    for part in range(0, HIDDEN, 16):
        put_chunks(both_s, both_ref, range(part, part + 16))
        span = pl.ds(part, 16)
        pltpu.make_async_copy(both_ref.at[span], both_any.at[span], out_sem).start()
    pltpu.make_async_copy(both_ref, both_any, out_sem).wait()


def project(valid, *operands):
    scratch = [pltpu.VMEM(each.shape, each.dtype) for each in (BOTH_CHUNKS,) + operands]
    scratch.insert(1, pltpu.SMEM(valid.shape, valid.dtype))
    sems = [pltpu.SemaphoreType.DMA((14,)), pltpu.SemaphoreType.DMA]
    return call(
        project_kernel,
        BOTH_CHUNKS,
        [ANY] * 5,
        [BOTH_SCRATCH] + scratch + sems,
        outs=ANY,
        grant=60,
    )(valid, *operands)


def gate_kernel(which, place_ref, chain_ref, gate_ref, vectors_ref, pair_ref, _, out_ref):
    row = lax.broadcasted_iota(jnp.int32, (COLUMNS, WIDTH), 0)
    chain_columns = jnp.full((COLUMNS, WIDTH), -1, jnp.int32)
    for column in range(COLUMNS):
        chain_columns = jnp.where(row == column, chain_ref[place_ref[1] + column], chain_columns)
    gain, bias, offset = [vectors_ref[n + which : n + which + 1] for n in (0, 2, 4)]

    def work(first, count):
        values = load_pairs(pair_ref, first, count)
        pieces = pad_rows(normalize(values, gain, bias), count)
        logit = jnp.dot(
            jnp.concatenate(pieces, axis=0), gate_ref[which], preferred_element_type=jnp.float32
        )
        for n, rows in enumerate(block_rows(first, count)):
            for group, row in enumerate(rows):
                same = chain_columns == chain_ref[place_ref[0] + row]
                start = n * LANES + group * COLUMNS
                place = pl.ds(group * COLUMNS, COLUMNS)
                out_ref[0, first + n, place] = jax.nn.sigmoid(
                    logit[start : start + COLUMNS] + jnp.where(same, offset, 0.0)
                )
                old = (n * count + group) * COLUMNS
                out_ref[1, first + n, place] = values[old : old + COLUMNS]

    batches(work)


def gates(which, place, chain, gate, vectors, pair, after):
    kernel = functools.partial(gate_kernel, which)
    return call(kernel, GATES, [SMEM, SMEM, VMEM, VMEM, VMEM, ANY])(
        place, chain, gate, vectors, pair, after
    )


def finish_kernel(which, place_ref, valid_ref, out_gain_ref, gates_ref, product_ref, out_weight_ref, *rest):
    then = which == 0
    if then:
        vectors_ref, weight_ref, out_ref, both_ref, hidden_s, both_s = rest
        new_s = out_ref
        columns = spread_columns(place_ref, valid_ref)
        weights = [weight_of(weight_ref, 1, start) for start in (0, 2 * HIDDEN)]

        def mask_at(first, count, shift):
            return mask_of(first, count, place_ref, valid_ref, columns, shift)

    else:
        out_ref, hidden_s, new_s, out_sem = rest

    def channel(n):
        return product_ref[n].astype(jnp.float32)

    average = channel(0)
    for n in range(1, HIDDEN):
        average = average + channel(n)
    average = average / HIDDEN
    spread = jnp.zeros_like(average)
    for n in range(HIDDEN):
        centred = channel(n) - average
        spread = spread + centred * centred
    scale = lax.rsqrt(spread / HIDDEN + EPS)
    for n in range(HIDDEN):
        hidden = (channel(n) - average) * scale * out_gain_ref[which, n]
        for part in range(DEPTH // SUB):
            place = pl.ds(n * STRIDE + part * SUB, SUB)
            hidden_s[place, :] = hidden[:, part * LANES : (part + 1) * LANES]

    def work(first, count):
        size = count * COLUMNS
        hidden = jnp.concatenate(
            [hidden_s[pl.ds(first + n, HIDDEN, stride=STRIDE), :] for n in range(BATCH)], axis=1
        ).astype(jnp.bfloat16)
        branch = lax.dot_general(
            hidden,
            out_weight_ref[which],
            (((0,), (0,)), ((), ())),
            preferred_element_type=jnp.float32,
        )
        new = jnp.concatenate(
            [
                gates_ref[1, first + n, pl.ds(0, size)]
                + gates_ref[0, first + n, pl.ds(0, size)] * branch[n * LANES : n * LANES + size]
                for n in range(BATCH)
            ],
            axis=0,
        )
        places = [row for rows in block_rows(first, count) for row in rows]
        for n, row in enumerate(places):
            new_s[row] = new[n * COLUMNS : (n + 1) * COLUMNS].astype(jnp.bfloat16)
        if not then:
            for group in range(count):
                span = pl.ds(block_rows(first, count)[0][group], BATCH)
                pltpu.make_async_copy(new_s.at[span], out_ref.at[span], out_sem).start()
            return
        new = new.astype(jnp.bfloat16).astype(jnp.float32)
        normed = normalize(new, vectors_ref[1:2], vectors_ref[3:4])
        factor_rows(first, count, normed, weights, mask_at, both_s)

    batches(work)
    if then:
        put_chunks(both_s, both_ref, range(HIDDEN))
    else:
        pltpu.make_async_copy(new_s, out_ref, out_sem).wait()


def finish(which, place, valid, out_gain, gate, product, out_weight, *then):
    shape = (ROWS, COLUMNS, WIDTH)
    out = jax.ShapeDtypeStruct(shape, jnp.bfloat16)
    last = [pltpu.VMEM(shape, jnp.bfloat16), pltpu.SemaphoreType.DMA]
    return call(
        functools.partial(finish_kernel, which),
        [out, BOTH_CHUNKS] if then else [out],
        [SMEM] * 3 + [VMEM] * (3 + len(then)),
        [SCRATCH] + ([BOTH_SCRATCH] if then else last),
        outs=None if then else [ANY],
    )(place, valid, out_gain, gate, product, out_weight, *then)


LEFT = (0, 6, 0)
RIGHT = (3, 6, COLUMNS)


def gather_rows(chunks_ref, zh, block, layout):
    tile, last_tile, last_lane = layout
    start = last_tile * LANES + last_lane
    if block < 9:
        start = (tile + block % 3) * LANES + block // 3 * COLUMNS
    return jnp.concatenate(
        [
            chunks_ref[spot(span, zh)].astype(jnp.float32)[:, start : start + COLUMNS]
            for span in range(SPAN)
        ],
        axis=1,
    )


def assemble_into(chunks_ref, layout, put):
    for zh in range(ZH):
        for block in range(0, ROWS // SUB, 2):
            rows = [gather_rows(chunks_ref, zh, block + n, layout) for n in range(2)]
            put(zh * ROWS + block * SUB, jnp.concatenate(rows, axis=0))


def assemble_kernel(layout, chunks_ref, out_ref):
    def put(start, values):
        out_ref[pl.ds(start, 2 * SUB), :] = values.astype(jnp.bfloat16)

    assemble_into(chunks_ref, layout, put)


def assemble(chunks, layout):
    out = jax.ShapeDtypeStruct((ZH * ROWS, SPAN * COLUMNS), jnp.bfloat16)
    return call(functools.partial(assemble_kernel, layout), out, [VMEM])(chunks)


def assemble_turned_kernel(layout, chunks_ref, out_ref, whole):
    def put(start, values):
        whole[pl.ds(start, 2 * SUB), :] = values

    assemble_into(chunks_ref, layout, put)
    whole[pl.ds(ZH * ROWS, 64), :] = jnp.zeros((64, SPAN * COLUMNS), jnp.float32)
    for part in range(SPAN * COLUMNS // 128):
        turned = whole[:, part * 128 : (part + 1) * 128].T
        out_ref[pl.ds(part * 128, 128), :] = turned[:, : ZH * ROWS].astype(jnp.bfloat16)


def assemble_turned(chunks, layout):
    out = jax.ShapeDtypeStruct((SPAN * COLUMNS, ZH * ROWS), jnp.bfloat16)
    scratch = [pltpu.VMEM((ZH * ROWS + 64, SPAN * COLUMNS), jnp.float32)]
    kernel = functools.partial(assemble_turned_kernel, layout)
    return call(kernel, out, [VMEM], scratch)(chunks)


def chunk_of(total, zh, start):
    pieces = [
        total[pl.ds(zh * ROWS + block * SUB, SUB), :][:, start : start + COLUMNS]
        for block in range(ROWS // SUB)
    ]
    lanes = []
    for tile in range(WHOLE):
        lanes += pieces[tile:9:3] + [jnp.zeros((SUB, LANES - 3 * COLUMNS), jnp.float32)]
    lanes += [pieces[9], jnp.zeros((SUB, LANES - COLUMNS), jnp.float32)]
    return jnp.concatenate(lanes, axis=1).astype(jnp.bfloat16)


def outgoing_kernel(core_ref, left_ref, *rest):
    rights, (_, out_ref, total) = rest[:X], rest[X:]
    for n, right_ref in enumerate(rights):
        total[:, n * ZH * ROWS : (n + 1) * ZH * ROWS] = lax.dot_general(
            left_ref[...],
            right_ref[...],
            (((1,), (1,)), ((), ())),
            preferred_element_type=jnp.float32,
        )
    for half in range(2):
        slot = lax.rem(core_ref[0] + half, 2)
        for n, ahead in enumerate(ORDER):
            x = lax.rem(core_ref[1] + ahead, X)
            for low in range(ZH):
                span = ((lax.rem(x, 2) * ZH + low) * ZH) * 2 + x // 2
                for zh in range(ZH):
                    start = ((n * ZH + low) * 2 + half) * COLUMNS
                    out_ref[slot, span + zh * 2] = chunk_of(total, zh, start)


def outgoing(core, left, rights, gate):
    out = jax.ShapeDtypeStruct((2,) + CHUNKS.shape, jnp.bfloat16)
    scratch = [pltpu.VMEM((ZH * ROWS, X * ZH * ROWS), jnp.float32)]
    specs = [SMEM] + [VMEM] * (1 + X) + [ANY]
    return call(outgoing_kernel, out, specs, scratch, 6 * 10**8)(core, left, *rights, gate)


def incoming_kernel(core_ref, own_ref, other_ref, *rest):
    rights, (_, out_ref, total) = rest[:X], rest[X:]
    for n, left_ref in enumerate((own_ref, other_ref)):
        side = lax.rem(core_ref[0] + n, 2)
        product = jnp.zeros((ZH * COLUMNS, SPAN * COLUMNS), jnp.float32)
        for ahead, right_ref in zip(ORDER, rights):
            product = product + jnp.dot(
                left_ref[lax.rem(core_ref[1] + ahead, X)],
                right_ref[...],
                preferred_element_type=jnp.float32,
            )
        for zh in range(ZH):
            start = pl.multiple_of(zh * ROWS + side * COLUMNS, 8)
            total[pl.ds(start, COLUMNS), :] = product[zh * COLUMNS : (zh + 1) * COLUMNS]
    for span in range(SPAN):
        for zh in range(ZH):
            out_ref[spot(span, zh)] = chunk_of(total, zh, span * COLUMNS)


def incoming(core, own, other, rights, gate):
    scratch = [pltpu.VMEM((ZH * ROWS, SPAN * COLUMNS), jnp.float32)]
    return call(
        incoming_kernel, CHUNKS, [SMEM] + [VMEM] * (2 + X) + [ANY], scratch, 6 * 10**8
    )(core, own, other, *rights, gate)


def gather_x(block):
    def shift(ahead):
        return lax.ppermute(block, "x", [(x, (x - ahead) % X) for x in range(X)])

    return [block] + [shift(ahead) for ahead in ORDER[1:]]


def exchange(values, axes):
    return lax.all_to_all(values, axes, split_axis=0, concat_axis=0, tiled=True)


def swap_cores(values):
    return lax.ppermute(values, "core", [(0, 1), (1, 0)])


def body(
    pair_acts,
    residue_valid,
    chain_index,
    norm_gain,
    norm_bias,
    projection,
    gate_weight,
    chain_bias,
    out_gain,
    out_weight,
):
    place = jnp.stack(place_of()).astype(jnp.int32)
    core = jnp.stack([lax.axis_index("core"), lax.axis_index("x")]).astype(jnp.int32)

    vectors = jnp.concatenate([norm_gain, norm_bias, chain_bias], axis=0)
    both = project(residue_valid, pair_acts, norm_gain, norm_bias, projection)
    both = exchange(both, PLANE)
    rights = gather_x(assemble(both, RIGHT))
    left = assemble(both, LEFT)
    gate = gates(0, place, chain_index, gate_weight, vectors, pair_acts, left)
    halves = outgoing(core, left, rights, gate)
    total = halves[0].astype(jnp.float32) + swap_cores(halves[1]).astype(jnp.float32)
    product = exchange(total.astype(jnp.bfloat16), PLANE)
    middle, both = finish(
        0, place, residue_valid, out_gain, gate, product, out_weight, vectors, projection
    )
    both = exchange(both, PLANE)
    rights = gather_x(assemble(both, RIGHT))
    left = assemble_turned(both, LEFT).reshape(X, ZH * COLUMNS, ZH * ROWS)
    gate = gates(1, place, chain_index, gate_weight, vectors, middle, left)
    left = exchange(left, "x")
    product = exchange(incoming(core, left, swap_cores(left), rights, gate), PLANE)
    return finish(1, place, residue_valid, out_gain, gate, product, out_weight)[0]


def solution(mesh):
    fine = Mesh(mesh.devices.reshape(SIZES), AXES)
    pairs = P(("x", "zh"), ("zl", "y", "core"), None)
    placed = (pairs, P(), P(), P(), P(), P(), P(), P(), P(), P())
    return jax.shard_map(body, mesh=fine, in_specs=placed, out_specs=pairs, check_vma=False)
```

```python
import functools

import jax
import jax.numpy as jnp
from jax import lax
from jax.experimental import pallas as pl
from jax.experimental.pallas import tpu as pltpu
from jax.sharding import Mesh
from jax.sharding import PartitionSpec as P

AXES = ("zl", "y", "core", "x", "zh")
SIZES = (2, 8, 2, 4, 4)
PLANE = ("y", "zh", "zl")
ROWS = 80
COLUMNS = 40
WIDTH = 128
HIDDEN = 64
X = 4
ZH = 4
SPAN = 16
EPS = 1e-05
DEPTH = 32
LANES = 128
SUB = 8
WHOLE = 3
TAIL = 8 * 9
ORDER = (0, 2, 1, 3)
HALF = 32
STRIDE = 40
BOTH = 56
BATCH = 8
CHUNKS = jax.ShapeDtypeStruct((HIDDEN, SUB, DEPTH // SUB * LANES), jnp.bfloat16)
BOTH_CHUNKS = jax.ShapeDtypeStruct((HIDDEN, SUB, BOTH // SUB * LANES), jnp.bfloat16)
GATES = jax.ShapeDtypeStruct((2, DEPTH, LANES, WIDTH), jnp.float32)
VMEM = pl.BlockSpec(memory_space=pltpu.VMEM)
ANY = pl.BlockSpec(memory_space=pl.ANY)
SMEM = pl.BlockSpec(memory_space=pltpu.SMEM)


def spot(span, zh):
    zl, y = divmod(span, 8)
    return (y * ZH + zh) * 2 + zl


def call(kernel, out_shape, in_specs, scratch_shapes=(), flops=10**8, outs=None, grant=40):
    outs = outs or jax.tree.map(lambda _: VMEM, out_shape)
    moved = 4 * 10**6
    return pl.pallas_call(
        kernel,
        out_shape=out_shape,
        in_specs=in_specs,
        out_specs=outs,
        scratch_shapes=scratch_shapes,
        compiler_params=pltpu.CompilerParams(vmem_limit_bytes=grant * 2**20),
        cost_estimate=pl.CostEstimate(flops=flops, bytes_accessed=moved, transcendentals=0),
    )


def normalize(values, gain, bias):
    average = jnp.mean(values, axis=-1, keepdims=True)
    centred = values - average
    spread = jnp.mean(centred * centred, axis=-1, keepdims=True)
    return centred * lax.rsqrt(spread + EPS) * gain + bias


def batches(work):
    for step in range(WHOLE):
        work(step * BATCH, 3)
    work(WHOLE * BATCH, 1)


def block_rows(first, count):
    if count == 1:
        return [[TAIL + n] for n in range(BATCH)]
    return [[first + n + WHOLE * SUB * group for group in range(count)] for n in range(BATCH)]


def load_pairs(pair_ref, first, count):
    rows = [row for rows in block_rows(first, count) for row in rows]
    return jnp.concatenate([pair_ref[row].astype(jnp.float32) for row in rows], axis=0)


def pad_rows(values, count):
    size = count * COLUMNS
    empty = jnp.zeros((LANES - size, WIDTH), jnp.float32)
    return [
        jnp.concatenate([values[n * size : (n + 1) * size], empty], axis=0).astype(jnp.bfloat16)
        for n in range(BATCH)
    ]


def spread_columns(place_ref, valid_ref):
    lane = lax.broadcasted_iota(jnp.int32, (1, LANES), 1)
    inside = lane % COLUMNS
    found = jnp.zeros((1, LANES), jnp.float32)
    for column in range(COLUMNS):
        value = valid_ref[place_ref[1] + column].astype(jnp.float32)
        found = jnp.where(inside == column, value, found)
    return jnp.where(lane < 3 * COLUMNS, found, 0.0)


def mask_of(first, count, place_ref, valid_ref, columns, shift=0):
    lane = lax.broadcasted_iota(jnp.int32, (1, LANES), 1)
    masks = []
    for rows in block_rows(first, count):
        mask = jnp.zeros((1, LANES), jnp.float32)
        for group, row in enumerate(rows):
            value = valid_ref[place_ref[0] + row].astype(jnp.float32)
            start = (group + shift) * COLUMNS
            inside = (lane >= start) & (lane < start + COLUMNS)
            mask = jnp.where(inside, value, mask)
        masks.append(mask * columns)
    return jnp.concatenate(masks, axis=1)


def weight_of(weight_ref, which, start):
    columns = weight_ref[which][:, start : start + 2 * HIDDEN]
    return columns.astype(jnp.float32).T.astype(jnp.bfloat16)


def factor_of(normed, weight, mask):
    proj = lax.dot_general(
        weight, normed, (((1,), (1,)), ((), ())), preferred_element_type=jnp.float32
    )
    return jax.nn.sigmoid(proj[HIDDEN:]) * proj[:HIDDEN] * mask


def keep_rows(factor, scratch, first, stride):
    for n in range(BATCH):
        place = pl.ds(first + n, HIDDEN, stride=stride)
        scratch[place, :] = factor[:, n * LANES : (n + 1) * LANES]


def put_chunks(scratch, out_ref, channels):
    for channel in channels:
        rows = scratch[pl.ds(channel * BOTH, BOTH), :]
        tiles = [rows[n : n + SUB] for n in range(0, BOTH, SUB)]
        out_ref[channel] = jnp.concatenate(tiles, axis=1).astype(jnp.bfloat16)


def factor_rows(first, count, normed, weights, mask_at, both_s):
    left_weight, right_weight = weights
    if count == 3:
        rows = jnp.concatenate(pad_rows(normed, count), axis=0)
        mask = mask_at(first, count, 0)
        keep_rows(factor_of(rows, left_weight, mask), both_s, first, BOTH)
        keep_rows(factor_of(rows, right_weight, mask), both_s, first + WHOLE * SUB, BOTH)
        return
    pieces = []
    for n in range(BATCH):
        piece = normed[n * COLUMNS : (n + 1) * COLUMNS]
        pieces += [piece, piece, jnp.zeros((LANES - 2 * COLUMNS, WIDTH), jnp.float32)]
    rows = jnp.concatenate(pieces, axis=0).astype(jnp.bfloat16)
    factor = factor_of(rows, left_weight, mask_at(first, count, 0))
    factor = factor + factor_of(rows, right_weight, mask_at(first, count, 1))
    keep_rows(factor, both_s, 2 * WHOLE * SUB, BOTH)


SCRATCH = pltpu.VMEM(((HIDDEN + 1) * STRIDE, LANES), jnp.float32)
BOTH_SCRATCH = pltpu.VMEM(((HIDDEN + 1) * BOTH, LANES), jnp.float32)


def place_of():
    row = (lax.axis_index("x") * ZH + lax.axis_index("zh")) * ROWS
    block = (lax.axis_index("zl") * 8 + lax.axis_index("y")) * 2 + lax.axis_index("core")
    return row, block * COLUMNS


def project_kernel(
    valid_any,
    pair_any,
    gain_any,
    bias_any,
    weight_any,
    both_any,
    both_s,
    both_ref,
    valid_ref,
    pair_ref,
    gain_ref,
    bias_ref,
    weight_ref,
    sems,
    out_sem,
):
    place = place_of()
    moves = [(valid_any, valid_ref), (gain_any, gain_ref), (bias_any, bias_ref)]
    moves.append((weight_any, weight_ref))
    parts = []
    for first in range(0, DEPTH, BATCH):
        for row in block_rows(first, 3 if first < WHOLE * BATCH else 1)[0]:
            parts.append(len(moves))
            rows = pl.ds(row, BATCH)
            moves.append((pair_any.at[rows], pair_ref.at[rows]))
    copies = [pltpu.make_async_copy(a, b, sems.at[n]) for n, (a, b) in enumerate(moves)]
    for copy in copies:
        copy.start()
    for copy in copies[: parts[0]]:
        copy.wait()
    columns = spread_columns(place, valid_ref)
    weights = [weight_of(weight_ref, 0, start) for start in (0, 2 * HIDDEN)]

    def mask_at(first, count, shift):
        return mask_of(first, count, place, valid_ref, columns, shift)

    def work(first, count):
        for part in parts[first // BATCH * 3 :][:count]:
            copies[part].wait()
        values = load_pairs(pair_ref, first, count)
        normed = normalize(values, gain_ref[0:1], bias_ref[0:1])
        factor_rows(first, count, normed, weights, mask_at, both_s)

    batches(work)
    for part in range(0, HIDDEN, 16):
        put_chunks(both_s, both_ref, range(part, part + 16))
        span = pl.ds(part, 16)
        pltpu.make_async_copy(both_ref.at[span], both_any.at[span], out_sem).start()
    pltpu.make_async_copy(both_ref, both_any, out_sem).wait()


def project(valid, *operands):
    scratch = [pltpu.VMEM(each.shape, each.dtype) for each in (BOTH_CHUNKS,) + operands]
    scratch.insert(1, pltpu.SMEM(valid.shape, valid.dtype))
    sems = [pltpu.SemaphoreType.DMA((14,)), pltpu.SemaphoreType.DMA]
    return call(
        project_kernel,
        BOTH_CHUNKS,
        [ANY] * 5,
        [BOTH_SCRATCH] + scratch + sems,
        outs=ANY,
        grant=60,
    )(valid, *operands)


def gate_kernel(which, place_ref, chain_ref, gate_ref, vectors_ref, pair_ref, _, out_ref):
    row = lax.broadcasted_iota(jnp.int32, (COLUMNS, WIDTH), 0)
    chain_columns = jnp.full((COLUMNS, WIDTH), -1, jnp.int32)
    for column in range(COLUMNS):
        chain_columns = jnp.where(row == column, chain_ref[place_ref[1] + column], chain_columns)
    gain, bias, offset = [vectors_ref[n + which : n + which + 1] for n in (0, 2, 4)]

    def work(first, count):
        values = load_pairs(pair_ref, first, count)
        pieces = pad_rows(normalize(values, gain, bias), count)
        logit = jnp.dot(
            jnp.concatenate(pieces, axis=0), gate_ref[which], preferred_element_type=jnp.float32
        )
        for n, rows in enumerate(block_rows(first, count)):
            for group, row in enumerate(rows):
                same = chain_columns == chain_ref[place_ref[0] + row]
                start = n * LANES + group * COLUMNS
                place = pl.ds(group * COLUMNS, COLUMNS)
                out_ref[0, first + n, place] = jax.nn.sigmoid(
                    logit[start : start + COLUMNS] + jnp.where(same, offset, 0.0)
                )
                old = (n * count + group) * COLUMNS
                out_ref[1, first + n, place] = values[old : old + COLUMNS]

    batches(work)


def gates(which, place, chain, gate, vectors, pair, after):
    kernel = functools.partial(gate_kernel, which)
    return call(kernel, GATES, [SMEM, SMEM, VMEM, VMEM, VMEM, ANY])(
        place, chain, gate, vectors, pair, after
    )


def finish_kernel(which, place_ref, valid_ref, out_gain_ref, gates_ref, product_ref, out_weight_ref, *rest):
    then = which == 0
    if then:
        vectors_ref, weight_ref, out_ref, both_ref, hidden_s, both_s = rest
        new_s = out_ref
        columns = spread_columns(place_ref, valid_ref)
        weights = [weight_of(weight_ref, 1, start) for start in (0, 2 * HIDDEN)]

        def mask_at(first, count, shift):
            return mask_of(first, count, place_ref, valid_ref, columns, shift)

    else:
        out_ref, hidden_s, new_s, out_sem = rest

    def channel(n):
        return product_ref[n].astype(jnp.float32)

    average = channel(0)
    for n in range(1, HIDDEN):
        average = average + channel(n)
    average = average / HIDDEN
    spread = jnp.zeros_like(average)
    for n in range(HIDDEN):
        centred = channel(n) - average
        spread = spread + centred * centred
    scale = lax.rsqrt(spread / HIDDEN + EPS)
    for n in range(HIDDEN):
        hidden = (channel(n) - average) * scale * out_gain_ref[which, n]
        for part in range(DEPTH // SUB):
            place = pl.ds(n * STRIDE + part * SUB, SUB)
            hidden_s[place, :] = hidden[:, part * LANES : (part + 1) * LANES]

    def work(first, count):
        size = count * COLUMNS
        hidden = jnp.concatenate(
            [hidden_s[pl.ds(first + n, HIDDEN, stride=STRIDE), :] for n in range(BATCH)], axis=1
        ).astype(jnp.bfloat16)
        branch = lax.dot_general(
            hidden,
            out_weight_ref[which],
            (((0,), (0,)), ((), ())),
            preferred_element_type=jnp.float32,
        )
        new = jnp.concatenate(
            [
                gates_ref[1, first + n, pl.ds(0, size)]
                + gates_ref[0, first + n, pl.ds(0, size)] * branch[n * LANES : n * LANES + size]
                for n in range(BATCH)
            ],
            axis=0,
        )
        places = [row for rows in block_rows(first, count) for row in rows]
        for n, row in enumerate(places):
            new_s[row] = new[n * COLUMNS : (n + 1) * COLUMNS].astype(jnp.bfloat16)
        if not then:
            for group in range(count):
                span = pl.ds(block_rows(first, count)[0][group], BATCH)
                pltpu.make_async_copy(new_s.at[span], out_ref.at[span], out_sem).start()
            return
        new = new.astype(jnp.bfloat16).astype(jnp.float32)
        normed = normalize(new, vectors_ref[1:2], vectors_ref[3:4])
        factor_rows(first, count, normed, weights, mask_at, both_s)

    batches(work)
    if then:
        put_chunks(both_s, both_ref, range(HIDDEN))
    else:
        pltpu.make_async_copy(new_s, out_ref, out_sem).wait()


def finish(which, place, valid, out_gain, gate, product, out_weight, *then):
    shape = (ROWS, COLUMNS, WIDTH)
    out = jax.ShapeDtypeStruct(shape, jnp.bfloat16)
    last = [pltpu.VMEM(shape, jnp.bfloat16), pltpu.SemaphoreType.DMA]
    return call(
        functools.partial(finish_kernel, which),
        [out, BOTH_CHUNKS] if then else [out],
        [SMEM] * 3 + [VMEM] * (3 + len(then)),
        [SCRATCH] + ([BOTH_SCRATCH] if then else last),
        outs=None if then else [ANY],
    )(place, valid, out_gain, gate, product, out_weight, *then)


LEFT = (0, 6, 0)
RIGHT = (3, 6, COLUMNS)


def gather_rows(chunks_ref, zh, block, layout):
    tile, last_tile, last_lane = layout
    start = last_tile * LANES + last_lane
    if block < 9:
        start = (tile + block % 3) * LANES + block // 3 * COLUMNS
    return jnp.concatenate(
        [
            chunks_ref[spot(span, zh)].astype(jnp.float32)[:, start : start + COLUMNS]
            for span in range(SPAN)
        ],
        axis=1,
    )


def assemble_into(chunks_ref, layout, put):
    for zh in range(ZH):
        for block in range(0, ROWS // SUB, 2):
            rows = [gather_rows(chunks_ref, zh, block + n, layout) for n in range(2)]
            put(zh * ROWS + block * SUB, jnp.concatenate(rows, axis=0))


def assemble_kernel(layout, chunks_ref, out_ref):
    def put(start, values):
        out_ref[pl.ds(start, 2 * SUB), :] = values.astype(jnp.bfloat16)

    assemble_into(chunks_ref, layout, put)


def assemble(chunks, layout):
    out = jax.ShapeDtypeStruct((ZH * ROWS, SPAN * COLUMNS), jnp.bfloat16)
    return call(functools.partial(assemble_kernel, layout), out, [VMEM])(chunks)


def assemble_turned_kernel(layout, chunks_ref, out_ref, whole):
    def put(start, values):
        whole[pl.ds(start, 2 * SUB), :] = values

    assemble_into(chunks_ref, layout, put)
    whole[pl.ds(ZH * ROWS, 64), :] = jnp.zeros((64, SPAN * COLUMNS), jnp.float32)
    for part in range(SPAN * COLUMNS // 128):
        turned = whole[:, part * 128 : (part + 1) * 128].T
        out_ref[pl.ds(part * 128, 128), :] = turned[:, : ZH * ROWS].astype(jnp.bfloat16)


def assemble_turned(chunks, layout):
    out = jax.ShapeDtypeStruct((SPAN * COLUMNS, ZH * ROWS), jnp.bfloat16)
    scratch = [pltpu.VMEM((ZH * ROWS + 64, SPAN * COLUMNS), jnp.float32)]
    kernel = functools.partial(assemble_turned_kernel, layout)
    return call(kernel, out, [VMEM], scratch)(chunks)


def chunk_of(total, zh, start):
    pieces = [
        total[pl.ds(zh * ROWS + block * SUB, SUB), :][:, start : start + COLUMNS]
        for block in range(ROWS // SUB)
    ]
    lanes = []
    for tile in range(WHOLE):
        lanes += pieces[tile:9:3] + [jnp.zeros((SUB, LANES - 3 * COLUMNS), jnp.float32)]
    lanes += [pieces[9], jnp.zeros((SUB, LANES - COLUMNS), jnp.float32)]
    return jnp.concatenate(lanes, axis=1).astype(jnp.bfloat16)


def outgoing_part(core_ref, left_ref, rights, aheads, base, out_ref, total):
    for n, right_ref in enumerate(rights):
        total[:, n * ZH * ROWS : (n + 1) * ZH * ROWS] = lax.dot_general(
            left_ref[...],
            right_ref[...],
            (((1,), (1,)), ((), ())),
            preferred_element_type=jnp.float32,
        )
    for half in range(2):
        slot = lax.rem(core_ref[0] + half, 2)
        for n, ahead in enumerate(aheads):
            zl = lax.rem(core_ref[1] + ahead, X) // 2
            for low in range(ZH):
                start = ((n * ZH + low) * 2 + half) * COLUMNS
                for zh in range(ZH):
                    place = base + (low * ZH + zh) * 2 + zl
                    out_ref[slot, place] = chunk_of(total, zh, start)


def outgoing_first_kernel(core_ref, left_ref, own_ref, across_ref, out_ref, total):
    outgoing_part(core_ref, left_ref, (own_ref, across_ref), ORDER[:2], 0, out_ref, total)


def outgoing_last_kernel(core_ref, left_ref, next_ref, last_ref, first_ref, _, out_ref, total):
    parity = lax.rem(core_ref[1], 2)
    for slot in range(2):
        out_ref[slot, pl.ds(parity * HALF, HALF)] = first_ref[slot]
    base = (1 - parity) * HALF
    outgoing_part(core_ref, left_ref, (next_ref, last_ref), ORDER[2:], base, out_ref, total)


def outgoing(core, left, rights, gate):
    half = jax.ShapeDtypeStruct((2, HALF) + CHUNKS.shape[1:], jnp.bfloat16)
    out = jax.ShapeDtypeStruct((2,) + CHUNKS.shape, jnp.bfloat16)
    scratch = [pltpu.VMEM((ZH * ROWS, 2 * ZH * ROWS), jnp.float32)]
    first = call(outgoing_first_kernel, half, [SMEM] + [VMEM] * 3, scratch, 3 * 10**8)(
        core, left, *rights[:2]
    )
    return call(outgoing_last_kernel, out, [SMEM] + [VMEM] * 4 + [ANY], scratch, 3 * 10**8)(
        core, left, *rights[2:], first, gate
    )


def incoming_kernel(core_ref, own_ref, other_ref, *rest):
    rights, (_, out_ref, total) = rest[:X], rest[X:]
    for n, left_ref in enumerate((own_ref, other_ref)):
        side = lax.rem(core_ref[0] + n, 2)
        product = jnp.zeros((ZH * COLUMNS, SPAN * COLUMNS), jnp.float32)
        for ahead, right_ref in zip(ORDER, rights):
            product = product + jnp.dot(
                left_ref[lax.rem(core_ref[1] + ahead, X)],
                right_ref[...],
                preferred_element_type=jnp.float32,
            )
        for zh in range(ZH):
            start = pl.multiple_of(zh * ROWS + side * COLUMNS, 8)
            total[pl.ds(start, COLUMNS), :] = product[zh * COLUMNS : (zh + 1) * COLUMNS]
    for span in range(SPAN):
        for zh in range(ZH):
            out_ref[spot(span, zh)] = chunk_of(total, zh, span * COLUMNS)


def incoming(core, own, other, rights, gate):
    scratch = [pltpu.VMEM((ZH * ROWS, SPAN * COLUMNS), jnp.float32)]
    return call(
        incoming_kernel, CHUNKS, [SMEM] + [VMEM] * (2 + X) + [ANY], scratch, 6 * 10**8
    )(core, own, other, *rights, gate)


def gather_x(block):
    def shift(ahead):
        return lax.ppermute(block, "x", [(x, (x - ahead) % X) for x in range(X)])

    return [block] + [shift(ahead) for ahead in ORDER[1:]]


def exchange(values, axes):
    return lax.all_to_all(values, axes, split_axis=0, concat_axis=0, tiled=True)


def swap_cores(values):
    return lax.ppermute(values, "core", [(0, 1), (1, 0)])


def body(
    pair_acts,
    residue_valid,
    chain_index,
    norm_gain,
    norm_bias,
    projection,
    gate_weight,
    chain_bias,
    out_gain,
    out_weight,
):
    place = jnp.stack(place_of()).astype(jnp.int32)
    core = jnp.stack([lax.axis_index("core"), lax.axis_index("x")]).astype(jnp.int32)

    vectors = jnp.concatenate([norm_gain, norm_bias, chain_bias], axis=0)
    both = project(residue_valid, pair_acts, norm_gain, norm_bias, projection)
    both = exchange(both, PLANE)
    rights = gather_x(assemble(both, RIGHT))
    left = assemble(both, LEFT)
    gate = gates(0, place, chain_index, gate_weight, vectors, pair_acts, left)
    halves = outgoing(core, left, rights, gate)
    total = halves[0].astype(jnp.float32) + swap_cores(halves[1]).astype(jnp.float32)
    product = exchange(total.astype(jnp.bfloat16), PLANE)
    middle, both = finish(
        0, place, residue_valid, out_gain, gate, product, out_weight, vectors, projection
    )
    both = exchange(both, PLANE)
    rights = gather_x(assemble(both, RIGHT))
    left = assemble_turned(both, LEFT).reshape(X, ZH * COLUMNS, ZH * ROWS)
    gate = gates(1, place, chain_index, gate_weight, vectors, middle, left)
    left = exchange(left, "x")
    product = exchange(incoming(core, left, swap_cores(left), rights, gate), PLANE)
    return finish(1, place, residue_valid, out_gain, gate, product, out_weight)[0]


def solution(mesh):
    fine = Mesh(mesh.devices.reshape(SIZES), AXES)
    pairs = P(("x", "zh"), ("zl", "y", "core"), None)
    placed = (pairs, P(), P(), P(), P(), P(), P(), P(), P(), P())
    return jax.shard_map(body, mesh=fine, in_specs=placed, out_specs=pairs, check_vma=False)
```

```python
import functools

import jax
import jax.numpy as jnp
from jax import lax
from jax.experimental import pallas as pl
from jax.experimental.pallas import tpu as pltpu
from jax.sharding import Mesh
from jax.sharding import PartitionSpec as P

AXES = ("zl", "y", "core", "x", "zh")
SIZES = (2, 8, 2, 4, 4)
PLANE = ("y", "zh", "zl")
ROWS = 80
COLUMNS = 40
WIDTH = 128
HIDDEN = 64
X = 4
ZH = 4
SPAN = 16
EPS = 1e-05
DEPTH = 32
LANES = 128
SUB = 8
WHOLE = 3
TAIL = 8 * 9
ORDER = (0, 2, 1, 3)
HALF = 32
STRIDE = 40
BOTH = 56
BATCH = 8
CHUNKS = jax.ShapeDtypeStruct((HIDDEN, SUB, DEPTH // SUB * LANES), jnp.bfloat16)
BOTH_CHUNKS = jax.ShapeDtypeStruct((HIDDEN, SUB, BOTH // SUB * LANES), jnp.bfloat16)
GATES = jax.ShapeDtypeStruct((2, DEPTH, LANES, WIDTH), jnp.float32)
VMEM = pl.BlockSpec(memory_space=pltpu.VMEM)
ANY = pl.BlockSpec(memory_space=pl.ANY)
SMEM = pl.BlockSpec(memory_space=pltpu.SMEM)


def spot(span, zh):
    zl, y = divmod(span, 8)
    return (y * ZH + zh) * 2 + zl


def call(kernel, out_shape, in_specs, scratch_shapes=(), flops=10**8, outs=None, grant=40):
    outs = outs or jax.tree.map(lambda _: VMEM, out_shape)
    moved = 4 * 10**6
    return pl.pallas_call(
        kernel,
        out_shape=out_shape,
        in_specs=in_specs,
        out_specs=outs,
        scratch_shapes=scratch_shapes,
        compiler_params=pltpu.CompilerParams(vmem_limit_bytes=grant * 2**20),
        cost_estimate=pl.CostEstimate(flops=flops, bytes_accessed=moved, transcendentals=0),
    )


def normalize(values, gain, bias):
    average = jnp.mean(values, axis=-1, keepdims=True)
    centred = values - average
    spread = jnp.mean(centred * centred, axis=-1, keepdims=True)
    return centred * lax.rsqrt(spread + EPS) * gain + bias


def batches(work):
    for step in range(WHOLE):
        work(step * BATCH, 3)
    work(WHOLE * BATCH, 1)


def block_rows(first, count):
    if count == 1:
        return [[TAIL + n] for n in range(BATCH)]
    return [[first + n + WHOLE * SUB * group for group in range(count)] for n in range(BATCH)]


def load_pairs(pair_ref, first, count):
    rows = [row for rows in block_rows(first, count) for row in rows]
    return jnp.concatenate([pair_ref[row].astype(jnp.float32) for row in rows], axis=0)


def pad_rows(values, count):
    size = count * COLUMNS
    empty = jnp.zeros((LANES - size, WIDTH), jnp.float32)
    return [
        jnp.concatenate([values[n * size : (n + 1) * size], empty], axis=0).astype(jnp.bfloat16)
        for n in range(BATCH)
    ]


def spread_columns(place_ref, valid_ref):
    lane = lax.broadcasted_iota(jnp.int32, (1, LANES), 1)
    inside = lane % COLUMNS
    found = jnp.zeros((1, LANES), jnp.float32)
    for column in range(COLUMNS):
        value = valid_ref[place_ref[1] + column].astype(jnp.float32)
        found = jnp.where(inside == column, value, found)
    return jnp.where(lane < 3 * COLUMNS, found, 0.0)


def mask_of(first, count, place_ref, valid_ref, columns, shift=0):
    lane = lax.broadcasted_iota(jnp.int32, (1, LANES), 1)
    masks = []
    for rows in block_rows(first, count):
        mask = jnp.zeros((1, LANES), jnp.float32)
        for group, row in enumerate(rows):
            value = valid_ref[place_ref[0] + row].astype(jnp.float32)
            start = (group + shift) * COLUMNS
            inside = (lane >= start) & (lane < start + COLUMNS)
            mask = jnp.where(inside, value, mask)
        masks.append(mask * columns)
    return jnp.concatenate(masks, axis=1)


def weight_of(weight_ref, which, start):
    columns = weight_ref[which][:, start : start + 2 * HIDDEN]
    return columns.astype(jnp.float32).T.astype(jnp.bfloat16)


def factor_of(normed, weight, mask):
    proj = lax.dot_general(
        weight, normed, (((1,), (1,)), ((), ())), preferred_element_type=jnp.float32
    )
    return jax.nn.sigmoid(proj[HIDDEN:]) * proj[:HIDDEN] * mask


def keep_rows(factor, scratch, first, stride):
    for n in range(BATCH):
        place = pl.ds(first + n, HIDDEN, stride=stride)
        scratch[place, :] = factor[:, n * LANES : (n + 1) * LANES]


def put_chunks(scratch, out_ref, channels):
    for channel in channels:
        rows = scratch[pl.ds(channel * BOTH, BOTH), :]
        tiles = [rows[n : n + SUB] for n in range(0, BOTH, SUB)]
        out_ref[channel] = jnp.concatenate(tiles, axis=1).astype(jnp.bfloat16)


def factor_rows(first, count, normed, weights, mask_at, both_s):
    left_weight, right_weight = weights
    if count == 3:
        rows = jnp.concatenate(pad_rows(normed, count), axis=0)
        mask = mask_at(first, count, 0)
        keep_rows(factor_of(rows, left_weight, mask), both_s, first, BOTH)
        keep_rows(factor_of(rows, right_weight, mask), both_s, first + WHOLE * SUB, BOTH)
        return
    pieces = []
    for n in range(BATCH):
        piece = normed[n * COLUMNS : (n + 1) * COLUMNS]
        pieces += [piece, piece, jnp.zeros((LANES - 2 * COLUMNS, WIDTH), jnp.float32)]
    rows = jnp.concatenate(pieces, axis=0).astype(jnp.bfloat16)
    factor = factor_of(rows, left_weight, mask_at(first, count, 0))
    factor = factor + factor_of(rows, right_weight, mask_at(first, count, 1))
    keep_rows(factor, both_s, 2 * WHOLE * SUB, BOTH)


SCRATCH = pltpu.VMEM(((HIDDEN + 1) * STRIDE, LANES), jnp.float32)
BOTH_SCRATCH = pltpu.VMEM(((HIDDEN + 1) * BOTH, LANES), jnp.float32)


def place_of():
    row = (lax.axis_index("x") * ZH + lax.axis_index("zh")) * ROWS
    block = (lax.axis_index("zl") * 8 + lax.axis_index("y")) * 2 + lax.axis_index("core")
    return row, block * COLUMNS


def project_kernel(
    valid_any,
    pair_any,
    gain_any,
    bias_any,
    weight_any,
    both_any,
    both_s,
    both_ref,
    valid_ref,
    pair_ref,
    gain_ref,
    bias_ref,
    weight_ref,
    sems,
    out_sem,
):
    place = place_of()
    moves = [(valid_any, valid_ref), (gain_any, gain_ref), (bias_any, bias_ref)]
    moves.append((weight_any, weight_ref))
    parts = []
    for first in range(0, DEPTH, BATCH):
        for row in block_rows(first, 3 if first < WHOLE * BATCH else 1)[0]:
            parts.append(len(moves))
            rows = pl.ds(row, BATCH)
            moves.append((pair_any.at[rows], pair_ref.at[rows]))
    copies = [pltpu.make_async_copy(a, b, sems.at[n]) for n, (a, b) in enumerate(moves)]
    for copy in copies:
        copy.start()
    for copy in copies[: parts[0]]:
        copy.wait()
    columns = spread_columns(place, valid_ref)
    weights = [weight_of(weight_ref, 0, start) for start in (0, 2 * HIDDEN)]

    def mask_at(first, count, shift):
        return mask_of(first, count, place, valid_ref, columns, shift)

    def work(first, count):
        for part in parts[first // BATCH * 3 :][:count]:
            copies[part].wait()
        values = load_pairs(pair_ref, first, count)
        normed = normalize(values, gain_ref[0:1], bias_ref[0:1])
        factor_rows(first, count, normed, weights, mask_at, both_s)

    batches(work)
    for part in range(0, HIDDEN, 16):
        put_chunks(both_s, both_ref, range(part, part + 16))
        span = pl.ds(part, 16)
        pltpu.make_async_copy(both_ref.at[span], both_any.at[span], out_sem).start()
    pltpu.make_async_copy(both_ref, both_any, out_sem).wait()


def project(valid, *operands):
    scratch = [pltpu.VMEM(each.shape, each.dtype) for each in (BOTH_CHUNKS,) + operands]
    scratch.insert(1, pltpu.SMEM(valid.shape, valid.dtype))
    sems = [pltpu.SemaphoreType.DMA((14,)), pltpu.SemaphoreType.DMA]
    return call(
        project_kernel,
        BOTH_CHUNKS,
        [ANY] * 5,
        [BOTH_SCRATCH] + scratch + sems,
        outs=ANY,
        grant=60,
    )(valid, *operands)


def gate_kernel(which, place_ref, chain_ref, gate_ref, vectors_ref, pair_ref, _, out_ref):
    row = lax.broadcasted_iota(jnp.int32, (COLUMNS, WIDTH), 0)
    chain_columns = jnp.full((COLUMNS, WIDTH), -1, jnp.int32)
    for column in range(COLUMNS):
        chain_columns = jnp.where(row == column, chain_ref[place_ref[1] + column], chain_columns)
    gain, bias, offset = [vectors_ref[n + which : n + which + 1] for n in (0, 2, 4)]

    def work(first, count):
        values = load_pairs(pair_ref, first, count)
        pieces = pad_rows(normalize(values, gain, bias), count)
        logit = jnp.dot(
            jnp.concatenate(pieces, axis=0), gate_ref[which], preferred_element_type=jnp.float32
        )
        for n, rows in enumerate(block_rows(first, count)):
            for group, row in enumerate(rows):
                same = chain_columns == chain_ref[place_ref[0] + row]
                start = n * LANES + group * COLUMNS
                place = pl.ds(group * COLUMNS, COLUMNS)
                out_ref[0, first + n, place] = jax.nn.sigmoid(
                    logit[start : start + COLUMNS] + jnp.where(same, offset, 0.0)
                )
                old = (n * count + group) * COLUMNS
                out_ref[1, first + n, place] = values[old : old + COLUMNS]

    batches(work)


def gates(which, place, chain, gate, vectors, pair, after):
    kernel = functools.partial(gate_kernel, which)
    return call(kernel, GATES, [SMEM, SMEM, VMEM, VMEM, VMEM, ANY])(
        place, chain, gate, vectors, pair, after
    )


def finish_kernel(which, place_ref, valid_ref, out_gain_ref, gates_ref, product_ref, out_weight_ref, *rest):
    then = which == 0
    if then:
        vectors_ref, weight_ref, out_ref, both_ref, hidden_s, both_s = rest
        new_s = out_ref
        columns = spread_columns(place_ref, valid_ref)
        weights = [weight_of(weight_ref, 1, start) for start in (0, 2 * HIDDEN)]

        def mask_at(first, count, shift):
            return mask_of(first, count, place_ref, valid_ref, columns, shift)

    else:
        out_ref, hidden_s, new_s, out_sem = rest

    def channel(n):
        return product_ref[n].astype(jnp.float32)

    average = channel(0)
    for n in range(1, HIDDEN):
        average = average + channel(n)
    average = average / HIDDEN
    spread = jnp.zeros_like(average)
    for n in range(HIDDEN):
        centred = channel(n) - average
        spread = spread + centred * centred
    scale = lax.rsqrt(spread / HIDDEN + EPS)
    for n in range(HIDDEN):
        hidden = (channel(n) - average) * scale * out_gain_ref[which, n]
        for part in range(DEPTH // SUB):
            place = pl.ds(n * STRIDE + part * SUB, SUB)
            hidden_s[place, :] = hidden[:, part * LANES : (part + 1) * LANES]

    def work(first, count):
        size = count * COLUMNS
        hidden = jnp.concatenate(
            [hidden_s[pl.ds(first + n, HIDDEN, stride=STRIDE), :] for n in range(BATCH)], axis=1
        ).astype(jnp.bfloat16)
        branch = lax.dot_general(
            hidden,
            out_weight_ref[which],
            (((0,), (0,)), ((), ())),
            preferred_element_type=jnp.float32,
        )
        new = jnp.concatenate(
            [
                gates_ref[1, first + n, pl.ds(0, size)]
                + gates_ref[0, first + n, pl.ds(0, size)] * branch[n * LANES : n * LANES + size]
                for n in range(BATCH)
            ],
            axis=0,
        )
        places = [row for rows in block_rows(first, count) for row in rows]
        for n, row in enumerate(places):
            new_s[row] = new[n * COLUMNS : (n + 1) * COLUMNS].astype(jnp.bfloat16)
        if not then:
            for group in range(count):
                span = pl.ds(block_rows(first, count)[0][group], BATCH)
                pltpu.make_async_copy(new_s.at[span], out_ref.at[span], out_sem).start()
            return
        new = new.astype(jnp.bfloat16).astype(jnp.float32)
        normed = normalize(new, vectors_ref[1:2], vectors_ref[3:4])
        factor_rows(first, count, normed, weights, mask_at, both_s)

    batches(work)
    if then:
        put_chunks(both_s, both_ref, range(HIDDEN))
    else:
        pltpu.make_async_copy(new_s, out_ref, out_sem).wait()


def finish(which, place, valid, out_gain, gate, product, out_weight, *then):
    shape = (ROWS, COLUMNS, WIDTH)
    out = jax.ShapeDtypeStruct(shape, jnp.bfloat16)
    last = [pltpu.VMEM(shape, jnp.bfloat16), pltpu.SemaphoreType.DMA]
    return call(
        functools.partial(finish_kernel, which),
        [out, BOTH_CHUNKS] if then else [out],
        [SMEM] * 3 + [VMEM] * (3 + len(then)),
        [SCRATCH] + ([BOTH_SCRATCH] if then else last),
        outs=None if then else [ANY],
    )(place, valid, out_gain, gate, product, out_weight, *then)


LEFT = (0, 6, 0)
RIGHT = (3, 6, COLUMNS)


def gather_rows(chunks_ref, zh, block, layout):
    tile, last_tile, last_lane = layout
    start = last_tile * LANES + last_lane
    if block < 9:
        start = (tile + block % 3) * LANES + block // 3 * COLUMNS
    return jnp.concatenate(
        [
            chunks_ref[spot(span, zh)].astype(jnp.float32)[:, start : start + COLUMNS]
            for span in range(SPAN)
        ],
        axis=1,
    )


def assemble_into(chunks_ref, layout, put):
    for zh in range(ZH):
        for block in range(0, ROWS // SUB, 2):
            rows = [gather_rows(chunks_ref, zh, block + n, layout) for n in range(2)]
            put(zh * ROWS + block * SUB, jnp.concatenate(rows, axis=0))


def assemble_kernel(layout, chunks_ref, out_ref):
    def put(start, values):
        out_ref[pl.ds(start, 2 * SUB), :] = values.astype(jnp.bfloat16)

    assemble_into(chunks_ref, layout, put)


def assemble(chunks, layout):
    out = jax.ShapeDtypeStruct((ZH * ROWS, SPAN * COLUMNS), jnp.bfloat16)
    return call(functools.partial(assemble_kernel, layout), out, [VMEM])(chunks)


def assemble_turned_kernel(layout, chunks_ref, out_ref, whole, turned_s, sem):
    def put(start, values):
        whole[pl.ds(start, 2 * SUB), :] = values

    assemble_into(chunks_ref, layout, put)
    whole[pl.ds(ZH * ROWS, 64), :] = jnp.zeros((64, SPAN * COLUMNS), jnp.float32)
    for part in range(SPAN * COLUMNS // 128):
        turned = whole[:, part * 128 : (part + 1) * 128].T
        rows = pl.ds(part * 128, 128)
        turned_s[rows, :] = turned[:, : ZH * ROWS].astype(jnp.bfloat16)
        pltpu.make_async_copy(turned_s.at[rows], out_ref.at[rows], sem).start()
    pltpu.make_async_copy(turned_s, out_ref, sem).wait()


def assemble_turned(chunks, layout):
    out = jax.ShapeDtypeStruct((SPAN * COLUMNS, ZH * ROWS), jnp.bfloat16)
    scratch = [
        pltpu.VMEM((ZH * ROWS + 64, SPAN * COLUMNS), jnp.float32),
        pltpu.VMEM(out.shape, out.dtype),
        pltpu.SemaphoreType.DMA,
    ]
    kernel = functools.partial(assemble_turned_kernel, layout)
    return call(kernel, out, [VMEM], scratch, outs=ANY)(chunks)


def chunk_of(total, zh, start):
    pieces = [
        total[pl.ds(zh * ROWS + block * SUB, SUB), :][:, start : start + COLUMNS]
        for block in range(ROWS // SUB)
    ]
    lanes = []
    for tile in range(WHOLE):
        lanes += pieces[tile:9:3] + [jnp.zeros((SUB, LANES - 3 * COLUMNS), jnp.float32)]
    lanes += [pieces[9], jnp.zeros((SUB, LANES - COLUMNS), jnp.float32)]
    return jnp.concatenate(lanes, axis=1).astype(jnp.bfloat16)


def outgoing_part(core_ref, left_ref, rights, aheads, base, out_ref, total):
    for n, right_ref in enumerate(rights):
        total[:, n * ZH * ROWS : (n + 1) * ZH * ROWS] = lax.dot_general(
            left_ref[...],
            right_ref[...],
            (((1,), (1,)), ((), ())),
            preferred_element_type=jnp.float32,
        )
    for half in range(2):
        slot = lax.rem(core_ref[0] + half, 2)
        for n, ahead in enumerate(aheads):
            zl = lax.rem(core_ref[1] + ahead, X) // 2
            for low in range(ZH):
                start = ((n * ZH + low) * 2 + half) * COLUMNS
                for zh in range(ZH):
                    place = base + (low * ZH + zh) * 2 + zl
                    out_ref[slot, place] = chunk_of(total, zh, start)


def outgoing_first_kernel(core_ref, left_ref, own_ref, across_ref, out_ref, total):
    outgoing_part(core_ref, left_ref, (own_ref, across_ref), ORDER[:2], 0, out_ref, total)


def outgoing_last_kernel(core_ref, left_ref, next_ref, last_ref, first_ref, _, out_ref, total):
    parity = lax.rem(core_ref[1], 2)
    for slot in range(2):
        out_ref[slot, pl.ds(parity * HALF, HALF)] = first_ref[slot]
    base = (1 - parity) * HALF
    outgoing_part(core_ref, left_ref, (next_ref, last_ref), ORDER[2:], base, out_ref, total)


def outgoing(core, left, rights, gate):
    half = jax.ShapeDtypeStruct((2, HALF) + CHUNKS.shape[1:], jnp.bfloat16)
    out = jax.ShapeDtypeStruct((2,) + CHUNKS.shape, jnp.bfloat16)
    scratch = [pltpu.VMEM((ZH * ROWS, 2 * ZH * ROWS), jnp.float32)]
    first = call(outgoing_first_kernel, half, [SMEM] + [VMEM] * 3, scratch, 3 * 10**8)(
        core, left, *rights[:2]
    )
    return call(outgoing_last_kernel, out, [SMEM] + [VMEM] * 4 + [ANY], scratch, 3 * 10**8)(
        core, left, *rights[2:], first, gate
    )


def incoming_kernel(core_ref, own_ref, other_ref, *rest):
    rights, (_, out_ref, total) = rest[:X], rest[X:]
    for n, left_ref in enumerate((own_ref, other_ref)):
        side = lax.rem(core_ref[0] + n, 2)
        product = jnp.zeros((ZH * COLUMNS, SPAN * COLUMNS), jnp.float32)
        for ahead, right_ref in zip(ORDER, rights):
            product = product + jnp.dot(
                left_ref[lax.rem(core_ref[1] + ahead, X)],
                right_ref[...],
                preferred_element_type=jnp.float32,
            )
        for zh in range(ZH):
            start = pl.multiple_of(zh * ROWS + side * COLUMNS, 8)
            total[pl.ds(start, COLUMNS), :] = product[zh * COLUMNS : (zh + 1) * COLUMNS]
    for span in range(SPAN):
        for zh in range(ZH):
            out_ref[spot(span, zh)] = chunk_of(total, zh, span * COLUMNS)


def incoming(core, own, other, rights, gate):
    scratch = [pltpu.VMEM((ZH * ROWS, SPAN * COLUMNS), jnp.float32)]
    return call(
        incoming_kernel, CHUNKS, [SMEM] + [VMEM] * (2 + X) + [ANY], scratch, 6 * 10**8
    )(core, own, other, *rights, gate)


def gather_x(block):
    def shift(ahead):
        return lax.ppermute(block, "x", [(x, (x - ahead) % X) for x in range(X)])

    return [block] + [shift(ahead) for ahead in ORDER[1:]]


def exchange(values, axes):
    return lax.all_to_all(values, axes, split_axis=0, concat_axis=0, tiled=True)


def swap_cores(values):
    return lax.ppermute(values, "core", [(0, 1), (1, 0)])


def body(
    pair_acts,
    residue_valid,
    chain_index,
    norm_gain,
    norm_bias,
    projection,
    gate_weight,
    chain_bias,
    out_gain,
    out_weight,
):
    place = jnp.stack(place_of()).astype(jnp.int32)
    core = jnp.stack([lax.axis_index("core"), lax.axis_index("x")]).astype(jnp.int32)

    vectors = jnp.concatenate([norm_gain, norm_bias, chain_bias], axis=0)
    both = project(residue_valid, pair_acts, norm_gain, norm_bias, projection)
    both = exchange(both, PLANE)
    rights = gather_x(assemble(both, RIGHT))
    left = assemble(both, LEFT)
    gate = gates(0, place, chain_index, gate_weight, vectors, pair_acts, left)
    halves = outgoing(core, left, rights, gate)
    total = halves[0].astype(jnp.float32) + swap_cores(halves[1]).astype(jnp.float32)
    product = exchange(total.astype(jnp.bfloat16), PLANE)
    middle, both = finish(
        0, place, residue_valid, out_gain, gate, product, out_weight, vectors, projection
    )
    both = exchange(both, PLANE)
    rights = gather_x(assemble(both, RIGHT))
    left = assemble_turned(both, LEFT).reshape(X, ZH * COLUMNS, ZH * ROWS)
    gate = gates(1, place, chain_index, gate_weight, vectors, middle, left)
    left = exchange(left, "x")
    product = exchange(incoming(core, left, swap_cores(left), rights, gate), PLANE)
    return finish(1, place, residue_valid, out_gain, gate, product, out_weight)[0]


def solution(mesh):
    fine = Mesh(mesh.devices.reshape(SIZES), AXES)
    pairs = P(("x", "zh"), ("zl", "y", "core"), None)
    placed = (pairs, P(), P(), P(), P(), P(), P(), P(), P(), P())
    return jax.shard_map(body, mesh=fine, in_specs=placed, out_specs=pairs, check_vma=False)
```

```python
import functools

import jax
import jax.numpy as jnp
from jax import lax
from jax.experimental import pallas as pl
from jax.experimental.pallas import tpu as pltpu
from jax.sharding import Mesh
from jax.sharding import PartitionSpec as P

AXES = ("zl", "y", "core", "x", "zh")
SIZES = (2, 8, 2, 4, 4)
PLANE = ("y", "zh", "zl")
ROWS = 80
COLUMNS = 40
WIDTH = 128
HIDDEN = 64
X = 4
ZH = 4
SPAN = 16
EPS = 1e-05
DEPTH = 32
LANES = 128
SUB = 8
WHOLE = 3
TAIL = 8 * 9
ORDER = (0, 2, 1, 3)
HALF = 32
STRIDE = 40
BOTH = 56
BATCH = 8
CHUNKS = jax.ShapeDtypeStruct((HIDDEN, SUB, DEPTH // SUB * LANES), jnp.bfloat16)
BOTH_CHUNKS = jax.ShapeDtypeStruct((HIDDEN, SUB, BOTH // SUB * LANES), jnp.bfloat16)
GATES = jax.ShapeDtypeStruct((2, DEPTH, LANES, WIDTH), jnp.float32)
VMEM = pl.BlockSpec(memory_space=pltpu.VMEM)
ANY = pl.BlockSpec(memory_space=pl.ANY)
SMEM = pl.BlockSpec(memory_space=pltpu.SMEM)


def spot(span, zh):
    zl, y = divmod(span, 8)
    return (y * ZH + zh) * 2 + zl


def call(kernel, out_shape, in_specs, scratch_shapes=(), flops=10**8, outs=None, grant=40):
    outs = outs or jax.tree.map(lambda _: VMEM, out_shape)
    moved = 4 * 10**6
    return pl.pallas_call(
        kernel,
        out_shape=out_shape,
        in_specs=in_specs,
        out_specs=outs,
        scratch_shapes=scratch_shapes,
        compiler_params=pltpu.CompilerParams(vmem_limit_bytes=grant * 2**20),
        cost_estimate=pl.CostEstimate(flops=flops, bytes_accessed=moved, transcendentals=0),
    )


def normalize(values, gain, bias):
    average = jnp.mean(values, axis=-1, keepdims=True)
    centred = values - average
    spread = jnp.mean(centred * centred, axis=-1, keepdims=True)
    return centred * lax.rsqrt(spread + EPS) * gain + bias


def batches(work):
    for step in range(WHOLE):
        work(step * BATCH, 3)
    work(WHOLE * BATCH, 1)


def block_rows(first, count):
    if count == 1:
        return [[TAIL + n] for n in range(BATCH)]
    return [[first + n + WHOLE * SUB * group for group in range(count)] for n in range(BATCH)]


def load_pairs(pair_ref, first, count):
    rows = [row for rows in block_rows(first, count) for row in rows]
    return jnp.concatenate([pair_ref[row].astype(jnp.float32) for row in rows], axis=0)


def pad_rows(values, count):
    size = count * COLUMNS
    empty = jnp.zeros((LANES - size, WIDTH), jnp.float32)
    return [
        jnp.concatenate([values[n * size : (n + 1) * size], empty], axis=0).astype(jnp.bfloat16)
        for n in range(BATCH)
    ]


def spread_columns(place_ref, valid_ref):
    lane = lax.broadcasted_iota(jnp.int32, (1, LANES), 1)
    inside = lane % COLUMNS
    found = jnp.zeros((1, LANES), jnp.float32)
    for column in range(COLUMNS):
        value = valid_ref[place_ref[1] + column].astype(jnp.float32)
        found = jnp.where(inside == column, value, found)
    return jnp.where(lane < 3 * COLUMNS, found, 0.0)


def mask_of(first, count, place_ref, valid_ref, columns, shift=0):
    lane = lax.broadcasted_iota(jnp.int32, (1, LANES), 1)
    masks = []
    for rows in block_rows(first, count):
        mask = jnp.zeros((1, LANES), jnp.float32)
        for group, row in enumerate(rows):
            value = valid_ref[place_ref[0] + row].astype(jnp.float32)
            start = (group + shift) * COLUMNS
            inside = (lane >= start) & (lane < start + COLUMNS)
            mask = jnp.where(inside, value, mask)
        masks.append(mask * columns)
    return jnp.concatenate(masks, axis=1)


def weight_of(weight_ref, which, start):
    columns = weight_ref[which][:, start : start + 2 * HIDDEN]
    return columns.astype(jnp.float32).T.astype(jnp.bfloat16)


def factor_of(normed, weight, mask):
    proj = lax.dot_general(
        weight, normed, (((1,), (1,)), ((), ())), preferred_element_type=jnp.float32
    )
    return jax.nn.sigmoid(proj[HIDDEN:]) * proj[:HIDDEN] * mask


def keep_rows(factor, scratch, first, stride):
    for n in range(BATCH):
        place = pl.ds(first + n, HIDDEN, stride=stride)
        scratch[place, :] = factor[:, n * LANES : (n + 1) * LANES]


def put_chunks(scratch, out_ref, channels):
    for channel in channels:
        rows = scratch[pl.ds(channel * BOTH, BOTH), :]
        tiles = [rows[n : n + SUB] for n in range(0, BOTH, SUB)]
        out_ref[channel] = jnp.concatenate(tiles, axis=1).astype(jnp.bfloat16)


def factor_rows(first, count, normed, weights, mask_at, both_s):
    left_weight, right_weight = weights
    if count == 3:
        rows = jnp.concatenate(pad_rows(normed, count), axis=0)
        mask = mask_at(first, count, 0)
        keep_rows(factor_of(rows, left_weight, mask), both_s, first, BOTH)
        keep_rows(factor_of(rows, right_weight, mask), both_s, first + WHOLE * SUB, BOTH)
        return
    pieces = []
    for n in range(BATCH):
        piece = normed[n * COLUMNS : (n + 1) * COLUMNS]
        pieces += [piece, piece, jnp.zeros((LANES - 2 * COLUMNS, WIDTH), jnp.float32)]
    rows = jnp.concatenate(pieces, axis=0).astype(jnp.bfloat16)
    factor = factor_of(rows, left_weight, mask_at(first, count, 0))
    factor = factor + factor_of(rows, right_weight, mask_at(first, count, 1))
    keep_rows(factor, both_s, 2 * WHOLE * SUB, BOTH)


SCRATCH = pltpu.VMEM(((HIDDEN + 1) * STRIDE, LANES), jnp.float32)
BOTH_SCRATCH = pltpu.VMEM(((HIDDEN + 1) * BOTH, LANES), jnp.float32)


def place_of():
    row = (lax.axis_index("x") * ZH + lax.axis_index("zh")) * ROWS
    block = (lax.axis_index("zl") * 8 + lax.axis_index("y")) * 2 + lax.axis_index("core")
    return row, block * COLUMNS


def project_kernel(
    valid_any,
    pair_any,
    gain_any,
    bias_any,
    weight_any,
    both_any,
    both_s,
    both_ref,
    valid_ref,
    pair_ref,
    gain_ref,
    bias_ref,
    weight_ref,
    sems,
    out_sem,
):
    place = place_of()
    moves = [(valid_any, valid_ref), (gain_any, gain_ref), (bias_any, bias_ref)]
    moves.append((weight_any, weight_ref))
    parts = []
    for first in range(0, DEPTH, BATCH):
        for row in block_rows(first, 3 if first < WHOLE * BATCH else 1)[0]:
            parts.append(len(moves))
            rows = pl.ds(row, BATCH)
            moves.append((pair_any.at[rows], pair_ref.at[rows]))
    copies = [pltpu.make_async_copy(a, b, sems.at[n]) for n, (a, b) in enumerate(moves)]
    for copy in copies:
        copy.start()
    for copy in copies[: parts[0]]:
        copy.wait()
    columns = spread_columns(place, valid_ref)
    weights = [weight_of(weight_ref, 0, start) for start in (0, 2 * HIDDEN)]

    def mask_at(first, count, shift):
        return mask_of(first, count, place, valid_ref, columns, shift)

    def work(first, count):
        for part in parts[first // BATCH * 3 :][:count]:
            copies[part].wait()
        values = load_pairs(pair_ref, first, count)
        normed = normalize(values, gain_ref[0:1], bias_ref[0:1])
        factor_rows(first, count, normed, weights, mask_at, both_s)

    batches(work)
    for part in range(0, HIDDEN, 16):
        put_chunks(both_s, both_ref, range(part, part + 16))
        span = pl.ds(part, 16)
        pltpu.make_async_copy(both_ref.at[span], both_any.at[span], out_sem).start()
    pltpu.make_async_copy(both_ref, both_any, out_sem).wait()


def project(valid, *operands):
    scratch = [pltpu.VMEM(each.shape, each.dtype) for each in (BOTH_CHUNKS,) + operands]
    scratch.insert(1, pltpu.SMEM(valid.shape, valid.dtype))
    sems = [pltpu.SemaphoreType.DMA((14,)), pltpu.SemaphoreType.DMA]
    return call(
        project_kernel,
        BOTH_CHUNKS,
        [ANY] * 5,
        [BOTH_SCRATCH] + scratch + sems,
        outs=ANY,
        grant=60,
    )(valid, *operands)


def gate_kernel(which, place_ref, chain_ref, gate_ref, vectors_ref, pair_ref, _, out_ref):
    row = lax.broadcasted_iota(jnp.int32, (COLUMNS, WIDTH), 0)
    chain_columns = jnp.full((COLUMNS, WIDTH), -1, jnp.int32)
    for column in range(COLUMNS):
        chain_columns = jnp.where(row == column, chain_ref[place_ref[1] + column], chain_columns)
    gain, bias, offset = [vectors_ref[n + which : n + which + 1] for n in (0, 2, 4)]

    def work(first, count):
        values = load_pairs(pair_ref, first, count)
        pieces = pad_rows(normalize(values, gain, bias), count)
        logit = jnp.dot(
            jnp.concatenate(pieces, axis=0), gate_ref[which], preferred_element_type=jnp.float32
        )
        for n, rows in enumerate(block_rows(first, count)):
            for group, row in enumerate(rows):
                same = chain_columns == chain_ref[place_ref[0] + row]
                start = n * LANES + group * COLUMNS
                place = pl.ds(group * COLUMNS, COLUMNS)
                out_ref[0, first + n, place] = jax.nn.sigmoid(
                    logit[start : start + COLUMNS] + jnp.where(same, offset, 0.0)
                )
                old = (n * count + group) * COLUMNS
                out_ref[1, first + n, place] = values[old : old + COLUMNS]

    batches(work)


def gates(which, place, chain, gate, vectors, pair, after):
    kernel = functools.partial(gate_kernel, which)
    return call(kernel, GATES, [SMEM, SMEM, VMEM, VMEM, VMEM, ANY])(
        place, chain, gate, vectors, pair, after
    )


def finish_kernel(which, place_ref, valid_ref, out_gain_ref, gates_ref, product_ref, out_weight_ref, *rest):
    then = which == 0
    if then:
        vectors_ref, weight_ref, out_ref, both_ref, hidden_s, both_s = rest
        new_s = out_ref
        columns = spread_columns(place_ref, valid_ref)
        weights = [weight_of(weight_ref, 1, start) for start in (0, 2 * HIDDEN)]

        def mask_at(first, count, shift):
            return mask_of(first, count, place_ref, valid_ref, columns, shift)

    else:
        out_ref, hidden_s, new_s, out_sem = rest

    def channel(n):
        return product_ref[n].astype(jnp.float32)

    average = channel(0)
    for n in range(1, HIDDEN):
        average = average + channel(n)
    average = average / HIDDEN
    spread = jnp.zeros_like(average)
    for n in range(HIDDEN):
        centred = channel(n) - average
        spread = spread + centred * centred
    scale = lax.rsqrt(spread / HIDDEN + EPS)
    for n in range(HIDDEN):
        hidden = (channel(n) - average) * scale * out_gain_ref[which, n]
        for part in range(DEPTH // SUB):
            place = pl.ds(n * STRIDE + part * SUB, SUB)
            hidden_s[place, :] = hidden[:, part * LANES : (part + 1) * LANES]

    def work(first, count):
        size = count * COLUMNS
        hidden = jnp.concatenate(
            [hidden_s[pl.ds(first + n, HIDDEN, stride=STRIDE), :] for n in range(BATCH)], axis=1
        ).astype(jnp.bfloat16)
        branch = lax.dot_general(
            hidden,
            out_weight_ref[which],
            (((0,), (0,)), ((), ())),
            preferred_element_type=jnp.float32,
        )
        new = jnp.concatenate(
            [
                gates_ref[1, first + n, pl.ds(0, size)]
                + gates_ref[0, first + n, pl.ds(0, size)] * branch[n * LANES : n * LANES + size]
                for n in range(BATCH)
            ],
            axis=0,
        )
        places = [row for rows in block_rows(first, count) for row in rows]
        for n, row in enumerate(places):
            new_s[row] = new[n * COLUMNS : (n + 1) * COLUMNS].astype(jnp.bfloat16)
        if not then:
            for group in range(count):
                span = pl.ds(block_rows(first, count)[0][group], BATCH)
                pltpu.make_async_copy(new_s.at[span], out_ref.at[span], out_sem).start()
            return
        new = new.astype(jnp.bfloat16).astype(jnp.float32)
        normed = normalize(new, vectors_ref[1:2], vectors_ref[3:4])
        factor_rows(first, count, normed, weights, mask_at, both_s)

    batches(work)
    if then:
        put_chunks(both_s, both_ref, range(HIDDEN))
    else:
        pltpu.make_async_copy(new_s, out_ref, out_sem).wait()


def finish(which, place, valid, out_gain, gate, product, out_weight, *then):
    shape = (ROWS, COLUMNS, WIDTH)
    out = jax.ShapeDtypeStruct(shape, jnp.bfloat16)
    last = [pltpu.VMEM(shape, jnp.bfloat16), pltpu.SemaphoreType.DMA]
    return call(
        functools.partial(finish_kernel, which),
        [out, BOTH_CHUNKS] if then else [out],
        [SMEM] * 3 + [VMEM] * (3 + len(then)),
        [SCRATCH] + ([BOTH_SCRATCH] if then else last),
        outs=None if then else [ANY],
    )(place, valid, out_gain, gate, product, out_weight, *then)


LEFT = (0, 6, 0)
RIGHT = (3, 6, COLUMNS)


def gather_rows(chunks_ref, zh, block, layout):
    tile, last_tile, last_lane = layout
    start = last_tile * LANES + last_lane
    if block < 9:
        start = (tile + block % 3) * LANES + block // 3 * COLUMNS
    return jnp.concatenate(
        [
            chunks_ref[spot(span, zh)].astype(jnp.float32)[:, start : start + COLUMNS]
            for span in range(SPAN)
        ],
        axis=1,
    )


def assemble_into(chunks_ref, layout, put):
    for zh in range(ZH):
        for block in range(0, ROWS // SUB, 2):
            rows = [gather_rows(chunks_ref, zh, block + n, layout) for n in range(2)]
            put(zh * ROWS + block * SUB, jnp.concatenate(rows, axis=0))


def assemble_kernel(layout, chunks_ref, out_ref):
    def put(start, values):
        out_ref[pl.ds(start, 2 * SUB), :] = values.astype(jnp.bfloat16)

    assemble_into(chunks_ref, layout, put)


def assemble(chunks, layout):
    out = jax.ShapeDtypeStruct((ZH * ROWS, SPAN * COLUMNS), jnp.bfloat16)
    return call(functools.partial(assemble_kernel, layout), out, [VMEM])(chunks)


def assemble_turned_kernel(layout, chunks_ref, out_ref, whole, turned_s, sem):
    def put(start, values):
        whole[pl.ds(start, 2 * SUB), :] = values

    assemble_into(chunks_ref, layout, put)
    whole[pl.ds(ZH * ROWS, 64), :] = jnp.zeros((64, SPAN * COLUMNS), jnp.float32)
    for part in range(SPAN * COLUMNS // 128):
        turned = whole[:, part * 128 : (part + 1) * 128].T
        rows = pl.ds(part * 128, 128)
        turned_s[rows, :] = turned[:, : ZH * ROWS].astype(jnp.bfloat16)
        pltpu.make_async_copy(turned_s.at[rows], out_ref.at[rows], sem).start()
    pltpu.make_async_copy(turned_s, out_ref, sem).wait()


def assemble_turned(chunks, layout):
    out = jax.ShapeDtypeStruct((SPAN * COLUMNS, ZH * ROWS), jnp.bfloat16)
    scratch = [
        pltpu.VMEM((ZH * ROWS + 64, SPAN * COLUMNS), jnp.float32),
        pltpu.VMEM(out.shape, out.dtype),
        pltpu.SemaphoreType.DMA,
    ]
    kernel = functools.partial(assemble_turned_kernel, layout)
    return call(kernel, out, [VMEM], scratch, outs=ANY)(chunks)


def chunk_of(total, zh, start):
    pieces = [
        total[pl.ds(zh * ROWS + block * SUB, SUB), :][:, start : start + COLUMNS]
        for block in range(ROWS // SUB)
    ]
    lanes = []
    for tile in range(WHOLE):
        lanes += pieces[tile:9:3] + [jnp.zeros((SUB, LANES - 3 * COLUMNS), jnp.float32)]
    lanes += [pieces[9], jnp.zeros((SUB, LANES - COLUMNS), jnp.float32)]
    return jnp.concatenate(lanes, axis=1).astype(jnp.bfloat16)


def outgoing_part(core_ref, left_ref, rights, aheads, base, out_ref, total):
    for n, right_ref in enumerate(rights):
        total[:, n * ZH * ROWS : (n + 1) * ZH * ROWS] = lax.dot_general(
            left_ref[...],
            right_ref[...],
            (((1,), (1,)), ((), ())),
            preferred_element_type=jnp.float32,
        )
    for half in range(2):
        slot = lax.rem(core_ref[0] + half, 2)
        for n, ahead in enumerate(aheads):
            zl = lax.rem(core_ref[1] + ahead, X) // 2
            for low in range(ZH):
                start = ((n * ZH + low) * 2 + half) * COLUMNS
                for zh in range(ZH):
                    place = base + (low * ZH + zh) * 2 + zl
                    out_ref[slot, place] = chunk_of(total, zh, start)


def outgoing_first_kernel(core_ref, left_ref, own_ref, across_ref, out_ref, total):
    outgoing_part(core_ref, left_ref, (own_ref, across_ref), ORDER[:2], 0, out_ref, total)


def outgoing_last_kernel(core_ref, left_ref, next_ref, last_ref, first_ref, _, out_ref, total):
    parity = lax.rem(core_ref[1], 2)
    for slot in range(2):
        out_ref[slot, pl.ds(parity * HALF, HALF)] = first_ref[slot]
    base = (1 - parity) * HALF
    outgoing_part(core_ref, left_ref, (next_ref, last_ref), ORDER[2:], base, out_ref, total)


def outgoing(core, left, rights, gate):
    half = jax.ShapeDtypeStruct((2, HALF) + CHUNKS.shape[1:], jnp.bfloat16)
    out = jax.ShapeDtypeStruct((2,) + CHUNKS.shape, jnp.bfloat16)
    scratch = [pltpu.VMEM((ZH * ROWS, 2 * ZH * ROWS), jnp.float32)]
    first = call(outgoing_first_kernel, half, [SMEM] + [VMEM] * 3, scratch, 3 * 10**8)(
        core, left, *rights[:2]
    )
    return call(outgoing_last_kernel, out, [SMEM] + [VMEM] * 4 + [ANY], scratch, 3 * 10**8)(
        core, left, *rights[2:], first, gate
    )


def incoming_part(core_ref, lefts, rights, aheads, total, before=None):
    for n, left_ref in enumerate(lefts):
        side = lax.rem(core_ref[0] + n, 2)
        product = jnp.zeros((ZH * COLUMNS, SPAN * COLUMNS), jnp.float32)
        for ahead, right_ref in zip(aheads, rights):
            product = product + jnp.dot(
                left_ref[lax.rem(core_ref[1] + ahead, X)],
                right_ref[...],
                preferred_element_type=jnp.float32,
            )
        for zh in range(ZH):
            place = pl.ds(pl.multiple_of(zh * ROWS + side * COLUMNS, 8), COLUMNS)
            part = product[zh * COLUMNS : (zh + 1) * COLUMNS]
            total[place, :] = part if before is None else part + before[place, :]


def incoming_first_kernel(core_ref, own_ref, other_ref, here_ref, across_ref, out_ref):
    incoming_part(core_ref, (own_ref, other_ref), (here_ref, across_ref), ORDER[:2], out_ref)


def incoming_last_kernel(
    core_ref, own_ref, other_ref, next_ref, last_ref, before_ref, _, out_ref, total
):
    rights = (next_ref, last_ref)
    incoming_part(core_ref, (own_ref, other_ref), rights, ORDER[2:], total, before_ref)
    for span in range(SPAN):
        for zh in range(ZH):
            out_ref[spot(span, zh)] = chunk_of(total, zh, span * COLUMNS)


def incoming(core, own, other, rights, gate):
    size = (ZH * ROWS, SPAN * COLUMNS)
    half = jax.ShapeDtypeStruct(size, jnp.float32)
    first = call(incoming_first_kernel, half, [SMEM] + [VMEM] * 4, (), 3 * 10**8)(
        core, own, other, *rights[:2]
    )
    specs = [SMEM] + [VMEM] * 5 + [ANY]
    scratch = [pltpu.VMEM(size, jnp.float32)]
    return call(incoming_last_kernel, CHUNKS, specs, scratch, 3 * 10**8)(
        core, own, other, *rights[2:], first, gate
    )


def gather_x(block):
    def shift(ahead):
        return lax.ppermute(block, "x", [(x, (x - ahead) % X) for x in range(X)])

    return [block] + [shift(ahead) for ahead in ORDER[1:]]


def exchange(values, axes):
    return lax.all_to_all(values, axes, split_axis=0, concat_axis=0, tiled=True)


def swap_cores(values):
    return lax.ppermute(values, "core", [(0, 1), (1, 0)])


def body(
    pair_acts,
    residue_valid,
    chain_index,
    norm_gain,
    norm_bias,
    projection,
    gate_weight,
    chain_bias,
    out_gain,
    out_weight,
):
    place = jnp.stack(place_of()).astype(jnp.int32)
    core = jnp.stack([lax.axis_index("core"), lax.axis_index("x")]).astype(jnp.int32)

    vectors = jnp.concatenate([norm_gain, norm_bias, chain_bias], axis=0)
    both = project(residue_valid, pair_acts, norm_gain, norm_bias, projection)
    both = exchange(both, PLANE)
    rights = gather_x(assemble(both, RIGHT))
    left = assemble(both, LEFT)
    gate = gates(0, place, chain_index, gate_weight, vectors, pair_acts, left)
    halves = outgoing(core, left, rights, gate)
    total = halves[0].astype(jnp.float32) + swap_cores(halves[1]).astype(jnp.float32)
    product = exchange(total.astype(jnp.bfloat16), PLANE)
    middle, both = finish(
        0, place, residue_valid, out_gain, gate, product, out_weight, vectors, projection
    )
    both = exchange(both, PLANE)
    rights = gather_x(assemble(both, RIGHT))
    left = assemble_turned(both, LEFT).reshape(X, ZH * COLUMNS, ZH * ROWS)
    gate = gates(1, place, chain_index, gate_weight, vectors, middle, left)
    left = exchange(left, "x")
    product = exchange(incoming(core, left, swap_cores(left), rights, gate), PLANE)
    return finish(1, place, residue_valid, out_gain, gate, product, out_weight)[0]


def solution(mesh):
    fine = Mesh(mesh.devices.reshape(SIZES), AXES)
    pairs = P(("x", "zh"), ("zl", "y", "core"), None)
    placed = (pairs, P(), P(), P(), P(), P(), P(), P(), P(), P())
    return jax.shard_map(body, mesh=fine, in_specs=placed, out_specs=pairs, check_vma=False)
```
